32 devices in a mesh: lag: 2 (over y), patch: 16 (over z, x, core).
Axes of the slice: x: 2, y: 2, z: 4, core: 2. Of those that a mesh axis runs over, the one named last changes fastest.
Arguments:
- incident: bfloat16 [4, 8192, 128], P(None, 'patch'), may hold values from -6 to 6
- pending: float32 [2, 8192, 128], P('lag', 'patch'), may hold values from -6 to 6
- self_inverse: float32 [64, 128, 128], P('patch'), may hold values from -0.5 to 0.5
- retarded: float32 [2, 16, 56, 128, 128], P('lag', 'patch'), may hold values from -0.1875 to 0.1875
- block_rows: int32 [2, 16, 56], P('lag', 'patch'), may hold values from -1 to 3, as said below
- block_sources: int32 [2, 16, 56], P('lag', 'patch'), may hold values from -1 to 63, as said below
- owner_map: int32 [64], replicated, may hold values from 0 to 63, as said below
Outputs:
- currents: bfloat16 [4, 8192, 128], P(None, 'patch')
- fields_ahead: float32 [2, 8192, 128], P('lag', 'patch')
The draws below stay inside these ranges and needn't reach their ends.
Inputs may be any that keep to these rules, and one draw needn't show every extreme that they name: `block_sources`: each device's list holds its live entries first and -1 after them; at most 56 live entries, a count that some device reaches in every draw; the live entries of one device name no (row, source) pair twice and, among them, at most one storage block of each patch owner. `block_rows`: -1 exactly where block_sources is -1. `owner_map`: A permutation of the 64 storage blocks; storage block q is owned by patch q // 4.
All inputs are finite; a program needn't handle non-finite values.
Results may differ from the reference program's by a relative error of at most 0.0055.
Values may be sent and summed in bfloat16 or wider, within the bound.
No kernel may reach another device: no remote copies, remote signals or barrier semaphores. Data moves between devices by JAX's collectives and lax.ppermute only.
A program may use at most 64 MiB of HBM per device.

```python
import jax
import jax.numpy as jnp
from jax import lax

EXC = 128
BSIZE = 128
BLK_DEV = 4
BLOCKS_DEV = 56
STEPS = 4
LAGS = 2
PATCHES = 16
SRC = 64
UNKNOWNS = 8192


def layout_tables(key):
    base_key = jax.random.fold_in(key, 7)
    perm_key, count_key, full_key, order_key, row_key, local_key = jax.random.split(base_key, 6)
    owner_table = jax.random.permutation(perm_key, SRC).astype(jnp.int32)
    storage_source = jnp.argsort(owner_table).astype(jnp.int32)
    devices = LAGS * PATCHES
    lowest = BLOCKS_DEV - BLOCKS_DEV // 7
    counts = jax.random.randint(count_key, (devices,), lowest, BLOCKS_DEV + 1)
    full_device = jax.random.randint(full_key, (), 0, devices)
    counts = jnp.where(jnp.arange(devices) == full_device, BLOCKS_DEV, counts)
    order_keys = jax.random.split(order_key, devices)
    owner_orders = jax.vmap(lambda one_key: jax.random.permutation(one_key, PATCHES))(order_keys)
    entry = jnp.arange(BLOCKS_DEV)
    owner_patch = owner_orders[:, entry % PATCHES]
    base_rows = jax.random.randint(row_key, (devices, PATCHES), 0, BLK_DEV)
    start_row = jnp.take_along_axis(base_rows, owner_patch, axis=1)
    row_index = (start_row + (entry // PATCHES)[None, :]) % BLK_DEV
    local_pick = jax.random.randint(local_key, (devices, PATCHES), 0, BLK_DEV)
    chosen = jnp.take_along_axis(local_pick, owner_patch, axis=1)
    source_index = storage_source[owner_patch * BLK_DEV + chosen]
    is_live = entry[None, :] < counts[:, None]
    row_index = jnp.where(is_live, row_index, -1).reshape(LAGS, PATCHES, BLOCKS_DEV).astype(jnp.int32)
    source_index = jnp.where(is_live, source_index, -1).reshape(LAGS, PATCHES, BLOCKS_DEV).astype(jnp.int32)
    return (owner_table, row_index, source_index)


def draw_block_rows(key, part):
    return layout_tables(key)[1]


def draw_block_sources(key, part):
    return layout_tables(key)[2]


def draw_owner_map(key, part):
    return layout_tables(key)[0]


def shard_levels(own_key, dims, cuts, low, top_value):
    gain = 1.0
    for axis_at, shards_of in cuts:
        steps = jax.random.uniform(jax.random.fold_in(jax.random.fold_in(own_key, 6), axis_at), (shards_of,), jnp.float32, low / len(cuts), top_value / len(cuts))
        gain = gain * jnp.repeat(jnp.exp(steps), dims[axis_at] // shards_of).reshape((-1,) + (1,) * (len(dims) - 1 - axis_at))
    return gain


def noise(own_key, shape, scale, reach, cuts=(), held_as=jnp.bfloat16):
    result = jax.random.normal(own_key, shape, jnp.float32) * scale
    if len(cuts) > 0:
        result = shard_levels(own_key, shape, cuts, -0.22, 0.18) * result
    return jnp.clip(result, min=-reach, max=reach).astype(held_as)


def setup_inputs(seed: int = 0) -> dict:
    key_list = jax.random.split(jax.random.key(seed), 8)
    return {
        "incident": noise(key_list[0], (STEPS, UNKNOWNS, EXC), 1.0, 6.0, ((1, 16),)),
        "pending": noise(key_list[1], (LAGS, UNKNOWNS, EXC), 1.0, 6.0, ((0, 2), (1, 16)), jnp.float32),
        "self_inverse": noise(key_list[2], (SRC, BSIZE, BSIZE), BSIZE ** -0.5, 0.5, ((0, 16),), jnp.float32),
        "retarded": noise(key_list[3], (LAGS, PATCHES, BLOCKS_DEV, BSIZE, BSIZE), (BSIZE * 8) ** -0.5, 0.1875, ((0, 2), (1, 16)), jnp.float32),
        "block_rows": draw_block_rows(jax.random.fold_in(key_list[7], 71), 0),
        "block_sources": draw_block_sources(jax.random.fold_in(key_list[7], 71), 0),
        "owner_map": draw_owner_map(jax.random.fold_in(key_list[7], 71), 0),
    }


def reference(incident, pending, self_inverse, retarded, block_rows, block_sources, owner_map):
    fields = jnp.concatenate([pending, jnp.zeros((STEPS, UNKNOWNS, EXC), jnp.float32)], axis=0)
    row_choices = jnp.arange(BLK_DEV).astype(jnp.int32)
    currents = []
    for time_step in range(STEPS):
        excess = incident[time_step].astype(jnp.float32) - fields[time_step]
        solved = jnp.einsum("kab,kbe->kae", self_inverse, excess.reshape(SRC, BSIZE, EXC),
                            precision=lax.Precision.HIGHEST)
        current = solved.reshape(UNKNOWNS, EXC).astype(jnp.bfloat16)
        currents.append(current)
        source_blocks = current.reshape(SRC, BSIZE, EXC)

        def lag_term(operands):
            weights, row_index, source_index = operands
            is_live = (source_index >= 0).astype(jnp.float32)
            storage = owner_map[jnp.maximum(source_index, 0)]
            picked = source_blocks[storage].astype(jnp.float32) * is_live[:, :, None, None]
            product = jnp.einsum("pjab,pjbe->pjae", weights, picked, precision=lax.Precision.HIGHEST)
            row_select = (row_index[:, :, None] == row_choices[None, None, :]).astype(jnp.float32)
            summed = jnp.einsum("pjr,pjae->prae", row_select, product, precision=lax.Precision.HIGHEST)
            return summed.reshape(UNKNOWNS, EXC)

        terms = lax.map(lag_term, (retarded, block_rows, block_sources))
        fields = fields.at[time_step + 1:time_step + 1 + LAGS].add(terms)
    return jnp.stack(currents), fields[STEPS:STEPS + LAGS]
```

```python
import jax
import jax.numpy as jnp
from jax import lax
from jax.experimental import pallas as pl
from jax.experimental.pallas import tpu as pltpu
from jax.sharding import PartitionSpec as P

VMEM = pl.BlockSpec(memory_space=pltpu.VMEM)
SMEM = pl.BlockSpec(memory_space=pltpu.SMEM)
MIB = 1 << 20


def call(kernel, outs, in_specs, flops, nbytes):
    return pl.pallas_call(
        kernel,
        out_shape=outs,
        in_specs=in_specs,
        out_specs=jax.tree.map(lambda _: VMEM, outs),
        cost_estimate=pl.CostEstimate(flops=flops, bytes_accessed=nbytes, transcendentals=0),
        compiler_params=pltpu.CompilerParams(vmem_limit_bytes=32 * MIB),
    )


def shape(dims, dtype):
    return jax.ShapeDtypeStruct(dims, dtype)


def request_kernel(per_patch, sources, owner_map, wanted):
    patch = lax.broadcasted_iota(jnp.int32, wanted.shape, 0)

    def entry(j, table):
        source = sources[0, 0, j]
        storage = owner_map[jnp.maximum(source, 0)]
        here = (patch == storage // per_patch) & (source >= 0)
        return jnp.where(here, storage % per_patch, table)

    wanted[...] = lax.fori_loop(
        0, sources.shape[2], entry, jnp.full(wanted.shape, -1, jnp.int32), unroll=8
    )


def panel_kernel(per_patch, rows, sources, owner_map, retarded, panel):
    size = retarded.shape[-1]
    panel[...] = jnp.zeros_like(panel)

    def entry(j, carry):
        source = sources[0, 0, j]

        @pl.when(source >= 0)
        def _():
            owner = owner_map[source] // per_patch
            row = pl.multiple_of(rows[0, 0, j] * size, size)
            column = pl.multiple_of(owner * size, size)
            panel[pl.ds(row, size), pl.ds(column, size)] = retarded[0, 0, j].astype(panel.dtype)

        return carry

    lax.fori_loop(0, sources.shape[2], entry, 0)


def solved(excess, self_inverse):
    blocks, size, _ = self_inverse.shape
    parts = [
        jnp.dot(
            self_inverse[k],
            excess[k * size : (k + 1) * size],
            precision=lax.Precision.HIGHEST,
            preferred_element_type=jnp.float32,
        )
        for k in range(blocks)
    ]
    return jnp.concatenate(parts, axis=0).astype(jnp.bfloat16)


def first_kernel(time_step, incident, field, self_inverse, current):
    excess = incident[time_step].astype(jnp.float32) - field[...]
    current[...] = solved(excess, self_inverse)


def product(panel, arrived):
    patches, size, columns = arrived.shape
    return jnp.dot(
        panel[...],
        arrived[...].reshape(patches * size, columns),
        preferred_element_type=jnp.float32,
    )


def step_kernel(time_step, panel, arrived, field, incident, self_inverse, partial, current):
    partial[...] = field[...] + product(panel, arrived)
    excess = incident[time_step].astype(jnp.float32) - partial[...]
    current[...] = solved(excess, self_inverse)


def last_kernel(panel, arrived, field, ahead):
    ahead[...] = field[...] + product(panel, arrived)


def pack_kernel(keeps, asked, own, received, outgoing, current):
    size = outgoing.shape[1]
    mine = lax.axis_index("lag") < keeps
    current[...] = jnp.where(mine, own[...], received[...])

    def one(q, carry):
        start = pl.multiple_of(jnp.maximum(asked[q, 0, 0], 0) * size, size)
        outgoing[q] = current[pl.ds(start, size), :]
        return carry

    lax.fori_loop(0, outgoing.shape[0], one, 0, unroll=4)


def shifted(x):
    sections = lax.axis_size("lag")
    return lax.ppermute(x, "lag", [(i, i - 1) for i in range(1, sections)])


def spread(x):
    sections = lax.axis_size("lag")
    section = lax.axis_index("lag")
    received, keeps = x, 1
    while keeps < sections:
        if keeps > 1:
            x = jnp.where(section < keeps // 2, x, received)
        pairs = [(i, i + keeps) for i in range(keeps) if i + keeps < sections]
        received = lax.ppermute(x, "lag", pairs)
        keeps *= 2
    return x, received, max(keeps // 2, 1)


def body(incident, pending, self_inverse, retarded, block_rows, block_sources, owner_map):
    steps, unknowns, columns = incident.shape
    per_patch, size, _ = self_inverse.shape
    listed = retarded.shape[2]
    patches = lax.axis_size("patch")
    bf16, f32 = jnp.bfloat16, jnp.float32
    all_flops = 2 * unknowns * patches * size * columns
    solve_flops = 12 * unknowns * size * columns

    def exchange(x):
        return lax.all_to_all(x, "patch", split_axis=0, concat_axis=0, tiled=True)

    wanted = call(
        lambda *refs: request_kernel(per_patch, *refs),
        shape((patches, 1, 128), jnp.int32),
        [SMEM, SMEM],
        0,
        patches * 512,
    )(block_sources, owner_map)
    asked = exchange(wanted)
    own, received, keeps = spread(pending[0])
    field = jnp.where(lax.axis_index("lag") < keeps, own, received)
    current = call(
        lambda *refs: first_kernel(0, *refs),
        shape((unknowns, columns), bf16),
        [VMEM] * 3,
        solve_flops,
        4 * unknowns * columns,
    )(incident, field, self_inverse)
    panel = call(
        lambda *refs: panel_kernel(per_patch, *refs),
        shape((unknowns, patches * size), bf16),
        [SMEM, SMEM, SMEM, VMEM],
        0,
        listed * size * size * 4 + unknowns * patches * size * 2,
    )(block_rows, block_sources, owner_map, retarded)

    own, received = current, current
    field = pending[0]
    currents = []
    for time_step in range(steps):
        outgoing, current = call(
            lambda *refs: pack_kernel(keeps, *refs),
            (shape((patches, size, columns), bf16), shape((unknowns, columns), bf16)),
            [SMEM, VMEM, VMEM],
            0,
            4 * patches * size * columns,
        )(asked, own, received)
        currents.append(current)
        arrived = exchange(outgoing)
        field = shifted(field)
        if time_step + 1 < steps:
            field, current = call(
                lambda *refs, n=time_step + 1: step_kernel(n, *refs),
                (shape((unknowns, columns), f32), shape((unknowns, columns), bf16)),
                [VMEM] * 5,
                all_flops + solve_flops,
                2 * unknowns * patches * size,
            )(panel, arrived, field, incident, self_inverse)
            own, received, keeps = spread(current)
        else:
            field = call(
                last_kernel,
                shape((unknowns, columns), f32),
                [VMEM] * 3,
                all_flops,
                2 * unknowns * patches * size,
            )(panel, arrived, field)
    return jnp.stack(currents), field[None]


def solution(mesh):
    in_specs = (
        P(None, "patch", None),
        P("lag", "patch", None),
        P("patch", None, None),
        P("lag", "patch", None, None, None),
        P("lag", "patch", None),
        P("lag", "patch", None),
        P(),
    )
    out_specs = (P(None, "patch", None), P("lag", "patch", None))
    return jax.shard_map(body, mesh=mesh, in_specs=in_specs, out_specs=out_specs, check_vma=False)
```

```python
import jax
import jax.numpy as jnp
from jax import lax
from jax.experimental import pallas as pl
from jax.experimental.pallas import tpu as pltpu
from jax.sharding import PartitionSpec as P

VMEM = pl.BlockSpec(memory_space=pltpu.VMEM)
SMEM = pl.BlockSpec(memory_space=pltpu.SMEM)
HBM = pl.BlockSpec(memory_space=pltpu.HBM)
ANY = pl.BlockSpec(memory_space=pl.ANY)
DMA = pltpu.SemaphoreType.DMA
MIB = 1 << 20


def call(kernel, outs, in_specs, out_specs, scratch=(), flops=0, nbytes=MIB, aliases=None):
    return pl.pallas_call(
        kernel,
        out_shape=outs,
        in_specs=in_specs,
        out_specs=out_specs,
        scratch_shapes=scratch,
        input_output_aliases=aliases or {},
        cost_estimate=pl.CostEstimate(flops=flops, bytes_accessed=nbytes, transcendentals=0),
        compiler_params=pltpu.CompilerParams(vmem_limit_bytes=32 * MIB),
    )


def shape(dims, dtype):
    return jax.ShapeDtypeStruct(dims, dtype)


def started(*copies):
    copies = [pltpu.make_async_copy(*copy) for copy in copies]
    for copy in copies:
        copy.start()
    return copies


def request_kernel(per_patch, sources_hbm, owner_hbm, wanted, sources, owner_map, sems):
    copies = started(
        (sources_hbm, sources, sems.at[0]),
        (owner_hbm, owner_map, sems.at[1]),
    )
    patch = lax.broadcasted_iota(jnp.int32, wanted.shape, 0)
    for copy in copies:
        copy.wait()

    def entry(j, table):
        source = sources[0, 0, j]
        storage = owner_map[jnp.maximum(source, 0)]
        here = (patch == storage // per_patch) & (source >= 0)
        return jnp.where(here, storage % per_patch, table)

    wanted[...] = lax.fori_loop(
        0, sources.shape[2], entry, jnp.full(wanted.shape, -1, jnp.int32), unroll=8
    )


def panel_kernel(per_patch, rows, sources, owner_map, retarded, panel):
    size = retarded.shape[-1]
    panel[...] = jnp.zeros_like(panel)

    def entry(j, carry):
        source = sources[0, 0, j]

        @pl.when(source >= 0)
        def _():
            owner = owner_map[source] // per_patch
            row = pl.multiple_of(rows[0, 0, j] * size, size)
            column = pl.multiple_of(owner * size, size)
            block = retarded[0, 0, j]
            high = block.astype(panel.dtype)
            low = (block - high.astype(jnp.float32)).astype(panel.dtype)
            panel[0, pl.ds(row, size), pl.ds(column, size)] = high
            panel[1, pl.ds(row, size), pl.ds(column, size)] = low

        return carry

    lax.fori_loop(0, sources.shape[2], entry, 0)


def solved(excess, self_inverse):
    blocks, size, _ = self_inverse.shape
    parts = [
        jnp.dot(
            self_inverse[k],
            excess[k * size : (k + 1) * size],
            precision=lax.Precision.HIGHEST,
            preferred_element_type=jnp.float32,
        )
        for k in range(blocks)
    ]
    return jnp.concatenate(parts, axis=0).astype(jnp.bfloat16)


def product(panel, arrived):
    patches, size, columns = arrived.shape
    flat = arrived[...].reshape(patches * size, columns)
    high = jnp.dot(panel[0], flat, preferred_element_type=jnp.float32)
    return high + jnp.dot(panel[1], flat, preferred_element_type=jnp.float32)


def first_kernel(keeps, incident_hbm, own, received, inverse_hbm, current, incident, field, inverse, sems):
    copies = started(
        (incident_hbm.at[0], incident, sems.at[0]),
        (inverse_hbm, inverse, sems.at[1]),
    )
    mine = lax.axis_index("lag") < keeps

    @pl.when(mine)
    def _():
        started((own, field, sems.at[2]))[0].wait()

    @pl.when(jnp.logical_not(mine))
    def _():
        started((received, field, sems.at[2]))[0].wait()

    for copy in copies:
        copy.wait()
    current[...] = solved(incident[...].astype(jnp.float32) - field[...], inverse)


def solve_kernel(
    step, panel, arrived, field_hbm, incident_hbm, inverse_hbm, current, field, incident, inverse, sems
):
    @pl.when(lax.axis_index("lag") == 0)
    def _():
        copies = started(
            (field_hbm, field, sems.at[0]),
            (incident_hbm.at[step], incident, sems.at[1]),
            (inverse_hbm, inverse, sems.at[2]),
        )
        fresh = product(panel, arrived)
        for copy in copies:
            copy.wait()
        excess = incident[...].astype(jnp.float32) - (field[...] + fresh)
        current[...] = solved(excess, inverse)


def partial_kernel(panel, arrived, field_hbm, after, partial_hbm, field, sem):
    del after

    @pl.when(lax.axis_index("lag") > 0)
    def _():
        (copy,) = started((field_hbm, field, sem))
        fresh = product(panel, arrived)
        copy.wait()
        field[...] = field[...] + fresh
        started((field, partial_hbm, sem))[0].wait()


def ahead_kernel(panel, arrived, field_hbm, ahead, field, sem):
    (copy,) = started((field_hbm, field, sem))
    fresh = product(panel, arrived)
    copy.wait()
    ahead[...] = field[...] + fresh


def pack_kernel(step, keeps, asked, own, received, *refs):
    outgoing, currents, sems = refs[-3:]
    patches, size, _ = outgoing.shape

    def send(current):
        copies = [(current, currents.at[step], sems.at[patches])]
        for q in range(patches):
            start = pl.multiple_of(jnp.maximum(asked[q, 0, 0], 0) * size, size)
            copies.append((current.at[pl.ds(start, size)], outgoing.at[q], sems.at[q]))
        for copy in started(*copies):
            copy.wait()

    mine = lax.axis_index("lag") < keeps
    pl.when(mine)(lambda: send(own))
    pl.when(jnp.logical_not(mine))(lambda: send(received))


def shifted(x):
    sections = lax.axis_size("lag")
    return lax.ppermute(x, "lag", [(i, i - 1) for i in range(1, sections)])


def spread(x):
    sections = lax.axis_size("lag")
    section = lax.axis_index("lag")
    received, keeps = x, 1
    while keeps < sections:
        if keeps > 1:
            x = jnp.where(section < keeps // 2, x, received)
        pairs = [(i, i + keeps) for i in range(keeps) if i + keeps < sections]
        received = lax.ppermute(x, "lag", pairs)
        keeps *= 2
    return x, received, max(keeps // 2, 1)


def body(incident, pending, self_inverse, retarded, block_rows, block_sources, owner_map):
    steps, unknowns, columns = incident.shape
    per_patch, size, _ = self_inverse.shape
    listed = retarded.shape[2]
    patches = lax.axis_size("patch")
    bf16, f32 = jnp.bfloat16, jnp.float32
    all_flops = 4 * unknowns * patches * size * columns
    solve_flops = 12 * unknowns * size * columns
    panel_bytes = 4 * unknowns * patches * size
    column = (unknowns, columns)

    def exchange(x):
        return lax.all_to_all(x, "patch", split_axis=0, concat_axis=0, tiled=True)

    wanted = call(
        lambda *refs: request_kernel(per_patch, *refs),
        shape((patches, 1, 128), jnp.int32),
        [HBM, HBM],
        VMEM,
        [
            pltpu.SMEM(block_sources.shape, jnp.int32),
            pltpu.SMEM(owner_map.shape, jnp.int32),
            DMA((2,)),
        ],
    )(block_sources, owner_map)
    asked = exchange(wanted)
    own, received, keeps = spread(pending[0])
    current = call(
        lambda *refs: first_kernel(keeps, *refs),
        shape(column, bf16),
        [HBM] * 4,
        VMEM,
        [
            pltpu.VMEM(column, bf16),
            pltpu.VMEM(column, f32),
            pltpu.VMEM(self_inverse.shape, f32),
            DMA((3,)),
        ],
        solve_flops,
    )(incident, own, received, self_inverse)
    panel = call(
        lambda *refs: panel_kernel(per_patch, *refs),
        shape((2, unknowns, patches * size), bf16),
        [SMEM, SMEM, SMEM, VMEM],
        VMEM,
        nbytes=listed * size * size * 4 + panel_bytes,
    )(block_rows, block_sources, owner_map, retarded)

    own, received = current, current
    field = pending[0]
    currents = []
    for step in range(steps):
        outgoing, *currents = call(
            lambda *refs, n=step: pack_kernel(n, keeps, *refs),
            (shape((patches, size, columns), bf16), shape(incident.shape, bf16)),
            [SMEM, VMEM, VMEM] + [HBM] * len(currents),
            (HBM, HBM),
            [DMA((patches + 1,))],
            nbytes=4 * patches * size * columns,
            aliases={3: 1} if currents else None,
        )(asked, own, received, *currents)
        arrived = exchange(outgoing)
        field = shifted(field)
        if step + 1 < steps:
            current = call(
                lambda *refs, n=step + 1: solve_kernel(n, *refs),
                shape(column, bf16),
                [VMEM, VMEM, HBM, HBM, HBM],
                VMEM,
                [
                    pltpu.VMEM(column, f32),
                    pltpu.VMEM(column, bf16),
                    pltpu.VMEM(self_inverse.shape, f32),
                    DMA((3,)),
                ],
                all_flops + solve_flops,
                panel_bytes,
            )(panel, arrived, field, incident, self_inverse)
            own, received, keeps = spread(current)
            field = call(
                partial_kernel,
                shape(column, f32),
                [VMEM, VMEM, HBM, ANY],
                HBM,
                [pltpu.VMEM(column, f32), DMA],
                all_flops,
                panel_bytes,
            )(panel, arrived, field, current)
        else:
            field = call(
                ahead_kernel,
                shape(column, f32),
                [VMEM, VMEM, HBM],
                VMEM,
                [pltpu.VMEM(column, f32), DMA],
                all_flops,
                panel_bytes,
            )(panel, arrived, field)
    return currents[0], field[None]


def solution(mesh):
    in_specs = (
        P(None, "patch", None),
        P("lag", "patch", None),
        P("patch", None, None),
        P("lag", "patch", None, None, None),
        P("lag", "patch", None),
        P("lag", "patch", None),
        P(),
    )
    out_specs = (P(None, "patch", None), P("lag", "patch", None))
    return jax.shard_map(body, mesh=mesh, in_specs=in_specs, out_specs=out_specs, check_vma=False)
```

```python
import jax
import jax.numpy as jnp
from jax import lax
from jax.experimental import pallas as pl
from jax.experimental.pallas import tpu as pltpu
from jax.sharding import PartitionSpec as P

VMEM = pl.BlockSpec(memory_space=pltpu.VMEM)
SMEM = pl.BlockSpec(memory_space=pltpu.SMEM)
HBM = pl.BlockSpec(memory_space=pltpu.HBM)
ANY = pl.BlockSpec(memory_space=pl.ANY)
DMA = pltpu.SemaphoreType.DMA
MIB = 1 << 20


def call(kernel, outs, in_specs, out_specs, scratch=(), flops=0, nbytes=0, vmem=0, aliases=None):
    return pl.pallas_call(
        kernel,
        out_shape=outs,
        in_specs=in_specs,
        out_specs=out_specs,
        scratch_shapes=scratch,
        input_output_aliases=aliases or {},
        cost_estimate=pl.CostEstimate(flops=flops, bytes_accessed=nbytes, transcendentals=0),
        compiler_params=pltpu.CompilerParams(vmem_limit_bytes=vmem + 6 * MIB),
    )


def shape(dims, dtype):
    return jax.ShapeDtypeStruct(dims, dtype)


def started(*copies):
    copies = [pltpu.make_async_copy(*copy) for copy in copies]
    for copy in copies:
        copy.start()
    return copies


def request_kernel(per_patch, sources_hbm, owner_hbm, wanted, sources, owner_map, sems):
    copies = started(
        (sources_hbm, sources, sems.at[0]),
        (owner_hbm, owner_map, sems.at[1]),
    )
    patch = lax.broadcasted_iota(jnp.int32, wanted.shape, 0)
    for copy in copies:
        copy.wait()

    def entry(j, table):
        source = sources[0, 0, j]
        storage = owner_map[jnp.maximum(source, 0)]
        here = (patch == storage // per_patch) & (source >= 0)
        return jnp.where(here, storage % per_patch, table)

    wanted[...] = lax.fori_loop(
        0, sources.shape[2], entry, jnp.full(wanted.shape, -1, jnp.int32), unroll=8
    )


def panel_kernel(per_patch, rows, sources, owner_map, retarded, panel):
    size = retarded.shape[-1]
    panel[...] = jnp.zeros_like(panel)

    def entry(j, carry):
        source = sources[0, 0, j]

        @pl.when(source >= 0)
        def _():
            owner = owner_map[source] // per_patch
            row = pl.multiple_of(rows[0, 0, j] * size, size)
            column = pl.multiple_of(owner * size, size)
            block = retarded[0, 0, j]
            high = block.astype(panel.dtype)
            low = (block - high.astype(jnp.float32)).astype(panel.dtype)
            panel[0, pl.ds(row, size), pl.ds(column, size)] = high
            panel[1, pl.ds(row, size), pl.ds(column, size)] = low

        return carry

    lax.fori_loop(0, sources.shape[2], entry, 0)


def solved(excess, self_inverse):
    blocks, size, _ = self_inverse.shape
    parts = [
        jnp.dot(
            self_inverse[k],
            excess[k * size : (k + 1) * size],
            precision=lax.Precision.HIGHEST,
            preferred_element_type=jnp.float32,
        )
        for k in range(blocks)
    ]
    return jnp.concatenate(parts, axis=0).astype(jnp.bfloat16)


def product(panel, arrived):
    patches, size, columns = arrived.shape
    flat = arrived[...].reshape(patches * size, columns)
    high = jnp.dot(panel[0], flat, preferred_element_type=jnp.float32)
    return high + jnp.dot(panel[1], flat, preferred_element_type=jnp.float32)


def first_kernel(incident_hbm, field_hbm, inverse_hbm, after, current, incident, field, inverse, sems):
    del after

    @pl.when(lax.axis_index("lag") == 0)
    def _():
        copies = started(
            (incident_hbm.at[0], incident, sems.at[0]),
            (inverse_hbm, inverse, sems.at[1]),
            (field_hbm, field, sems.at[2]),
        )
        for copy in copies:
            copy.wait()
        current[...] = solved(incident[...].astype(jnp.float32) - field[...], inverse)


def solve_kernel(
    step, panel, arrived, field_hbm, incident_hbm, inverse_hbm, current, incident, field, inverse, sems
):
    @pl.when(lax.axis_index("lag") == 0)
    def _():
        copies = started(
            (field_hbm, field, sems.at[0]),
            (incident_hbm.at[step], incident, sems.at[1]),
            (inverse_hbm, inverse, sems.at[2]),
        )
        fresh = product(panel, arrived)
        for copy in copies:
            copy.wait()
        excess = incident[...].astype(jnp.float32) - (field[...] + fresh)
        current[...] = solved(excess, inverse)


def partial_kernel(panel, arrived, field_hbm, after, partial_hbm, field, sem):
    del after

    @pl.when(lax.axis_index("lag") > 0)
    def _():
        (copy,) = started((field_hbm, field, sem))
        fresh = product(panel, arrived)
        copy.wait()
        field[...] = field[...] + fresh
        started((field, partial_hbm, sem))[0].wait()


def ahead_kernel(panel, arrived, field_hbm, ahead, field, sem):
    (copy,) = started((field_hbm, field, sem))
    fresh = product(panel, arrived)
    copy.wait()
    ahead[...] = field[...] + fresh


def pack_kernel(step, keeps, early, asked_any, current, *refs):
    outgoing, currents, asked, sems = refs[-4:]
    patches, size, _ = outgoing.shape
    section = lax.axis_index("lag")

    @pl.when(section < keeps if early else section >= keeps)
    def _():
        (copy,) = started((asked_any, asked, sems.at[0]))
        (whole,) = started((current, currents.at[step], sems.at[patches]))
        copy.wait()
        copies = []
        for q in range(patches):
            start = pl.multiple_of(jnp.maximum(asked[q, 0, 0], 0) * size, size)
            copies.append((current.at[pl.ds(start, size)], outgoing.at[q], sems.at[q]))
        for copy in started(*copies):
            copy.wait()
        whole.wait()


def shifted(x):
    sections = lax.axis_size("lag")
    return lax.ppermute(x, "lag", [(i, i - 1) for i in range(1, sections)])


def spread(x):
    sections = lax.axis_size("lag")
    section = lax.axis_index("lag")
    received, keeps = x, 1
    while keeps < sections:
        if keeps > 1:
            x = jnp.where(section < keeps // 2, x, received)
        pairs = [(i, i + keeps) for i in range(keeps) if i + keeps < sections]
        received = lax.ppermute(x, "lag", pairs)
        keeps *= 2
    return x, received, max(keeps // 2, 1)


def body(incident, pending, self_inverse, retarded, block_rows, block_sources, owner_map):
    steps, unknowns, columns = incident.shape
    per_patch, size, _ = self_inverse.shape
    listed = retarded.shape[2]
    patches = lax.axis_size("patch")
    bf16, f32 = jnp.bfloat16, jnp.float32
    all_flops = 4 * unknowns * patches * size * columns
    solve_flops = 12 * unknowns * size * columns
    panel_bytes = 4 * unknowns * patches * size
    column = (unknowns, columns)

    column_bytes = 4 * unknowns * columns
    arrived_bytes = 2 * patches * size * columns

    def exchange(x):
        return lax.all_to_all(x, "patch", split_axis=0, concat_axis=0, tiled=True)

    def pack(step, keeps, early, current, filled, after):
        held = [x for x in filled if x is not None]
        first_held = 2 + len(after)
        aliases = {}
        for out, x in enumerate(filled):
            if x is not None:
                aliases[first_held + len(aliases)] = out
        return call(
            lambda *refs: pack_kernel(step, keeps, early, *refs),
            (shape((patches, size, columns), bf16), shape(incident.shape, bf16)),
            [ANY, VMEM] + [ANY] * len(after) + [HBM] * len(held),
            (HBM, HBM),
            [pltpu.SMEM(asked.shape, jnp.int32), DMA((patches + 1,))],
            vmem=column_bytes,
            aliases=aliases,
        )(asked, current, *after, *held)

    wanted = call(
        lambda *refs: request_kernel(per_patch, *refs),
        shape((patches, 1, 128), jnp.int32),
        [HBM, HBM],
        VMEM,
        [
            pltpu.SMEM(block_sources.shape, jnp.int32),
            pltpu.SMEM(owner_map.shape, jnp.int32),
            DMA((2,)),
        ],
    )(block_sources, owner_map)
    asked = exchange(wanted)
    solve_scratch = [
        pltpu.VMEM(column, bf16),
        pltpu.VMEM(column, f32),
        pltpu.VMEM(self_inverse.shape, f32),
        DMA((3,)),
    ]
    current = call(
        first_kernel,
        shape(column, bf16),
        [HBM, HBM, HBM, ANY],
        VMEM,
        solve_scratch,
        solve_flops,
        vmem=4 * column_bytes,
    )(incident, pending[0], self_inverse, wanted)
    panel = call(
        lambda *refs: panel_kernel(per_patch, *refs),
        shape((2, unknowns, patches * size), bf16),
        [SMEM, SMEM, SMEM, VMEM],
        VMEM,
        nbytes=listed * size * size * 4 + panel_bytes,
        vmem=listed * size * size * 4 + panel_bytes,
    )(block_rows, block_sources, owner_map, retarded)

    field = pending[0]
    currents = None
    after = []
    for step in range(steps):
        own, received, keeps = spread(current)
        outgoing, currents = pack(step, keeps, True, own, (None, currents), [])
        if lax.axis_size("lag") > 1:
            outgoing, currents = pack(step, keeps, False, received, (outgoing, currents), after)
        arrived = exchange(outgoing)
        field = shifted(field)
        if step + 1 < steps:
            current = call(
                lambda *refs, n=step + 1: solve_kernel(n, *refs),
                shape(column, bf16),
                [VMEM, VMEM, HBM, HBM, HBM],
                VMEM,
                solve_scratch,
                all_flops + solve_flops,
                panel_bytes + arrived_bytes,
                panel_bytes + arrived_bytes + 6 * column_bytes,
            )(panel, arrived, field, incident, self_inverse)
            field = call(
                partial_kernel,
                shape(column, f32),
                [VMEM, VMEM, HBM, ANY],
                HBM,
                [pltpu.VMEM(column, f32), DMA],
                all_flops,
                panel_bytes + arrived_bytes,
                panel_bytes + arrived_bytes + 4 * column_bytes,
            )(panel, arrived, field, current)
            after = [field]
        else:
            field = call(
                ahead_kernel,
                shape(column, f32),
                [VMEM, VMEM, HBM],
                VMEM,
                [pltpu.VMEM(column, f32), DMA],
                all_flops,
                panel_bytes + arrived_bytes,
                panel_bytes + arrived_bytes + 4 * column_bytes,
            )(panel, arrived, field)
    return currents, field[None]


def solution(mesh):
    in_specs = (
        P(None, "patch", None),
        P("lag", "patch", None),
        P("patch", None, None),
        P("lag", "patch", None, None, None),
        P("lag", "patch", None),
        P("lag", "patch", None),
        P(),
    )
    out_specs = (P(None, "patch", None), P("lag", "patch", None))
    return jax.shard_map(body, mesh=mesh, in_specs=in_specs, out_specs=out_specs, check_vma=False)
```

```python
import jax
import jax.numpy as jnp
from jax import lax
from jax.experimental import pallas as pl
from jax.experimental.pallas import tpu as pltpu
from jax.sharding import PartitionSpec as P

VMEM = pl.BlockSpec(memory_space=pltpu.VMEM)
SMEM = pl.BlockSpec(memory_space=pltpu.SMEM)
HBM = pl.BlockSpec(memory_space=pltpu.HBM)
ANY = pl.BlockSpec(memory_space=pl.ANY)
DMA = pltpu.SemaphoreType.DMA
MIB = 1 << 20


def call(kernel, outs, in_specs, out_specs, scratch=(), flops=0, nbytes=0, vmem=0, aliases=None):
    return pl.pallas_call(
        kernel,
        out_shape=outs,
        in_specs=in_specs,
        out_specs=out_specs,
        scratch_shapes=scratch,
        input_output_aliases=aliases or {},
        cost_estimate=pl.CostEstimate(flops=flops, bytes_accessed=nbytes, transcendentals=0),
        compiler_params=pltpu.CompilerParams(vmem_limit_bytes=vmem + 6 * MIB if vmem else None),
    )


def shape(dims, dtype):
    return jax.ShapeDtypeStruct(dims, dtype)


def started(*copies):
    copies = [pltpu.make_async_copy(*copy) for copy in copies]
    for copy in copies:
        copy.start()
    return copies


def request_kernel(per_patch, sources_hbm, owner_hbm, wanted, sources, owner_map, sems):
    copies = started(
        (sources_hbm, sources, sems.at[0]),
        (owner_hbm, owner_map, sems.at[1]),
    )
    patch = lax.broadcasted_iota(jnp.int32, wanted.shape, 0)
    for copy in copies:
        copy.wait()

    def entry(j, table):
        source = sources[0, 0, j]
        storage = owner_map[jnp.maximum(source, 0)]
        here = (patch == storage // per_patch) & (source >= 0)
        return jnp.where(here, storage % per_patch, table)

    wanted[...] = lax.fori_loop(
        0, sources.shape[2], entry, jnp.full(wanted.shape, -1, jnp.int32), unroll=8
    )


def panel_kernel(per_patch, rows, sources, owner_map, retarded, high, low):
    size = retarded.shape[-1]
    high[...] = jnp.zeros_like(high)
    low[...] = jnp.zeros_like(low)

    def entry(j, carry):
        source = sources[0, 0, j]

        @pl.when(source >= 0)
        def _():
            owner = owner_map[source] // per_patch
            row = pl.multiple_of(rows[0, 0, j] * size, size)
            column = pl.multiple_of(owner * size, size)
            block = retarded[0, 0, j]
            rounded = block.astype(high.dtype)
            rest = (block - rounded.astype(jnp.float32)).astype(low.dtype)
            high[pl.ds(row, size), pl.ds(column, size)] = rounded
            low[pl.ds(row, size), pl.ds(column, size)] = rest

        return carry

    lax.fori_loop(0, sources.shape[2], entry, 0)


def solved(excess, self_inverse):
    blocks, size, _ = self_inverse.shape
    parts = [
        jnp.dot(
            self_inverse[k],
            excess[k * size : (k + 1) * size],
            precision=lax.Precision.HIGHEST,
            preferred_element_type=jnp.float32,
        )
        for k in range(blocks)
    ]
    return jnp.concatenate(parts, axis=0).astype(jnp.bfloat16)


def product(high, low, arrived):
    patches, size, columns = arrived.shape
    flat = arrived[...].reshape(patches * size, columns)
    fresh = jnp.dot(high[...], flat, preferred_element_type=jnp.float32)
    return fresh + jnp.dot(low[...], flat, preferred_element_type=jnp.float32)


def first_kernel(incident_hbm, field_hbm, inverse_hbm, after, current, incident, field, inverse, sems):
    del after

    @pl.when(lax.axis_index("lag") == 0)
    def _():
        copies = started(
            (incident_hbm.at[0], incident, sems.at[0]),
            (inverse_hbm, inverse, sems.at[1]),
            (field_hbm, field, sems.at[2]),
        )
        for copy in copies:
            copy.wait()
        current[...] = solved(incident[...].astype(jnp.float32) - field[...], inverse)


def solve_kernel(
    step, high, low, arrived, field_hbm, incident_hbm, inverse_hbm, current, incident, field, inverse, sems
):
    @pl.when(lax.axis_index("lag") == 0)
    def _():
        copies = started(
            (field_hbm, field, sems.at[0]),
            (incident_hbm.at[step], incident, sems.at[1]),
            (inverse_hbm, inverse, sems.at[2]),
        )
        fresh = product(high, low, arrived)
        for copy in copies:
            copy.wait()
        excess = incident[...].astype(jnp.float32) - (field[...] + fresh)
        current[...] = solved(excess, inverse)


def partial_kernel(high, low, arrived, field_hbm, after, partial_hbm, field, sem):
    del after

    @pl.when(lax.axis_index("lag") > 0)
    def _():
        (copy,) = started((field_hbm, field, sem))
        fresh = product(high, low, arrived)
        copy.wait()
        field[...] = field[...] + fresh
        started((field, partial_hbm, sem))[0].wait()


def ahead_kernel(high, low, arrived, field_hbm, ahead, field, sem):
    (copy,) = started((field_hbm, field, sem))
    fresh = product(high, low, arrived)
    copy.wait()
    ahead[...] = field[...] + fresh


def pack_kernel(step, keeps, early, asked, current, *refs):
    outgoing, currents, sems = refs[-3:]
    patches, size, _ = outgoing.shape
    section = lax.axis_index("lag")

    @pl.when(section < keeps if early else section >= keeps)
    def _():
        copies = []
        for q in range(patches):
            block = jnp.max(jnp.maximum(asked[q], 0))
            start = pl.multiple_of(block * size, size)
            copies.append((current.at[pl.ds(start, size)], outgoing.at[q], sems.at[q]))
        copies.append((current, currents.at[step], sems.at[patches]))
        for copy in started(*copies):
            copy.wait()


def shifted(x):
    sections = lax.axis_size("lag")
    return lax.ppermute(x, "lag", [(i, i - 1) for i in range(1, sections)])


def spread(x):
    sections = lax.axis_size("lag")
    section = lax.axis_index("lag")
    received, keeps = x, 1
    while keeps < sections:
        if keeps > 1:
            x = jnp.where(section < keeps // 2, x, received)
        pairs = [(i, i + keeps) for i in range(keeps) if i + keeps < sections]
        received = lax.ppermute(x, "lag", pairs)
        keeps *= 2
    return x, received, max(keeps // 2, 1)


def body(incident, pending, self_inverse, retarded, block_rows, block_sources, owner_map):
    steps, unknowns, columns = incident.shape
    per_patch, size, _ = self_inverse.shape
    listed = retarded.shape[2]
    patches = lax.axis_size("patch")
    bf16, f32 = jnp.bfloat16, jnp.float32
    all_flops = 4 * unknowns * patches * size * columns
    solve_flops = 12 * unknowns * size * columns
    panel_bytes = 4 * unknowns * patches * size
    column = (unknowns, columns)

    column_bytes = 4 * unknowns * columns
    arrived_bytes = 2 * patches * size * columns

    def exchange(x):
        return lax.all_to_all(x, "patch", split_axis=0, concat_axis=0, tiled=True)

    def pack(step, keeps, early, current, filled, after):
        held = [x for x in filled if x is not None]
        first_held = 2 + len(after)
        aliases = {}
        for out, x in enumerate(filled):
            if x is not None:
                aliases[first_held + len(aliases)] = out
        return call(
            lambda *refs: pack_kernel(step, keeps, early, *refs),
            (shape((patches, size, columns), bf16), shape(incident.shape, bf16)),
            [VMEM, VMEM] + [ANY] * len(after) + [HBM] * len(held),
            (HBM, HBM),
            [DMA((patches + 1,))],
            vmem=column_bytes,
            aliases=aliases,
        )(asked, current, *after, *held)

    wanted = call(
        lambda *refs: request_kernel(per_patch, *refs),
        shape((patches, 1, 128), jnp.int32),
        [HBM, HBM],
        VMEM,
        [
            pltpu.SMEM(block_sources.shape, jnp.int32),
            pltpu.SMEM(owner_map.shape, jnp.int32),
            DMA((2,)),
        ],
    )(block_sources, owner_map)
    asked = exchange(wanted)
    solve_scratch = [
        pltpu.VMEM(column, bf16),
        pltpu.VMEM(column, f32),
        pltpu.VMEM(self_inverse.shape, f32),
        DMA((3,)),
    ]
    current = call(
        first_kernel,
        shape(column, bf16),
        [HBM, HBM, HBM, ANY],
        VMEM,
        solve_scratch,
        solve_flops,
    )(incident, pending[0], self_inverse, wanted)
    high, low = call(
        lambda *refs: panel_kernel(per_patch, *refs),
        (shape((unknowns, patches * size), bf16),) * 2,
        [SMEM, SMEM, SMEM, VMEM],
        (VMEM, VMEM),
        nbytes=listed * size * size * 4 + panel_bytes,
        vmem=listed * size * size * 4 + panel_bytes,
    )(block_rows, block_sources, owner_map, retarded)

    field = pending[0]
    currents = None
    after = []
    for step in range(steps):
        own, received, keeps = spread(current)
        outgoing, currents = pack(step, keeps, True, own, (None, currents), [])
        if lax.axis_size("lag") > 1:
            outgoing, currents = pack(step, keeps, False, received, (outgoing, currents), after)
        arrived = exchange(outgoing)
        field = shifted(field)
        if step + 1 < steps:
            current = call(
                lambda *refs, n=step + 1: solve_kernel(n, *refs),
                shape(column, bf16),
                [VMEM, VMEM, VMEM, HBM, HBM, HBM],
                VMEM,
                solve_scratch,
                all_flops + solve_flops,
                panel_bytes + arrived_bytes,
                panel_bytes + arrived_bytes + 6 * column_bytes,
            )(high, low, arrived, field, incident, self_inverse)
            field = call(
                partial_kernel,
                shape(column, f32),
                [VMEM, VMEM, VMEM, HBM, ANY],
                HBM,
                [pltpu.VMEM(column, f32), DMA],
                all_flops,
                panel_bytes + arrived_bytes,
                panel_bytes + arrived_bytes + 4 * column_bytes,
            )(high, low, arrived, field, current)
            after = [field]
        else:
            field = call(
                ahead_kernel,
                shape(column, f32),
                [VMEM, VMEM, VMEM, HBM],
                VMEM,
                [pltpu.VMEM(column, f32), DMA],
                all_flops,
                panel_bytes + arrived_bytes,
                panel_bytes + arrived_bytes + 4 * column_bytes,
            )(high, low, arrived, field)
    return currents, field[None]


def solution(mesh):
    in_specs = (
        P(None, "patch", None),
        P("lag", "patch", None),
        P("patch", None, None),
        P("lag", "patch", None, None, None),
        P("lag", "patch", None),
        P("lag", "patch", None),
        P(),
    )
    out_specs = (P(None, "patch", None), P("lag", "patch", None))
    return jax.shard_map(body, mesh=mesh, in_specs=in_specs, out_specs=out_specs, check_vma=False)
```

```python
import jax
import jax.numpy as jnp
from jax import lax
from jax.experimental import pallas as pl
from jax.experimental.pallas import tpu as pltpu
from jax.sharding import PartitionSpec as P

VMEM, HBM, ANY = pltpu.VMEM, pltpu.HBM, pl.ANY
DMA = pltpu.SemaphoreType.DMA
MIB = 1 << 20


def call(kernel, outs, ins, scratch=(), flops=0, nbytes=0, vmem=0, aliases=None):
    out_shape = tuple(space(dims, dtype) for space, dims, dtype in outs)
    out_specs = tuple(pl.BlockSpec(memory_space=space) for space, _, _ in outs)
    run = pl.pallas_call(
        kernel,
        out_shape=out_shape,
        in_specs=[pl.BlockSpec(memory_space=space) for space, _ in ins],
        out_specs=out_specs,
        scratch_shapes=scratch,
        input_output_aliases=aliases or {},
        cost_estimate=pl.CostEstimate(flops=flops, bytes_accessed=nbytes, transcendentals=0),
        compiler_params=pltpu.CompilerParams(vmem_limit_bytes=vmem + 6 * MIB),
    )
    results = run(*(pltpu.with_memory_space_constraint(x, space) for space, x in ins))
    return results if len(outs) > 1 else results[0]


def started(*copies):
    copies = [pltpu.make_async_copy(*copy) for copy in copies]
    for copy in copies:
        copy.start()
    return copies


def request_kernel(per_patch, sources_hbm, owner_hbm, wanted_hbm, wanted, sources, owner_map, sems):
    copies = started(
        (sources_hbm, sources, sems.at[0]),
        (owner_hbm, owner_map, sems.at[1]),
    )
    patch = lax.broadcasted_iota(jnp.int32, wanted.shape, 0)
    for copy in copies:
        copy.wait()

    def entry(j, table):
        source = sources[0, 0, j]
        storage = owner_map[jnp.maximum(source, 0)]
        here = (patch == storage // per_patch) & (source >= 0)
        return jnp.where(here, storage % per_patch, table)

    wanted[...] = lax.fori_loop(
        0, sources.shape[2], entry, jnp.full(wanted.shape, -1, jnp.int32), unroll=8
    )
    started((wanted, wanted_hbm, sems.at[0]))[0].wait()


def panel_kernel(per_patch, rows_hbm, sources_hbm, owner_hbm, retarded, panel, rows, sources, owner_map, parts, sems):
    size = retarded.shape[-1]
    slots, chunk = parts.shape[:2]
    chunks = retarded.shape[2] // chunk

    def fetch(c):
        part = retarded.at[0, 0, pl.ds(c * chunk, chunk)]
        return pltpu.make_async_copy(part, parts.at[c % slots], sems.at[c % slots])

    lists = started(
        (rows_hbm, rows, sems.at[slots]),
        (sources_hbm, sources, sems.at[slots + 1]),
        (owner_hbm, owner_map, sems.at[slots + 2]),
    )
    for c in range(min(slots, chunks)):
        fetch(c).start()
    panel[...] = jnp.zeros_like(panel)
    for copy in lists:
        copy.wait()

    def entry(c, k, carry):
        source = sources[0, 0, c * chunk + k]

        @pl.when(source >= 0)
        def _():
            owner = owner_map[source] // per_patch
            row = pl.multiple_of(rows[0, 0, c * chunk + k] * size, size)
            column = pl.multiple_of(owner * size, size)
            block = parts[c % slots, k]
            high = block.astype(panel.dtype)
            low = (block - high.astype(jnp.float32)).astype(panel.dtype)
            panel[0, pl.ds(row, size), pl.ds(column, size)] = high
            panel[1, pl.ds(row, size), pl.ds(column, size)] = low

        return carry

    for c in range(chunks):
        fetch(c).wait()
        lax.fori_loop(0, chunk, lambda k, carry, c=c: entry(c, k, carry), 0)
        if c + slots < chunks:
            fetch(c + slots).start()


def solved(excess, self_inverse):
    blocks, size, _ = self_inverse.shape
    parts = [
        jnp.dot(
            self_inverse[k],
            excess[k * size : (k + 1) * size],
            precision=lax.Precision.HIGHEST,
            preferred_element_type=jnp.float32,
        )
        for k in range(blocks)
    ]
    return jnp.concatenate(parts, axis=0).astype(jnp.bfloat16)


def product(panel, arrived):
    patches, size, columns = arrived.shape
    flat = arrived[...].reshape(patches * size, columns)
    fresh = jnp.dot(panel[0], flat, preferred_element_type=jnp.float32)
    return fresh + jnp.dot(panel[1], flat, preferred_element_type=jnp.float32)


def first_kernel(incident_hbm, field_hbm, inverse_hbm, after, current, incident, field, inverse, sems):
    del after

    @pl.when(lax.axis_index("lag") == 0)
    def _():
        copies = started(
            (incident_hbm.at[0], incident, sems.at[0]),
            (inverse_hbm, inverse, sems.at[1]),
            (field_hbm, field, sems.at[2]),
        )
        for copy in copies:
            copy.wait()
        current[...] = solved(incident[...].astype(jnp.float32) - field[...], inverse)


def solve_kernel(step, panel, arrived, field, incident_hbm, inverse_hbm, current, incident, inverse, sems):
    @pl.when(lax.axis_index("lag") == 0)
    def _():
        copies = started(
            (incident_hbm.at[step], incident, sems.at[0]),
            (inverse_hbm, inverse, sems.at[1]),
        )
        fresh = product(panel, arrived)
        for copy in copies:
            copy.wait()
        excess = incident[...].astype(jnp.float32) - (field[...] + fresh)
        current[...] = solved(excess, inverse)


def partial_kernel(panel, arrived, field, after, partial):
    del after

    @pl.when(lax.axis_index("lag") > 0)
    def _():
        partial[...] = field[...] + product(panel, arrived)


def ahead_kernel(panel, arrived, field, ahead_hbm, ahead, sem):
    ahead[...] = field[...] + product(panel, arrived)
    started((ahead, ahead_hbm, sem))[0].wait()


def pack_kernel(step, keeps, early, asked, current, *refs):
    outgoing, currents, sems = refs[-3:]
    patches, size, _ = outgoing.shape
    section = lax.axis_index("lag")

    @pl.when(section < keeps if early else section >= keeps)
    def _():
        copies = []
        for q in range(patches):
            block = jnp.max(jnp.maximum(asked[q], 0))
            start = pl.multiple_of(block * size, size)
            copies.append((current.at[pl.ds(start, size)], outgoing.at[q], sems.at[q]))
        copies.append((current, currents.at[step], sems.at[patches]))
        for copy in started(*copies):
            copy.wait()


def shifted(x):
    sections = lax.axis_size("lag")
    return lax.ppermute(x, "lag", [(i, i - 1) for i in range(1, sections)])


def spread(x):
    sections = lax.axis_size("lag")
    section = lax.axis_index("lag")
    received, keeps = x, 1
    while keeps < sections:
        if keeps > 1:
            x = jnp.where(section < keeps // 2, x, received)
        pairs = [(i, i + keeps) for i in range(keeps) if i + keeps < sections]
        received = lax.ppermute(x, "lag", pairs)
        keeps *= 2
    return x, received, max(keeps // 2, 1)


def body(incident, pending, self_inverse, retarded, block_rows, block_sources, owner_map):
    steps, unknowns, columns = incident.shape
    per_patch, size, _ = self_inverse.shape
    listed = retarded.shape[2]
    patches = lax.axis_size("patch")
    bf16, f32 = jnp.bfloat16, jnp.float32
    all_flops = 4 * unknowns * patches * size * columns
    solve_flops = 12 * unknowns * size * columns
    panel_bytes = 4 * unknowns * patches * size
    column = (unknowns, columns)

    column_bytes = 4 * unknowns * columns
    arrived_bytes = 2 * patches * size * columns

    def exchange(x):
        return lax.all_to_all(x, "patch", split_axis=0, concat_axis=0, tiled=True)

    def pack(step, keeps, early, current, filled, after):
        held = [x for x in filled if x is not None]
        aliases = {}
        for out, x in enumerate(filled):
            if x is not None:
                aliases[2 + len(after) + len(aliases)] = out
        return call(
            lambda *refs: pack_kernel(step, keeps, early, *refs),
            [(HBM, (patches, size, columns), bf16), (HBM, incident.shape, bf16)],
            [(VMEM, asked), (VMEM, current)] + [(VMEM, x) for x in after] + [(HBM, x) for x in held],
            [DMA((patches + 1,))],
            aliases=aliases,
        )

    wanted = call(
        lambda *refs: request_kernel(per_patch, *refs),
        [(HBM, (patches, 1, 128), jnp.int32)],
        [(HBM, block_sources), (HBM, owner_map)],
        [
            pltpu.VMEM((patches, 1, 128), jnp.int32),
            pltpu.SMEM(block_sources.shape, jnp.int32),
            pltpu.SMEM(owner_map.shape, jnp.int32),
            DMA((2,)),
        ],
    )
    asked = exchange(wanted)
    solve_scratch = [pltpu.VMEM(column, bf16), pltpu.VMEM(self_inverse.shape, f32), DMA((3,))]
    current = call(
        first_kernel,
        [(VMEM, column, bf16)],
        [(HBM, incident), (HBM, pending[0]), (HBM, self_inverse), (HBM, wanted)],
        [solve_scratch[0], pltpu.VMEM(column, f32), *solve_scratch[1:]],
        solve_flops,
    )
    chunk = max(n for n in range(1, 9) if listed % n == 0)
    panel = call(
        lambda *refs: panel_kernel(per_patch, *refs),
        [(VMEM, (2, unknowns, patches * size), bf16)],
        [(HBM, block_rows), (HBM, block_sources), (HBM, owner_map), (HBM, retarded)],
        [
            pltpu.SMEM(block_rows.shape, jnp.int32),
            pltpu.SMEM(block_sources.shape, jnp.int32),
            pltpu.SMEM(owner_map.shape, jnp.int32),
            pltpu.VMEM((3, chunk, size, size), f32),
            DMA((6,)),
        ],
        nbytes=listed * size * size * 4 + panel_bytes,
    )

    field = pending[0]
    currents = None
    after = []
    for step in range(steps):
        own, received, keeps = spread(current)
        outgoing, currents = pack(step, keeps, True, own, (None, currents), [])
        if lax.axis_size("lag") > 1:
            outgoing, currents = pack(step, keeps, False, received, (outgoing, currents), after)
        arrived = exchange(outgoing)
        field = shifted(field)
        if step + 1 < steps:
            current = call(
                lambda *refs, n=step + 1: solve_kernel(n, *refs),
                [(VMEM, column, bf16)],
                [(VMEM, panel), (VMEM, arrived), (VMEM, field), (HBM, incident), (HBM, self_inverse)],
                solve_scratch,
                all_flops + solve_flops,
                panel_bytes + arrived_bytes,
            )
            field = call(
                partial_kernel,
                [(VMEM, column, f32)],
                [(VMEM, panel), (VMEM, arrived), (VMEM, field), (VMEM, current)],
                [],
                all_flops,
                panel_bytes + arrived_bytes,
            )
            after = [field]
        else:
            field = call(
                ahead_kernel,
                [(HBM, column, f32)],
                [(VMEM, panel), (VMEM, arrived), (VMEM, field)],
                [pltpu.VMEM(column, f32), DMA],
                all_flops,
                panel_bytes + arrived_bytes,
            )
    return currents, field[None]


def solution(mesh):
    in_specs = (
        P(None, "patch", None),
        P("lag", "patch", None),
        P("patch", None, None),
        P("lag", "patch", None, None, None),
        P("lag", "patch", None),
        P("lag", "patch", None),
        P(),
    )
    out_specs = (P(None, "patch", None), P("lag", "patch", None))
    return jax.shard_map(body, mesh=mesh, in_specs=in_specs, out_specs=out_specs, check_vma=False)
```

```python
import jax
import jax.numpy as jnp
from jax import lax
from jax.experimental import pallas as pl
from jax.experimental.pallas import tpu as pltpu
from jax.sharding import PartitionSpec as P

VMEM, HBM, ANY = pltpu.VMEM, pltpu.HBM, pl.ANY
DMA = pltpu.SemaphoreType.DMA
MIB = 1 << 20


def call(kernel, outs, ins, scratch=(), flops=0, nbytes=0, vmem=0, aliases=None):
    out_shape = tuple(space(dims, dtype) for space, dims, dtype in outs)
    out_specs = tuple(pl.BlockSpec(memory_space=space) for space, _, _ in outs)
    run = pl.pallas_call(
        kernel,
        out_shape=out_shape,
        in_specs=[pl.BlockSpec(memory_space=space) for space, _ in ins],
        out_specs=out_specs,
        scratch_shapes=scratch,
        input_output_aliases=aliases or {},
        cost_estimate=pl.CostEstimate(flops=flops, bytes_accessed=nbytes, transcendentals=0),
        compiler_params=pltpu.CompilerParams(vmem_limit_bytes=vmem + 6 * MIB),
    )
    results = run(*(pltpu.with_memory_space_constraint(x, space) for space, x in ins))
    return results if len(outs) > 1 else results[0]


def started(*copies):
    copies = [pltpu.make_async_copy(*copy) for copy in copies]
    for copy in copies:
        copy.start()
    return copies


def request_kernel(per_patch, sources_hbm, owner_hbm, wanted_hbm, wanted, sources, owner_map, sems):
    copies = started(
        (sources_hbm, sources, sems.at[0]),
        (owner_hbm, owner_map, sems.at[1]),
    )
    patch = lax.broadcasted_iota(jnp.int32, wanted.shape, 0)
    for copy in copies:
        copy.wait()

    def entry(j, table):
        source = sources[0, 0, j]
        storage = owner_map[jnp.maximum(source, 0)]
        here = (patch == storage // per_patch) & (source >= 0)
        return jnp.where(here, storage % per_patch, table)

    wanted[...] = lax.fori_loop(
        0, sources.shape[2], entry, jnp.full(wanted.shape, -1, jnp.int32), unroll=8
    )
    started((wanted, wanted_hbm, sems.at[0]))[0].wait()


def panel_kernel(
    per_patch, rows_hbm, sources_hbm, owner_hbm, retarded, high, low_hbm, rows, sources, owner_map, parts, low, sems
):
    size = retarded.shape[-1]
    slots, chunk = parts.shape[:2]
    chunks = retarded.shape[2] // chunk

    def fetch(c):
        part = retarded.at[0, 0, pl.ds(c * chunk, chunk)]
        return pltpu.make_async_copy(part, parts.at[c % slots], sems.at[c % slots])

    lists = started(
        (rows_hbm, rows, sems.at[slots]),
        (sources_hbm, sources, sems.at[slots + 1]),
        (owner_hbm, owner_map, sems.at[slots + 2]),
    )
    for c in range(min(slots, chunks)):
        fetch(c).start()
    high[...] = jnp.zeros_like(high)
    low[...] = jnp.zeros_like(low)
    for copy in lists:
        copy.wait()

    def entry(c, k, carry):
        source = sources[0, 0, c * chunk + k]

        @pl.when(source >= 0)
        def _():
            owner = owner_map[source] // per_patch
            row = pl.multiple_of(rows[0, 0, c * chunk + k] * size, size)
            column = pl.multiple_of(owner * size, size)
            block = parts[c % slots, k]
            rounded = block.astype(high.dtype)
            rest = (block - rounded.astype(jnp.float32)).astype(low.dtype)
            high[pl.ds(row, size), pl.ds(column, size)] = rounded
            low[pl.ds(row, size), pl.ds(column, size)] = rest

        return carry

    for c in range(chunks):
        fetch(c).wait()
        lax.fori_loop(0, chunk, lambda k, carry, c=c: entry(c, k, carry), 0)
        if c + slots < chunks:
            fetch(c + slots).start()
    started((low, low_hbm, sems.at[0]))[0].wait()


def solved(excess, self_inverse):
    blocks, size, _ = self_inverse.shape
    parts = [
        jnp.dot(
            self_inverse[k],
            excess[k * size : (k + 1) * size],
            precision=lax.Precision.HIGHEST,
            preferred_element_type=jnp.float32,
        )
        for k in range(blocks)
    ]
    return jnp.concatenate(parts, axis=0).astype(jnp.bfloat16)


def products(high, low_hbm, arrived, low, sem, parts=1):
    patches, size, columns = arrived.shape
    (copy,) = started((low_hbm, low, sem))
    rows = high.shape[0] // parts
    for part in range(parts):
        here = slice(part * rows, (part + 1) * rows)
        flat = arrived[...].reshape(patches * size, columns)
        fresh = jnp.dot(high[here], flat, preferred_element_type=jnp.float32)
        if part == 0:
            copy.wait()
        yield here, fresh + jnp.dot(low[here], flat, preferred_element_type=jnp.float32)


def first_kernel(incident_hbm, field_hbm, inverse_hbm, after, current, incident, field, inverse, sems):
    del after

    @pl.when(lax.axis_index("lag") == 0)
    def _():
        copies = started(
            (incident_hbm.at[0], incident, sems.at[0]),
            (inverse_hbm, inverse, sems.at[1]),
            (field_hbm, field, sems.at[2]),
        )
        for copy in copies:
            copy.wait()
        current[...] = solved(incident[...].astype(jnp.float32) - field[...], inverse)


def solve_kernel(
    step, high, low_hbm, arrived, field, incident_hbm, inverse_hbm, current, low, incident, inverse, sems
):
    @pl.when(lax.axis_index("lag") == 0)
    def _():
        copies = started(
            (incident_hbm.at[step], incident, sems.at[0]),
            (inverse_hbm, inverse, sems.at[1]),
        )
        ((_, fresh),) = products(high, low_hbm, arrived, low, sems.at[2])
        for copy in copies:
            copy.wait()
        excess = incident[...].astype(jnp.float32) - (field[...] + fresh)
        current[...] = solved(excess, inverse)


def partial_kernel(high, low_hbm, arrived, field, after, partial, low, sem):
    del after

    @pl.when(lax.axis_index("lag") > 0)
    def _():
        ((_, fresh),) = products(high, low_hbm, arrived, low, sem)
        partial[...] = field[...] + fresh


def ahead_kernel(high, low_hbm, arrived, field, ahead_hbm, low, ahead, sems):
    copies = []
    for here, fresh in products(high, low_hbm, arrived, low, sems.at[0], 2):
        ahead[here] = field[here] + fresh
        copies += started((ahead.at[here], ahead_hbm.at[here], sems.at[len(copies) + 1]))
    for copy in copies:
        copy.wait()


def pack_kernel(step, keeps, early, asked, current, *refs):
    outgoing, currents, sems = refs[-3:]
    patches, size, _ = outgoing.shape
    section = lax.axis_index("lag")

    @pl.when(section < keeps if early else section >= keeps)
    def _():
        copies = []
        for q in range(patches):
            block = jnp.max(jnp.maximum(asked[q], 0))
            start = pl.multiple_of(block * size, size)
            copies.append((current.at[pl.ds(start, size)], outgoing.at[q], sems.at[q]))
        copies.append((current, currents.at[step], sems.at[patches]))
        for copy in started(*copies):
            copy.wait()


def shifted(x):
    sections = lax.axis_size("lag")
    return lax.ppermute(x, "lag", [(i, i - 1) for i in range(1, sections)])


def spread(x):
    sections = lax.axis_size("lag")
    section = lax.axis_index("lag")
    received, keeps = x, 1
    while keeps < sections:
        if keeps > 1:
            x = jnp.where(section < keeps // 2, x, received)
        pairs = [(i, i + keeps) for i in range(keeps) if i + keeps < sections]
        received = lax.ppermute(x, "lag", pairs)
        keeps *= 2
    return x, received, max(keeps // 2, 1)


def body(incident, pending, self_inverse, retarded, block_rows, block_sources, owner_map):
    steps, unknowns, columns = incident.shape
    per_patch, size, _ = self_inverse.shape
    listed = retarded.shape[2]
    patches = lax.axis_size("patch")
    bf16, f32 = jnp.bfloat16, jnp.float32
    all_flops = 4 * unknowns * patches * size * columns
    solve_flops = 12 * unknowns * size * columns
    panel_bytes = 4 * unknowns * patches * size
    column = (unknowns, columns)

    column_bytes = 4 * unknowns * columns
    arrived_bytes = 2 * patches * size * columns

    def exchange(x):
        return lax.all_to_all(x, "patch", split_axis=0, concat_axis=0, tiled=True)

    def pack(step, keeps, early, current, filled, after):
        held = [x for x in filled if x is not None]
        aliases = {}
        for out, x in enumerate(filled):
            if x is not None:
                aliases[2 + len(after) + len(aliases)] = out
        return call(
            lambda *refs: pack_kernel(step, keeps, early, *refs),
            [(HBM, (patches, size, columns), bf16), (HBM, incident.shape, bf16)],
            [(VMEM, asked), (VMEM, current)] + [(VMEM, x) for x in after] + [(HBM, x) for x in held],
            [DMA((patches + 1,))],
            aliases=aliases,
        )

    wanted = call(
        lambda *refs: request_kernel(per_patch, *refs),
        [(HBM, (patches, 1, 128), jnp.int32)],
        [(HBM, block_sources), (HBM, owner_map)],
        [
            pltpu.VMEM((patches, 1, 128), jnp.int32),
            pltpu.SMEM(block_sources.shape, jnp.int32),
            pltpu.SMEM(owner_map.shape, jnp.int32),
            DMA((2,)),
        ],
    )
    asked = exchange(wanted)
    solve_scratch = [pltpu.VMEM(column, bf16), pltpu.VMEM(self_inverse.shape, f32), DMA((3,))]
    current = call(
        first_kernel,
        [(VMEM, column, bf16)],
        [(HBM, incident), (HBM, pending[0]), (HBM, self_inverse), (HBM, wanted)],
        [solve_scratch[0], pltpu.VMEM(column, f32), *solve_scratch[1:]],
        solve_flops,
    )
    chunk = max(n for n in range(1, 9) if listed % n == 0)
    panel = (unknowns, patches * size)
    high, low = call(
        lambda *refs: panel_kernel(per_patch, *refs),
        [(VMEM, panel, bf16), (HBM, panel, bf16)],
        [(HBM, block_rows), (HBM, block_sources), (HBM, owner_map), (HBM, retarded)],
        [
            pltpu.SMEM(block_rows.shape, jnp.int32),
            pltpu.SMEM(block_sources.shape, jnp.int32),
            pltpu.SMEM(owner_map.shape, jnp.int32),
            pltpu.VMEM((3, chunk, size, size), f32),
            pltpu.VMEM(panel, bf16),
            DMA((6,)),
        ],
        nbytes=listed * size * size * 4 + panel_bytes,
        vmem=panel_bytes // 2,
    )

    field = pending[0]
    currents = None
    after = []
    for step in range(steps):
        own, received, keeps = spread(current)
        outgoing, currents = pack(step, keeps, True, own, (None, currents), [])
        if lax.axis_size("lag") > 1:
            outgoing, currents = pack(step, keeps, False, received, (outgoing, currents), after)
        arrived = exchange(outgoing)
        field = shifted(field)
        if step + 1 < steps:
            current = call(
                lambda *refs, n=step + 1: solve_kernel(n, *refs),
                [(VMEM, column, bf16)],
                [
                    (VMEM, high),
                    (HBM, low),
                    (VMEM, arrived),
                    (VMEM, field),
                    (HBM, incident),
                    (HBM, self_inverse),
                ],
                [pltpu.VMEM(panel, bf16), *solve_scratch],
                all_flops + solve_flops,
                panel_bytes + arrived_bytes,
                panel_bytes + arrived_bytes,
            )
            field = call(
                partial_kernel,
                [(VMEM, column, f32)],
                [(VMEM, high), (HBM, low), (VMEM, arrived), (VMEM, field), (VMEM, current)],
                [pltpu.VMEM(panel, bf16), DMA],
                all_flops,
                panel_bytes + arrived_bytes,
                panel_bytes + arrived_bytes,
            )
            after = [field]
        else:
            field = call(
                ahead_kernel,
                [(HBM, column, f32)],
                [(VMEM, high), (HBM, low), (VMEM, arrived), (VMEM, field)],
                [pltpu.VMEM(panel, bf16), pltpu.VMEM(column, f32), DMA((3,))],
                all_flops,
                panel_bytes + arrived_bytes,
                panel_bytes + arrived_bytes,
            )
    return currents, field[None]


def solution(mesh):
    in_specs = (
        P(None, "patch", None),
        P("lag", "patch", None),
        P("patch", None, None),
        P("lag", "patch", None, None, None),
        P("lag", "patch", None),
        P("lag", "patch", None),
        P(),
    )
    out_specs = (P(None, "patch", None), P("lag", "patch", None))
    return jax.shard_map(body, mesh=mesh, in_specs=in_specs, out_specs=out_specs, check_vma=False)
```

```python
import jax
import jax.numpy as jnp
from jax import lax
from jax.experimental import pallas as pl
from jax.experimental.pallas import tpu as pltpu
from jax.sharding import PartitionSpec as P

VMEM, HBM, ANY = pltpu.VMEM, pltpu.HBM, pl.ANY
DMA = pltpu.SemaphoreType.DMA
MIB = 1 << 20


def call(kernel, outs, ins, scratch=(), flops=0, nbytes=0, vmem=0, aliases=None):
    out_shape = tuple(space(dims, dtype) for space, dims, dtype in outs)
    out_specs = tuple(pl.BlockSpec(memory_space=space) for space, _, _ in outs)
    run = pl.pallas_call(
        kernel,
        out_shape=out_shape,
        in_specs=[pl.BlockSpec(memory_space=space) for space, _ in ins],
        out_specs=out_specs,
        scratch_shapes=scratch,
        input_output_aliases=aliases or {},
        cost_estimate=pl.CostEstimate(flops=flops, bytes_accessed=nbytes, transcendentals=0),
        compiler_params=pltpu.CompilerParams(vmem_limit_bytes=vmem + 6 * MIB),
    )
    results = run(*(pltpu.with_memory_space_constraint(x, space) for space, x in ins))
    return results if len(outs) > 1 else results[0]


def started(*copies):
    copies = [pltpu.make_async_copy(*copy) for copy in copies]
    for copy in copies:
        copy.start()
    return copies


def request_kernel(per_patch, sources_hbm, owner_hbm, wanted_hbm, wanted, sources, owner_map, sems):
    copies = started(
        (sources_hbm, sources, sems.at[0]),
        (owner_hbm, owner_map, sems.at[1]),
    )
    patch = lax.broadcasted_iota(jnp.int32, wanted.shape, 0)
    for copy in copies:
        copy.wait()

    def entry(j, table):
        source = sources[0, 0, j]
        storage = owner_map[jnp.maximum(source, 0)]
        here = (patch == storage // per_patch) & (source >= 0)
        return jnp.where(here, storage % per_patch, table)

    wanted[...] = lax.fori_loop(
        0, sources.shape[2], entry, jnp.full(wanted.shape, -1, jnp.int32), unroll=8
    )
    started((wanted, wanted_hbm, sems.at[0]))[0].wait()


def panel_kernel(
    per_patch, rows_hbm, sources_hbm, owner_hbm, retarded, high, low_hbm, rows, sources, owner_map, parts, low, sems
):
    size = retarded.shape[-1]
    slots, chunk = parts.shape[:2]
    chunks = retarded.shape[2] // chunk

    def fetch(c):
        part = retarded.at[0, 0, pl.ds(c * chunk, chunk)]
        return pltpu.make_async_copy(part, parts.at[c % slots], sems.at[c % slots])

    lists = started(
        (rows_hbm, rows, sems.at[slots]),
        (sources_hbm, sources, sems.at[slots + 1]),
        (owner_hbm, owner_map, sems.at[slots + 2]),
    )
    for c in range(min(slots, chunks)):
        fetch(c).start()
    high[...] = jnp.zeros_like(high)
    low[...] = jnp.zeros_like(low)
    for copy in lists:
        copy.wait()

    def entry(c, k, carry):
        source = sources[0, 0, c * chunk + k]

        @pl.when(source >= 0)
        def _():
            owner = owner_map[source] // per_patch
            row = pl.multiple_of(rows[0, 0, c * chunk + k] * size, size)
            column = pl.multiple_of(owner * size, size)
            block = parts[c % slots, k]
            rounded = block.astype(high.dtype)
            rest = (block - rounded.astype(jnp.float32)).astype(low.dtype)
            high[pl.ds(row, size), pl.ds(column, size)] = rounded
            low[pl.ds(row, size), pl.ds(column, size)] = rest

        return carry

    for c in range(chunks):
        fetch(c).wait()
        lax.fori_loop(0, chunk, lambda k, carry, c=c: entry(c, k, carry), 0)
        if c + slots < chunks:
            fetch(c + slots).start()
    started((low, low_hbm, sems.at[0]))[0].wait()


def solved(excess, self_inverse):
    blocks, size, _ = self_inverse.shape
    parts = [
        jnp.dot(
            self_inverse[k],
            excess[k * size : (k + 1) * size],
            precision=lax.Precision.HIGHEST,
            preferred_element_type=jnp.float32,
        )
        for k in range(blocks)
    ]
    return jnp.concatenate(parts, axis=0).astype(jnp.bfloat16)


def products(high, low_hbm, arrived, low, sem, parts=1):
    patches, size, columns = arrived.shape
    (copy,) = started((low_hbm, low, sem))
    rows = high.shape[0] // parts
    for part in range(parts):
        here = slice(part * rows, (part + 1) * rows)
        flat = arrived[...].reshape(patches * size, columns)
        fresh = jnp.dot(high[here], flat, preferred_element_type=jnp.float32)
        if part == 0:
            copy.wait()
        yield here, fresh + jnp.dot(low[here], flat, preferred_element_type=jnp.float32)


def first_kernel(incident_hbm, field_hbm, inverse_hbm, after, current, incident, field, inverse, sems):
    del after

    @pl.when(lax.axis_index("lag") == 0)
    def _():
        copies = started(
            (incident_hbm.at[0], incident, sems.at[0]),
            (inverse_hbm, inverse, sems.at[1]),
            (field_hbm, field, sems.at[2]),
        )
        for copy in copies:
            copy.wait()
        current[...] = solved(incident[...].astype(jnp.float32) - field[...], inverse)


def solve_kernel(
    step, high, low_hbm, arrived, field, incident_hbm, inverse_hbm, current, low, incident, inverse, sems
):
    @pl.when(lax.axis_index("lag") == 0)
    def _():
        copies = started(
            (incident_hbm.at[step], incident, sems.at[0]),
            (inverse_hbm, inverse, sems.at[1]),
        )
        ((_, fresh),) = products(high, low_hbm, arrived, low, sems.at[2])
        for copy in copies:
            copy.wait()
        excess = incident[...].astype(jnp.float32) - (field[...] + fresh)
        current[...] = solved(excess, inverse)


def partial_kernel(high, low_hbm, arrived, field, partial, low, sem):
    @pl.when(lax.axis_index("lag") > 0)
    def _():
        ((_, fresh),) = products(high, low_hbm, arrived, low, sem)
        partial[...] = field[...] + fresh


def ahead_kernel(high, low_hbm, arrived_first, arrived_rest, field, ahead_hbm, low, ahead, sems):
    def finish(arrived):
        copies = []
        for here, fresh in products(high, low_hbm, arrived, low, sems.at[0], 2):
            ahead[here] = field[here] + fresh
            copies += started((ahead.at[here], ahead_hbm.at[here], sems.at[len(copies) + 1]))
        for copy in copies:
            copy.wait()

    first = lax.axis_index("lag") == 0
    pl.when(first)(lambda: finish(arrived_first))
    pl.when(jnp.logical_not(first))(lambda: finish(arrived_rest))


def pack(step, asked, current, outgoing, currents, sems):
    patches, size, _ = outgoing.shape
    copies = []
    for q in range(patches):
        block = jnp.max(jnp.maximum(asked[q], 0))
        start = pl.multiple_of(block * size, size)
        copies.append((current.at[pl.ds(start, size)], outgoing.at[q], sems.at[q]))
    copies.append((current, currents.at[step], sems.at[patches]))
    for copy in started(*copies):
        copy.wait()


def first_pack_kernel(step, asked, current, *refs):
    outgoing, currents, _, sems = refs[-4:]
    pl.when(lax.axis_index("lag") == 0)(lambda: pack(step, asked, current, outgoing, currents, sems))


def rest_pack_kernel(step, keeps, asked, own, received, *refs):
    outgoing, currents, sems = refs[-3:]
    section = lax.axis_index("lag")
    if keeps > 1:
        mine = (section > 0) & (section < keeps)
        pl.when(mine)(lambda: pack(step, asked, own, outgoing, currents, sems))
    pl.when(section >= keeps)(lambda: pack(step, asked, received, outgoing, currents, sems))


def shifted(x):
    sections = lax.axis_size("lag")
    return lax.ppermute(x, "lag", [(i, i - 1) for i in range(1, sections)])


def spread(x):
    sections = lax.axis_size("lag")
    section = lax.axis_index("lag")
    received, keeps = x, 1
    while keeps < sections:
        if keeps > 1:
            x = jnp.where(section < keeps // 2, x, received)
        pairs = [(i, i + keeps) for i in range(keeps) if i + keeps < sections]
        received = lax.ppermute(x, "lag", pairs)
        keeps *= 2
    return x, received, max(keeps // 2, 1)


def body(incident, pending, self_inverse, retarded, block_rows, block_sources, owner_map):
    steps, unknowns, columns = incident.shape
    per_patch, size, _ = self_inverse.shape
    listed = retarded.shape[2]
    patches = lax.axis_size("patch")
    bf16, f32 = jnp.bfloat16, jnp.float32
    all_flops = 4 * unknowns * patches * size * columns
    solve_flops = 12 * unknowns * size * columns
    panel_bytes = 4 * unknowns * patches * size
    column = (unknowns, columns)

    column_bytes = 4 * unknowns * columns
    arrived_bytes = 2 * patches * size * columns

    def exchange(x):
        return lax.all_to_all(x, "patch", split_axis=0, concat_axis=0, tiled=True)

    blocks = (patches, size, columns)

    def first_pack(step, current, currents):
        held = [] if currents is None else [(HBM, currents)]
        return call(
            lambda *refs: first_pack_kernel(step, *refs),
            [(HBM, blocks, bf16), (HBM, incident.shape, bf16), (VMEM, column, bf16)],
            [(VMEM, asked), (VMEM, current)] + held,
            [DMA((patches + 1,))],
            aliases={1: 2, 2: 1} if held else {1: 2},
        )

    def rest_pack(step, keeps, own, received, currents, after):
        ins = [(VMEM, asked), (VMEM, own), (VMEM, received)] + [(VMEM, x) for x in after] + [(HBM, currents)]
        return call(
            lambda *refs: rest_pack_kernel(step, keeps, *refs),
            [(HBM, blocks, bf16), (HBM, incident.shape, bf16)],
            ins,
            [DMA((patches + 1,))],
            aliases={len(ins) - 1: 1},
        )

    wanted = call(
        lambda *refs: request_kernel(per_patch, *refs),
        [(HBM, (patches, 1, 128), jnp.int32)],
        [(HBM, block_sources), (HBM, owner_map)],
        [
            pltpu.VMEM((patches, 1, 128), jnp.int32),
            pltpu.SMEM(block_sources.shape, jnp.int32),
            pltpu.SMEM(owner_map.shape, jnp.int32),
            DMA((2,)),
        ],
    )
    asked = exchange(wanted)
    solve_scratch = [pltpu.VMEM(column, bf16), pltpu.VMEM(self_inverse.shape, f32), DMA((3,))]
    current = call(
        first_kernel,
        [(VMEM, column, bf16)],
        [(HBM, incident), (HBM, pending[0]), (HBM, self_inverse), (HBM, wanted)],
        [solve_scratch[0], pltpu.VMEM(column, f32), *solve_scratch[1:]],
        solve_flops,
    )
    chunk = max(n for n in range(1, 9) if listed % n == 0)
    panel = (unknowns, patches * size)
    high, low = call(
        lambda *refs: panel_kernel(per_patch, *refs),
        [(VMEM, panel, bf16), (HBM, panel, bf16)],
        [(HBM, block_rows), (HBM, block_sources), (HBM, owner_map), (HBM, retarded)],
        [
            pltpu.SMEM(block_rows.shape, jnp.int32),
            pltpu.SMEM(block_sources.shape, jnp.int32),
            pltpu.SMEM(owner_map.shape, jnp.int32),
            pltpu.VMEM((3, chunk, size, size), f32),
            pltpu.VMEM(panel, bf16),
            DMA((6,)),
        ],
        nbytes=listed * size * size * 4 + panel_bytes,
        vmem=panel_bytes // 2,
    )

    field = pending[0]
    currents = None
    after = []
    for step in range(steps):
        outgoing, currents, current = first_pack(step, current, currents)
        arrived_first = arrived_rest = exchange(outgoing)
        if lax.axis_size("lag") > 1:
            own, received, keeps = spread(current)
            outgoing, currents = rest_pack(step, keeps, own, received, currents, after)
            arrived_rest = exchange(outgoing)
        field = shifted(field)
        if step + 1 < steps:
            current = call(
                lambda *refs, n=step + 1: solve_kernel(n, *refs),
                [(VMEM, column, bf16)],
                [
                    (VMEM, high),
                    (HBM, low),
                    (VMEM, arrived_first),
                    (VMEM, field),
                    (HBM, incident),
                    (HBM, self_inverse),
                ],
                [pltpu.VMEM(panel, bf16), *solve_scratch],
                all_flops + solve_flops,
                panel_bytes + arrived_bytes,
                panel_bytes + arrived_bytes,
            )
            field = call(
                partial_kernel,
                [(VMEM, column, f32)],
                [(VMEM, high), (HBM, low), (VMEM, arrived_rest), (VMEM, field)],
                [pltpu.VMEM(panel, bf16), DMA],
                all_flops,
                panel_bytes + arrived_bytes,
                panel_bytes + arrived_bytes,
            )
            after = [field]
        else:
            field = call(
                ahead_kernel,
                [(HBM, column, f32)],
                [(VMEM, high), (HBM, low), (VMEM, arrived_first), (VMEM, arrived_rest), (VMEM, field)],
                [pltpu.VMEM(panel, bf16), pltpu.VMEM(column, f32), DMA((3,))],
                all_flops,
                panel_bytes + arrived_bytes,
                panel_bytes + arrived_bytes,
            )
    return currents, field[None]


def solution(mesh):
    in_specs = (
        P(None, "patch", None),
        P("lag", "patch", None),
        P("patch", None, None),
        P("lag", "patch", None, None, None),
        P("lag", "patch", None),
        P("lag", "patch", None),
        P(),
    )
    out_specs = (P(None, "patch", None), P("lag", "patch", None))
    return jax.shard_map(body, mesh=mesh, in_specs=in_specs, out_specs=out_specs, check_vma=False)
```

```python
import jax
import jax.numpy as jnp
from jax import lax
from jax.experimental import pallas as pl
from jax.experimental.pallas import tpu as pltpu
from jax.sharding import PartitionSpec as P

VMEM, HBM, ANY = pltpu.VMEM, pltpu.HBM, pl.ANY
DMA = pltpu.SemaphoreType.DMA
MIB = 1 << 20


def call(kernel, outs, ins, scratch=(), flops=0, nbytes=0, vmem=0, aliases=None):
    out_shape = tuple(space(dims, dtype) for space, dims, dtype in outs)
    out_specs = tuple(pl.BlockSpec(memory_space=space) for space, _, _ in outs)
    run = pl.pallas_call(
        kernel,
        out_shape=out_shape,
        in_specs=[pl.BlockSpec(memory_space=space) for space, _ in ins],
        out_specs=out_specs,
        scratch_shapes=scratch,
        input_output_aliases=aliases or {},
        cost_estimate=pl.CostEstimate(flops=flops, bytes_accessed=nbytes, transcendentals=0),
        compiler_params=pltpu.CompilerParams(vmem_limit_bytes=vmem + 6 * MIB),
    )
    results = run(*(pltpu.with_memory_space_constraint(x, space) for space, x in ins))
    return results if len(outs) > 1 else results[0]


def started(*copies):
    copies = [pltpu.make_async_copy(*copy) for copy in copies]
    for copy in copies:
        copy.start()
    return copies


def request_kernel(
    per_patch, sources_hbm, owner_hbm, field_hbm, wanted_hbm, field, wanted, sources, owner_map, sems
):
    copies = started(
        (sources_hbm, sources, sems.at[0]),
        (owner_hbm, owner_map, sems.at[1]),
        (field_hbm, field, sems.at[2]),
    )
    patch = lax.broadcasted_iota(jnp.int32, wanted.shape, 0)
    for copy in copies[:2]:
        copy.wait()

    def entry(j, table):
        source = sources[0, 0, j]
        storage = owner_map[jnp.maximum(source, 0)]
        here = (patch == storage // per_patch) & (source >= 0)
        return jnp.where(here, storage % per_patch, table)

    wanted[...] = lax.fori_loop(
        0, sources.shape[2], entry, jnp.full(wanted.shape, -1, jnp.int32), unroll=8
    )
    started((wanted, wanted_hbm, sems.at[0]))[0].wait()
    copies[2].wait()


def panel_kernel(
    per_patch, rows_hbm, sources_hbm, owner_hbm, retarded, high, low_hbm, rows, sources, owner_map, parts, low, sems
):
    size = retarded.shape[-1]
    slots, chunk = parts.shape[:2]
    chunks = retarded.shape[2] // chunk

    def fetch(c):
        part = retarded.at[0, 0, pl.ds(c * chunk, chunk)]
        return pltpu.make_async_copy(part, parts.at[c % slots], sems.at[c % slots])

    lists = started(
        (rows_hbm, rows, sems.at[slots]),
        (sources_hbm, sources, sems.at[slots + 1]),
        (owner_hbm, owner_map, sems.at[slots + 2]),
    )
    for c in range(min(slots, chunks)):
        fetch(c).start()
    high[...] = jnp.zeros_like(high)
    low[...] = jnp.zeros_like(low)
    for copy in lists:
        copy.wait()

    def entry(c, k, carry):
        source = sources[0, 0, c * chunk + k]

        @pl.when(source >= 0)
        def _():
            owner = owner_map[source] // per_patch
            row = pl.multiple_of(rows[0, 0, c * chunk + k] * size, size)
            column = pl.multiple_of(owner * size, size)
            block = parts[c % slots, k]
            rounded = block.astype(high.dtype)
            rest = (block - rounded.astype(jnp.float32)).astype(low.dtype)
            high[pl.ds(row, size), pl.ds(column, size)] = rounded
            low[pl.ds(row, size), pl.ds(column, size)] = rest

        return carry

    for c in range(chunks):
        fetch(c).wait()
        lax.fori_loop(0, chunk, lambda k, carry, c=c: entry(c, k, carry), 0)
        if c + slots < chunks:
            fetch(c + slots).start()
    started((low, low_hbm, sems.at[0]))[0].wait()


def solved(excess, self_inverse):
    blocks, size, _ = self_inverse.shape
    parts = [
        jnp.dot(
            self_inverse[k],
            excess[k * size : (k + 1) * size],
            precision=lax.Precision.HIGHEST,
            preferred_element_type=jnp.float32,
        )
        for k in range(blocks)
    ]
    return jnp.concatenate(parts, axis=0).astype(jnp.bfloat16)


def product(high, low_hbm, arrived, low, sem):
    patches, size, columns = arrived.shape
    (copy,) = started((low_hbm, low, sem))
    flat = arrived[...].reshape(patches * size, columns)
    fresh = jnp.dot(high[...], flat, preferred_element_type=jnp.float32)
    copy.wait()
    return fresh + jnp.dot(low[...], flat, preferred_element_type=jnp.float32)


def first_kernel(keeps, incident_hbm, own, received, inverse_hbm, current, incident, inverse, sems):
    copies = started(
        (incident_hbm.at[0], incident, sems.at[0]),
        (inverse_hbm, inverse, sems.at[1]),
    )
    field = jnp.where(lax.axis_index("lag") < keeps, own[...], received[...])
    for copy in copies:
        copy.wait()
    current[...] = solved(incident[...].astype(jnp.float32) - field, inverse)


def solve_kernel(
    step, high, low_hbm, arrived, field, incident_hbm, inverse_hbm, current, low, incident, inverse, sems
):
    @pl.when(lax.axis_index("lag") == 0)
    def _():
        copies = started(
            (incident_hbm.at[step], incident, sems.at[0]),
            (inverse_hbm, inverse, sems.at[1]),
        )
        fresh = product(high, low_hbm, arrived, low, sems.at[2])
        for copy in copies:
            copy.wait()
        excess = incident[...].astype(jnp.float32) - (field[...] + fresh)
        current[...] = solved(excess, inverse)


def partial_kernel(high, low_hbm, arrived, field, after, partial, low, sem):
    del after

    @pl.when(lax.axis_index("lag") > 0)
    def _():
        fresh = product(high, low_hbm, arrived, low, sem)
        partial[...] = field[...] + fresh


def ahead_kernel(high, arrived, field, ahead_hbm, ahead, sems):
    patches, size, columns = arrived.shape
    rows = ahead.shape[0] // sems.shape[0]
    copies = []
    for part in range(sems.shape[0]):
        here = pl.ds(part * rows, rows)
        flat = arrived[...].reshape(patches * size, columns)
        fresh = jnp.dot(high[here, :], flat, preferred_element_type=jnp.float32)
        ahead[here, :] = field[here, :] + fresh
        copies += started((ahead.at[here], ahead_hbm.at[here], sems.at[part]))
    for copy in copies:
        copy.wait()


def pack_kernel(step, keeps, early, asked, current, *refs):
    outgoing, currents, sems = refs[-3:]
    patches, size, _ = outgoing.shape
    section = lax.axis_index("lag")

    @pl.when(section < keeps if early else section >= keeps)
    def _():
        copies = []
        for q in range(patches):
            block = jnp.max(jnp.maximum(asked[q], 0))
            start = pl.multiple_of(block * size, size)
            copies.append((current.at[pl.ds(start, size)], outgoing.at[q], sems.at[q]))
        copies.append((current, currents.at[step], sems.at[patches]))
        for copy in started(*copies):
            copy.wait()


def shifted(x):
    sections = lax.axis_size("lag")
    return lax.ppermute(x, "lag", [(i, i - 1) for i in range(1, sections)])


def spread(x):
    sections = lax.axis_size("lag")
    section = lax.axis_index("lag")
    received, keeps = x, 1
    while keeps < sections:
        if keeps > 1:
            x = jnp.where(section < keeps // 2, x, received)
        pairs = [(i, i + keeps) for i in range(keeps) if i + keeps < sections]
        received = lax.ppermute(x, "lag", pairs)
        keeps *= 2
    return x, received, max(keeps // 2, 1)


def body(incident, pending, self_inverse, retarded, block_rows, block_sources, owner_map):
    steps, unknowns, columns = incident.shape
    per_patch, size, _ = self_inverse.shape
    listed = retarded.shape[2]
    patches = lax.axis_size("patch")
    bf16, f32 = jnp.bfloat16, jnp.float32
    all_flops = 4 * unknowns * patches * size * columns
    solve_flops = 12 * unknowns * size * columns
    panel_bytes = 4 * unknowns * patches * size
    column = (unknowns, columns)
    arrived_bytes = 2 * patches * size * columns

    def exchange(x):
        return lax.all_to_all(x, "patch", split_axis=0, concat_axis=0, tiled=True)

    def pack(step, keeps, early, current, filled, after=()):
        held = [x for x in filled if x is not None]
        aliases = {}
        for out, x in enumerate(filled):
            if x is not None:
                aliases[2 + len(after) + len(aliases)] = out
        return call(
            lambda *refs: pack_kernel(step, keeps, early, *refs),
            [(HBM, (patches, size, columns), bf16), (HBM, incident.shape, bf16)],
            [(VMEM, asked), (VMEM, current)] + [(VMEM, x) for x in after] + [(HBM, x) for x in held],
            [DMA((patches + 1,))],
            aliases=aliases,
        )

    wanted, first_field = call(
        lambda *refs: request_kernel(per_patch, *refs),
        [(HBM, (patches, 1, 128), jnp.int32), (VMEM, column, f32)],
        [(HBM, block_sources), (HBM, owner_map), (HBM, pending[0])],
        [
            pltpu.VMEM((patches, 1, 128), jnp.int32),
            pltpu.SMEM(block_sources.shape, jnp.int32),
            pltpu.SMEM(owner_map.shape, jnp.int32),
            DMA((3,)),
        ],
    )
    asked = exchange(wanted)
    own, received, keeps = spread(first_field)
    solve_scratch = [pltpu.VMEM(column, bf16), pltpu.VMEM(self_inverse.shape, f32), DMA((3,))]
    current = call(
        lambda *refs: first_kernel(keeps, *refs),
        [(VMEM, column, bf16)],
        [(HBM, incident), (VMEM, own), (VMEM, received), (HBM, self_inverse)],
        solve_scratch,
        solve_flops,
    )
    chunk = max(n for n in range(1, 9) if listed % n == 0)
    panel = (unknowns, patches * size)
    high, low = call(
        lambda *refs: panel_kernel(per_patch, *refs),
        [(VMEM, panel, bf16), (HBM, panel, bf16)],
        [(HBM, block_rows), (HBM, block_sources), (HBM, owner_map), (HBM, retarded)],
        [
            pltpu.SMEM(block_rows.shape, jnp.int32),
            pltpu.SMEM(block_sources.shape, jnp.int32),
            pltpu.SMEM(owner_map.shape, jnp.int32),
            pltpu.VMEM((3, chunk, size, size), f32),
            pltpu.VMEM(panel, bf16),
            DMA((6,)),
        ],
        nbytes=listed * size * size * 4 + panel_bytes,
        vmem=panel_bytes // 2,
    )

    field = pending[0]
    outgoing, currents = pack(0, lax.axis_size("lag"), True, current, (None, None))
    for step in range(steps):
        if step > 0:
            own, received, keeps = spread(current)
            outgoing, currents = pack(step, keeps, True, own, (None, currents))
            if lax.axis_size("lag") > 1:
                outgoing, currents = pack(step, keeps, False, received, (outgoing, currents), [field])
        arrived = exchange(outgoing)
        field = shifted(field)
        if step + 1 < steps:
            current = call(
                lambda *refs, n=step + 1: solve_kernel(n, *refs),
                [(VMEM, column, bf16)],
                [
                    (VMEM, high),
                    (HBM, low),
                    (VMEM, arrived),
                    (VMEM, field),
                    (HBM, incident),
                    (HBM, self_inverse),
                ],
                [pltpu.VMEM(panel, bf16), *solve_scratch],
                all_flops + solve_flops,
                panel_bytes + arrived_bytes,
                panel_bytes + arrived_bytes,
            )
            field = call(
                partial_kernel,
                [(VMEM, column, f32)],
                [(VMEM, high), (HBM, low), (VMEM, arrived), (VMEM, field), (VMEM, current)],
                [pltpu.VMEM(panel, bf16), DMA],
                all_flops,
                panel_bytes + arrived_bytes,
                panel_bytes + arrived_bytes,
            )
        else:
            field = call(
                ahead_kernel,
                [(HBM, column, f32)],
                [(VMEM, high), (VMEM, arrived), (VMEM, field)],
                [pltpu.VMEM(column, f32), DMA((2,))],
                all_flops,
                panel_bytes + arrived_bytes,
                panel_bytes + arrived_bytes,
            )
    return currents, field[None]


def solution(mesh):
    in_specs = (
        P(None, "patch", None),
        P("lag", "patch", None),
        P("patch", None, None),
        P("lag", "patch", None, None, None),
        P("lag", "patch", None),
        P("lag", "patch", None),
        P(),
    )
    out_specs = (P(None, "patch", None), P("lag", "patch", None))
    return jax.shard_map(body, mesh=mesh, in_specs=in_specs, out_specs=out_specs, check_vma=False)
```

```python
import jax
import jax.numpy as jnp
from jax import lax
from jax.experimental import pallas as pl
from jax.experimental.pallas import tpu as pltpu
from jax.sharding import PartitionSpec as P

VMEM, SMEM, HBM = pltpu.VMEM, pltpu.SMEM, pltpu.HBM
DMA = pltpu.SemaphoreType.DMA
MIB = 1 << 20


def call(kernel, outs, ins, scratch=(), flops=0, nbytes=0, vmem=0, aliases=None):
    out_shape = tuple(space(dims, dtype) for space, dims, dtype in outs)
    out_specs = tuple(pl.BlockSpec(memory_space=space) for space, _, _ in outs)
    run = pl.pallas_call(
        kernel,
        out_shape=out_shape,
        in_specs=[pl.BlockSpec(memory_space=space) for space, _ in ins],
        out_specs=out_specs,
        scratch_shapes=scratch,
        input_output_aliases=aliases or {},
        cost_estimate=pl.CostEstimate(flops=flops, bytes_accessed=nbytes, transcendentals=0),
        compiler_params=pltpu.CompilerParams(vmem_limit_bytes=vmem + 6 * MIB),
    )
    results = run(*(pltpu.with_memory_space_constraint(x, space) for space, x in ins))
    return results if len(outs) > 1 else results[0]


def started(*copies):
    copies = [pltpu.make_async_copy(*copy) for copy in copies]
    for copy in copies:
        copy.start()
    return copies


def request_kernel(
    per_patch, sources_hbm, owner_hbm, field_hbm, wanted_hbm, field, wanted, sources, owner_map, sems
):
    copies = started(
        (sources_hbm, sources, sems.at[0]),
        (owner_hbm, owner_map, sems.at[1]),
        (field_hbm, field, sems.at[2]),
    )
    patch = lax.broadcasted_iota(jnp.int32, wanted.shape, 0)
    for copy in copies[:2]:
        copy.wait()

    def entry(j, table):
        source = sources[0, 0, j]
        storage = owner_map[jnp.maximum(source, 0)]
        here = (patch == storage // per_patch) & (source >= 0)
        return jnp.where(here, storage % per_patch, table)

    wanted[...] = lax.fori_loop(
        0, sources.shape[2], entry, jnp.full(wanted.shape, -1, jnp.int32), unroll=8
    )
    started((wanted, wanted_hbm, sems.at[0]))[0].wait()
    copies[2].wait()


def panel_kernel(
    per_patch,
    rows_hbm,
    sources_hbm,
    owner_hbm,
    retarded,
    inverse_hbm,
    high,
    low_hbm,
    inverse,
    rows,
    sources,
    owner_map,
    parts,
    low,
    sems,
):
    size = retarded.shape[-1]
    slots, chunk = parts.shape[:2]
    chunks = retarded.shape[2] // chunk

    def fetch(c):
        part = retarded.at[0, 0, pl.ds(c * chunk, chunk)]
        return pltpu.make_async_copy(part, parts.at[c % slots], sems.at[c % slots])

    lists = started(
        (rows_hbm, rows, sems.at[slots]),
        (sources_hbm, sources, sems.at[slots + 1]),
        (owner_hbm, owner_map, sems.at[slots + 2]),
        (inverse_hbm, inverse, sems.at[slots + 3]),
    )
    for c in range(min(slots, chunks)):
        fetch(c).start()
    high[...] = jnp.zeros_like(high)
    low[...] = jnp.zeros_like(low)
    for copy in lists:
        copy.wait()

    def entry(c, k, carry):
        source = sources[0, 0, c * chunk + k]

        @pl.when(source >= 0)
        def _():
            owner = owner_map[source] // per_patch
            row = pl.multiple_of(rows[0, 0, c * chunk + k] * size, size)
            column = pl.multiple_of(owner * size, size)
            block = parts[c % slots, k]
            rounded = block.astype(high.dtype)
            rest = (block - rounded.astype(jnp.float32)).astype(low.dtype)
            high[pl.ds(row, size), pl.ds(column, size)] = rounded
            piece = column // low.shape[2]
            inside = pl.multiple_of(column - piece * low.shape[2], size)
            low[piece, pl.ds(row, size), pl.ds(inside, size)] = rest

        return carry

    for c in range(chunks):
        fetch(c).wait()
        lax.fori_loop(0, chunk, lambda k, carry, c=c: entry(c, k, carry), 0)
        if c + slots < chunks:
            fetch(c + slots).start()
    started((low, low_hbm, sems.at[0]))[0].wait()


def solved(excess, self_inverse):
    blocks, size, _ = self_inverse.shape
    parts = [
        jnp.dot(
            self_inverse[k],
            excess[k * size : (k + 1) * size],
            precision=lax.Precision.HIGHEST,
            preferred_element_type=jnp.float32,
        )
        for k in range(blocks)
    ]
    return jnp.concatenate(parts, axis=0).astype(jnp.bfloat16)


def product(high, low_hbm, arrived, low, sems):
    patches, size, columns = arrived.shape
    pieces, _, depth = low.shape
    copies = started(*((low_hbm.at[k], low.at[k], sems.at[k]) for k in range(pieces)))
    flat = arrived[...].reshape(patches * size, columns)
    fresh = jnp.dot(high[...], flat, preferred_element_type=jnp.float32)
    for k, copy in enumerate(copies):
        copy.wait()
        here = flat[k * depth : (k + 1) * depth]
        fresh = fresh + jnp.dot(low[k], here, preferred_element_type=jnp.float32)
    return fresh


def first_kernel(keeps, incident_hbm, own, received, inverse_hbm, current, incident, inverse, sems):
    copies = started(
        (incident_hbm.at[0], incident, sems.at[0]),
        (inverse_hbm, inverse, sems.at[1]),
    )
    field = jnp.where(lax.axis_index("lag") < keeps, own[...], received[...])
    for copy in copies:
        copy.wait()
    current[...] = solved(incident[...].astype(jnp.float32) - field, inverse)


def stage_kernel(step, incident_hbm, field, staged, incident, sem):
    first = lax.axis_index("lag") == 0

    @pl.when(first)
    def _():
        started((incident_hbm.at[step], incident, sem))[0].wait()
        staged[...] = incident[...].astype(jnp.float32) - field[...]

    @pl.when(jnp.logical_not(first))
    def _():
        staged[...] = field[...]


def solve_kernel(high, low_hbm, arrived, staged, inverse, current, low, sems):
    @pl.when(lax.axis_index("lag") == 0)
    def _():
        current[...] = solved(staged[...] - product(high, low_hbm, arrived, low, sems), inverse)


def partial_kernel(high, low_hbm, arrived, staged, after, partial, low, sems):
    del after

    @pl.when(lax.axis_index("lag") > 0)
    def _():
        partial[...] = staged[...] + product(high, low_hbm, arrived, low, sems)


def asked_kernel(table, asked, copy_of, sem):
    started((table, copy_of, sem))[0].wait()
    for q in range(table.shape[0]):
        asked[q] = jnp.maximum(copy_of[q, 0, 0], 0)


def ahead_kernel(high, arrived, field, ahead_hbm, ahead, sems):
    patches, size, columns = arrived.shape
    rows = ahead.shape[0] // sems.shape[0]
    copies = []
    for part in range(sems.shape[0]):
        here = pl.ds(part * rows, rows)
        flat = arrived[...].reshape(patches * size, columns)
        fresh = jnp.dot(high[here, :], flat, preferred_element_type=jnp.float32)
        ahead[here, :] = field[here, :] + fresh
        copies += started((ahead.at[here], ahead_hbm.at[here], sems.at[part]))
    for copy in copies:
        copy.wait()


def pack_kernel(step, keeps, early, asked, current, *refs):
    outgoing, currents, sems = refs[-3:]
    patches, size, _ = outgoing.shape
    section = lax.axis_index("lag")

    @pl.when(section < keeps if early else section >= keeps)
    def _():
        copies = []
        for q in range(patches):
            start = pl.multiple_of(asked[q] * size, size)
            copies.append((current.at[pl.ds(start, size)], outgoing.at[q], sems.at[q]))
        copies.append((current, currents.at[step], sems.at[patches]))
        for copy in started(*copies):
            copy.wait()


def shifted(x):
    sections = lax.axis_size("lag")
    return lax.ppermute(x, "lag", [(i, i - 1) for i in range(1, sections)])


def spread(x):
    sections = lax.axis_size("lag")
    section = lax.axis_index("lag")
    received, keeps = x, 1
    while keeps < sections:
        if keeps > 1:
            x = jnp.where(section < keeps // 2, x, received)
        pairs = [(i, i + keeps) for i in range(keeps) if i + keeps < sections]
        received = lax.ppermute(x, "lag", pairs)
        keeps *= 2
    return x, received, max(keeps // 2, 1)


def body(incident, pending, self_inverse, retarded, block_rows, block_sources, owner_map):
    steps, unknowns, columns = incident.shape
    per_patch, size, _ = self_inverse.shape
    listed = retarded.shape[2]
    patches = lax.axis_size("patch")
    bf16, f32 = jnp.bfloat16, jnp.float32
    all_flops = 4 * unknowns * patches * size * columns
    solve_flops = 12 * unknowns * size * columns
    panel_bytes = 4 * unknowns * patches * size
    column = (unknowns, columns)
    arrived_bytes = 2 * patches * size * columns

    def exchange(x):
        return lax.all_to_all(x, "patch", split_axis=0, concat_axis=0, tiled=True)

    def pack(step, keeps, early, current, filled, after=()):
        held = [x for x in filled if x is not None]
        aliases = {}
        for out, x in enumerate(filled):
            if x is not None:
                aliases[2 + len(after) + len(aliases)] = out
        return call(
            lambda *refs: pack_kernel(step, keeps, early, *refs),
            [(HBM, (patches, size, columns), bf16), (HBM, incident.shape, bf16)],
            [(SMEM, asked), (VMEM, current)] + [(VMEM, x) for x in after] + [(HBM, x) for x in held],
            [DMA((patches + 1,))],
            aliases=aliases,
        )

    wanted, first_field = call(
        lambda *refs: request_kernel(per_patch, *refs),
        [(HBM, (patches, 1, 128), jnp.int32), (VMEM, column, f32)],
        [(HBM, block_sources), (HBM, owner_map), (HBM, pending[0])],
        [
            pltpu.VMEM((patches, 1, 128), jnp.int32),
            pltpu.SMEM(block_sources.shape, jnp.int32),
            pltpu.SMEM(owner_map.shape, jnp.int32),
            DMA((3,)),
        ],
    )
    asked = call(
        asked_kernel,
        [(SMEM, (patches,), jnp.int32)],
        [(VMEM, exchange(wanted))],
        [pltpu.SMEM(wanted.shape, jnp.int32), DMA],
    )
    own, received, keeps = spread(first_field)
    solve_scratch = [pltpu.VMEM(column, bf16), pltpu.VMEM(self_inverse.shape, f32), DMA((3,))]
    current = call(
        lambda *refs: first_kernel(keeps, *refs),
        [(VMEM, column, bf16)],
        [(HBM, incident), (VMEM, own), (VMEM, received), (HBM, self_inverse)],
        solve_scratch,
        solve_flops,
    )
    chunk = max(n for n in range(1, 9) if listed % n == 0)
    panel = (unknowns, patches * size)
    pieces = 4 if patches % 4 == 0 else 1
    low_panel = (pieces, unknowns, patches * size // pieces)
    high, low, inverse = call(
        lambda *refs: panel_kernel(per_patch, *refs),
        [(VMEM, panel, bf16), (HBM, low_panel, bf16), (VMEM, self_inverse.shape, f32)],
        [(HBM, block_rows), (HBM, block_sources), (HBM, owner_map), (HBM, retarded), (HBM, self_inverse)],
        [
            pltpu.SMEM(block_rows.shape, jnp.int32),
            pltpu.SMEM(block_sources.shape, jnp.int32),
            pltpu.SMEM(owner_map.shape, jnp.int32),
            pltpu.VMEM((3, chunk, size, size), f32),
            pltpu.VMEM(low_panel, bf16),
            DMA((7,)),
        ],
        nbytes=listed * size * size * 4 + panel_bytes,
        vmem=panel_bytes // 2,
    )

    field = pending[0]
    outgoing, currents = pack(0, lax.axis_size("lag"), True, current, (None, None))
    for step in range(steps):
        if step > 0:
            own, received, keeps = spread(current)
            outgoing, currents = pack(step, keeps, True, own, (None, currents))
            if lax.axis_size("lag") > 1:
                outgoing, currents = pack(step, keeps, False, received, (outgoing, currents), [field])
        arrived = exchange(outgoing)
        field = shifted(field)
        if step + 1 < steps:
            staged = call(
                lambda *refs, n=step + 1: stage_kernel(n, *refs),
                [(VMEM, column, f32)],
                [(HBM, incident), (VMEM, field)],
                [pltpu.VMEM(column, bf16), DMA],
            )
            shared = [(VMEM, high), (HBM, low), (VMEM, arrived), (VMEM, staged)]
            scratch = [pltpu.VMEM(low_panel, bf16), DMA((pieces,))]
            sizes = [all_flops, panel_bytes + arrived_bytes, panel_bytes + arrived_bytes]
            current = call(
                solve_kernel, [(VMEM, column, bf16)], [*shared, (VMEM, inverse)], scratch, *sizes
            )
            field = call(
                partial_kernel, [(VMEM, column, f32)], [*shared, (VMEM, current)], scratch, *sizes
            )
        else:
            field = call(
                ahead_kernel,
                [(HBM, column, f32)],
                [(VMEM, high), (VMEM, arrived), (VMEM, field)],
                [pltpu.VMEM(column, f32), DMA((2,))],
                all_flops,
                panel_bytes + arrived_bytes,
                panel_bytes + arrived_bytes,
            )
    return currents, field[None]


def solution(mesh):
    in_specs = (
        P(None, "patch", None),
        P("lag", "patch", None),
        P("patch", None, None),
        P("lag", "patch", None, None, None),
        P("lag", "patch", None),
        P("lag", "patch", None),
        P(),
    )
    out_specs = (P(None, "patch", None), P("lag", "patch", None))
    return jax.shard_map(body, mesh=mesh, in_specs=in_specs, out_specs=out_specs, check_vma=False)
```

```python
import jax
import jax.numpy as jnp
from jax import lax
from jax.experimental import pallas as pl
from jax.experimental.pallas import tpu as pltpu
from jax.sharding import PartitionSpec as P

VMEM, SMEM, HBM = pltpu.VMEM, pltpu.SMEM, pltpu.HBM
DMA = pltpu.SemaphoreType.DMA
MIB = 1 << 20


def call(kernel, outs, ins, scratch=(), flops=0, nbytes=0, vmem=0, aliases=None):
    out_shape = tuple(space(dims, dtype) for space, dims, dtype in outs)
    out_specs = tuple(pl.BlockSpec(memory_space=space) for space, _, _ in outs)
    run = pl.pallas_call(
        kernel,
        out_shape=out_shape,
        in_specs=[pl.BlockSpec(memory_space=space) for space, _ in ins],
        out_specs=out_specs,
        scratch_shapes=scratch,
        input_output_aliases=aliases or {},
        cost_estimate=pl.CostEstimate(flops=flops, bytes_accessed=nbytes, transcendentals=0),
        compiler_params=pltpu.CompilerParams(vmem_limit_bytes=vmem + 6 * MIB),
    )
    results = run(*(pltpu.with_memory_space_constraint(x, space) for space, x in ins))
    return results if len(outs) > 1 else results[0]


def started(*copies):
    copies = [pltpu.make_async_copy(*copy) for copy in copies]
    for copy in copies:
        copy.start()
    return copies


def request_kernel(
    per_patch, sources_hbm, owner_hbm, field_hbm, wanted_hbm, field, wanted, sources, owner_map, sems
):
    copies = started(
        (sources_hbm, sources, sems.at[0]),
        (owner_hbm, owner_map, sems.at[1]),
        (field_hbm, field, sems.at[2]),
    )
    patch = lax.broadcasted_iota(jnp.int32, wanted.shape, 0)
    for copy in copies[:2]:
        copy.wait()

    def entry(j, table):
        source = sources[0, 0, j]
        storage = owner_map[jnp.maximum(source, 0)]
        here = (patch == storage // per_patch) & (source >= 0)
        return jnp.where(here, storage % per_patch, table)

    wanted[...] = lax.fori_loop(
        0, sources.shape[2], entry, jnp.full(wanted.shape, -1, jnp.int32), unroll=8
    )
    started((wanted, wanted_hbm, sems.at[0]))[0].wait()
    copies[2].wait()


def panel_kernel(
    per_patch,
    rows_hbm,
    sources_hbm,
    owner_hbm,
    retarded,
    inverse_hbm,
    high,
    low_hbm,
    inverse,
    rows,
    sources,
    owner_map,
    parts,
    low,
    sems,
):
    size = retarded.shape[-1]
    slots, chunk = parts.shape[:2]
    chunks = retarded.shape[2] // chunk

    def fetch(c):
        part = retarded.at[0, 0, pl.ds(c * chunk, chunk)]
        return pltpu.make_async_copy(part, parts.at[c % slots], sems.at[c % slots])

    lists = started(
        (rows_hbm, rows, sems.at[slots]),
        (sources_hbm, sources, sems.at[slots + 1]),
        (owner_hbm, owner_map, sems.at[slots + 2]),
        (inverse_hbm, inverse, sems.at[slots + 3]),
    )
    for c in range(min(slots, chunks)):
        fetch(c).start()
    high[...] = jnp.zeros_like(high)
    low[...] = jnp.zeros_like(low)
    for copy in lists:
        copy.wait()

    def entry(c, k, carry):
        source = sources[0, 0, c * chunk + k]

        @pl.when(source >= 0)
        def _():
            owner = owner_map[source] // per_patch
            row = pl.multiple_of(rows[0, 0, c * chunk + k] * size, size)
            column = pl.multiple_of(owner * size, size)
            block = parts[c % slots, k]
            rounded = block.astype(high.dtype)
            rest = (block - rounded.astype(jnp.float32)).astype(low.dtype)
            high[pl.ds(row, size), pl.ds(column, size)] = rounded
            piece = column // low.shape[2]
            inside = pl.multiple_of(column - piece * low.shape[2], size)
            low[piece, pl.ds(row, size), pl.ds(inside, size)] = rest

        return carry

    for c in range(chunks):
        fetch(c).wait()
        lax.fori_loop(0, chunk, lambda k, carry, c=c: entry(c, k, carry), 0)
        if c + slots < chunks:
            fetch(c + slots).start()
    started((low, low_hbm, sems.at[0]))[0].wait()


def solved(excess, self_inverse):
    blocks, size, _ = self_inverse.shape
    parts = [
        jnp.dot(
            self_inverse[k],
            excess[k * size : (k + 1) * size],
            precision=lax.Precision.HIGHEST,
            preferred_element_type=jnp.float32,
        )
        for k in range(blocks)
    ]
    return jnp.concatenate(parts, axis=0).astype(jnp.bfloat16)


def product(here, high, low_hbm, arrived, low, total, sems, finish):
    patches, size, columns = arrived.shape
    pieces, _, depth = low.shape
    copies = [pltpu.make_async_copy(low_hbm.at[k], low.at[k], sems.at[k]) for k in range(pieces)]

    @pl.when(here)
    def _():
        for copy in copies:
            copy.start()
        rows = total.shape[0] // 2

        def half(part, carry):
            flat = arrived[...].reshape(patches * size, columns)
            mine = pl.ds(pl.multiple_of(part * rows, rows), rows)
            total[mine, :] = jnp.dot(high[mine, :], flat, preferred_element_type=jnp.float32)
            return carry

        lax.fori_loop(0, 2, half, 0)
        fresh = total[...]
        flat = arrived[...].reshape(patches * size, columns)
        for k, copy in enumerate(copies):
            copy.wait()
            part = flat[k * depth : (k + 1) * depth]
            fresh = fresh + jnp.dot(low[k], part, preferred_element_type=jnp.float32)
        finish(fresh)


def first_kernel(keeps, incident_hbm, own, received, inverse_hbm, current, incident, inverse, sems):
    copies = started(
        (incident_hbm.at[0], incident, sems.at[0]),
        (inverse_hbm, inverse, sems.at[1]),
    )
    field = jnp.where(lax.axis_index("lag") < keeps, own[...], received[...])
    for copy in copies:
        copy.wait()
    current[...] = solved(incident[...].astype(jnp.float32) - field, inverse)


def stage_kernel(step, incident_hbm, field, staged, incident, sem):
    first = lax.axis_index("lag") == 0

    @pl.when(first)
    def _():
        started((incident_hbm.at[step], incident, sem))[0].wait()
        staged[...] = incident[...].astype(jnp.float32) - field[...]

    @pl.when(jnp.logical_not(first))
    def _():
        staged[...] = field[...]


def solve_kernel(high, low_hbm, arrived, staged, inverse, current, low, total, sems):
    def finish(fresh):
        current[...] = solved(staged[...] - fresh, inverse)

    product(lax.axis_index("lag") == 0, high, low_hbm, arrived, low, total, sems, finish)


def partial_kernel(high, low_hbm, arrived, staged, after, partial, low, total, sems):
    del after

    def finish(fresh):
        partial[...] = staged[...] + fresh

    product(lax.axis_index("lag") > 0, high, low_hbm, arrived, low, total, sems, finish)


def asked_kernel(table, after, asked, copy_of, sem):
    del after
    started((table, copy_of, sem))[0].wait()
    for q in range(table.shape[0]):
        asked[q] = jnp.maximum(copy_of[q, 0, 0], 0)


def ahead_kernel(high, arrived, field, ahead_hbm, ahead, sems):
    patches, size, columns = arrived.shape
    rows = ahead.shape[0] // sems.shape[0]
    copies = []
    for part in range(sems.shape[0]):
        here = pl.ds(part * rows, rows)
        flat = arrived[...].reshape(patches * size, columns)
        fresh = jnp.dot(high[here, :], flat, preferred_element_type=jnp.float32)
        ahead[here, :] = field[here, :] + fresh
        copies += started((ahead.at[here], ahead_hbm.at[here], sems.at[part]))
    for copy in copies:
        copy.wait()


def pack_kernel(step, keeps, early, asked, current, *refs):
    outgoing, currents, sems = refs[-3:]
    patches, size, _ = outgoing.shape
    section = lax.axis_index("lag")

    @pl.when(section < keeps if early else section >= keeps)
    def _():
        copies = []
        for q in range(patches):
            start = pl.multiple_of(asked[q] * size, size)
            copies.append((current.at[pl.ds(start, size)], outgoing.at[q], sems.at[q]))
        copies.append((current, currents.at[step], sems.at[patches]))
        for copy in started(*copies):
            copy.wait()


def shifted(x):
    sections = lax.axis_size("lag")
    return lax.ppermute(x, "lag", [(i, i - 1) for i in range(1, sections)])


def spread(x):
    sections = lax.axis_size("lag")
    section = lax.axis_index("lag")
    received, keeps = x, 1
    while keeps < sections:
        if keeps > 1:
            x = jnp.where(section < keeps // 2, x, received)
        pairs = [(i, i + keeps) for i in range(keeps) if i + keeps < sections]
        received = lax.ppermute(x, "lag", pairs)
        keeps *= 2
    return x, received, max(keeps // 2, 1)


def body(incident, pending, self_inverse, retarded, block_rows, block_sources, owner_map):
    steps, unknowns, columns = incident.shape
    per_patch, size, _ = self_inverse.shape
    listed = retarded.shape[2]
    patches = lax.axis_size("patch")
    bf16, f32 = jnp.bfloat16, jnp.float32
    all_flops = 4 * unknowns * patches * size * columns
    solve_flops = 12 * unknowns * size * columns
    panel_bytes = 4 * unknowns * patches * size
    column = (unknowns, columns)
    arrived_bytes = 2 * patches * size * columns

    def exchange(x):
        return lax.all_to_all(x, "patch", split_axis=0, concat_axis=0, tiled=True)

    def pack(step, keeps, early, current, filled, after=()):
        held = [x for x in filled if x is not None]
        aliases = {}
        for out, x in enumerate(filled):
            if x is not None:
                aliases[2 + len(after) + len(aliases)] = out
        return call(
            lambda *refs: pack_kernel(step, keeps, early, *refs),
            [(HBM, (patches, size, columns), bf16), (HBM, incident.shape, bf16)],
            [(SMEM, asked), (VMEM, current)] + [(VMEM, x) for x in after] + [(HBM, x) for x in held],
            [DMA((patches + 1,))],
            aliases=aliases,
        )

    wanted, first_field = call(
        lambda *refs: request_kernel(per_patch, *refs),
        [(HBM, (patches, 8, 128), jnp.int32), (VMEM, column, f32)],
        [(HBM, block_sources), (HBM, owner_map), (HBM, pending[0])],
        [
            pltpu.VMEM((patches, 8, 128), jnp.int32),
            pltpu.SMEM(block_sources.shape, jnp.int32),
            pltpu.SMEM(owner_map.shape, jnp.int32),
            DMA((3,)),
        ],
    )
    requests = exchange(wanted)
    own, received, keeps = spread(first_field)
    solve_scratch = [pltpu.VMEM(column, bf16), pltpu.VMEM(self_inverse.shape, f32), DMA((3,))]
    current = call(
        lambda *refs: first_kernel(keeps, *refs),
        [(VMEM, column, bf16)],
        [(HBM, incident), (VMEM, own), (VMEM, received), (HBM, self_inverse)],
        solve_scratch,
        solve_flops,
    )
    asked = call(
        asked_kernel,
        [(SMEM, (patches,), jnp.int32)],
        [(VMEM, requests), (VMEM, current)],
        [pltpu.SMEM(wanted.shape, jnp.int32), DMA],
    )
    chunk = max(n for n in range(1, 9) if listed % n == 0)
    panel = (unknowns, patches * size)
    pieces = 4 if patches % 4 == 0 else 1
    low_panel = (pieces, unknowns, patches * size // pieces)
    high, low, inverse = call(
        lambda *refs: panel_kernel(per_patch, *refs),
        [(VMEM, panel, bf16), (HBM, low_panel, bf16), (VMEM, self_inverse.shape, f32)],
        [(HBM, block_rows), (HBM, block_sources), (HBM, owner_map), (HBM, retarded), (HBM, self_inverse)],
        [
            pltpu.SMEM(block_rows.shape, jnp.int32),
            pltpu.SMEM(block_sources.shape, jnp.int32),
            pltpu.SMEM(owner_map.shape, jnp.int32),
            pltpu.VMEM((3, chunk, size, size), f32),
            pltpu.VMEM(low_panel, bf16),
            DMA((7,)),
        ],
        nbytes=listed * size * size * 4 + panel_bytes,
        vmem=panel_bytes // 2,
    )

    field = pending[0]
    outgoing, currents = pack(0, lax.axis_size("lag"), True, current, (None, None))
    for step in range(steps):
        if step > 0:
            own, received, keeps = spread(current)
            outgoing, currents = pack(step, keeps, True, own, (None, currents))
            if lax.axis_size("lag") > 1:
                outgoing, currents = pack(step, keeps, False, received, (outgoing, currents), [field])
        arrived = exchange(outgoing)
        field = shifted(field)
        if step + 1 < steps:
            staged = call(
                lambda *refs, n=step + 1: stage_kernel(n, *refs),
                [(VMEM, column, f32)],
                [(HBM, incident), (VMEM, field)],
                [pltpu.VMEM(column, bf16), DMA],
            )
            shared = [(VMEM, high), (HBM, low), (VMEM, arrived), (VMEM, staged)]
            scratch = [pltpu.VMEM(low_panel, bf16), pltpu.VMEM(column, f32), DMA((pieces,))]
            sizes = [all_flops, panel_bytes + arrived_bytes, panel_bytes + arrived_bytes]
            current = call(
                solve_kernel, [(VMEM, column, bf16)], [*shared, (VMEM, inverse)], scratch, *sizes
            )
            field = call(
                partial_kernel, [(VMEM, column, f32)], [*shared, (VMEM, current)], scratch, *sizes
            )
        else:
            field = call(
                ahead_kernel,
                [(HBM, column, f32)],
                [(VMEM, high), (VMEM, arrived), (VMEM, field)],
                [pltpu.VMEM(column, f32), DMA((2,))],
                all_flops,
                panel_bytes + arrived_bytes,
                panel_bytes + arrived_bytes,
            )
    return currents, field[None]


def solution(mesh):
    in_specs = (
        P(None, "patch", None),
        P("lag", "patch", None),
        P("patch", None, None),
        P("lag", "patch", None, None, None),
        P("lag", "patch", None),
        P("lag", "patch", None),
        P(),
    )
    out_specs = (P(None, "patch", None), P("lag", "patch", None))
    return jax.shard_map(body, mesh=mesh, in_specs=in_specs, out_specs=out_specs, check_vma=False)
```

```python
import jax
import jax.numpy as jnp
from jax import lax
from jax.experimental import pallas as pl
from jax.experimental.pallas import tpu as pltpu
from jax.sharding import PartitionSpec as P

VMEM, SMEM, HBM = pltpu.VMEM, pltpu.SMEM, pltpu.HBM
DMA = pltpu.SemaphoreType.DMA
MIB = 1 << 20


def call(kernel, outs, ins, scratch=(), flops=0, nbytes=0, vmem=0, aliases=None):
    out_shape = tuple(space(dims, dtype) for space, dims, dtype in outs)
    out_specs = tuple(pl.BlockSpec(memory_space=space) for space, _, _ in outs)
    run = pl.pallas_call(
        kernel,
        out_shape=out_shape,
        in_specs=[pl.BlockSpec(memory_space=space) for space, _ in ins],
        out_specs=out_specs,
        scratch_shapes=scratch,
        input_output_aliases=aliases or {},
        cost_estimate=pl.CostEstimate(flops=flops, bytes_accessed=nbytes, transcendentals=0),
        compiler_params=pltpu.CompilerParams(vmem_limit_bytes=vmem + 6 * MIB),
    )
    results = run(*(pltpu.with_memory_space_constraint(x, space) for space, x in ins))
    return results if len(outs) > 1 else results[0]


def started(*copies):
    copies = [pltpu.make_async_copy(*copy) for copy in copies]
    for copy in copies:
        copy.start()
    return copies


def request_kernel(per_patch, sources_hbm, owner_hbm, wanted_hbm, wanted, sources, owner_map, sems):
    copies = started(
        (sources_hbm, sources, sems.at[0]),
        (owner_hbm, owner_map, sems.at[1]),
    )
    patch = lax.broadcasted_iota(jnp.int32, wanted.shape, 0)
    for copy in copies:
        copy.wait()

    def entry(j, table):
        source = sources[0, 0, j]
        storage = owner_map[jnp.maximum(source, 0)]
        here = (patch == storage // per_patch) & (source >= 0)
        return jnp.where(here, storage % per_patch, table)

    wanted[...] = lax.fori_loop(
        0, sources.shape[2], entry, jnp.full(wanted.shape, -1, jnp.int32), unroll=8
    )
    started((wanted, wanted_hbm, sems.at[0]))[0].wait()


def panel_kernel(
    per_patch,
    rows_hbm,
    sources_hbm,
    owner_hbm,
    retarded,
    inverse_hbm,
    high,
    low_hbm,
    inverse,
    rows,
    sources,
    owner_map,
    parts,
    low,
    sems,
):
    size = retarded.shape[-1]
    slots, chunk = parts.shape[:2]
    chunks = retarded.shape[2] // chunk

    def fetch(c):
        part = retarded.at[0, 0, pl.ds(c * chunk, chunk)]
        return pltpu.make_async_copy(part, parts.at[c % slots], sems.at[c % slots])

    lists = started(
        (rows_hbm, rows, sems.at[slots]),
        (sources_hbm, sources, sems.at[slots + 1]),
        (owner_hbm, owner_map, sems.at[slots + 2]),
        (inverse_hbm, inverse, sems.at[slots + 3]),
    )
    for c in range(min(slots, chunks)):
        fetch(c).start()
    high[...] = jnp.zeros_like(high)
    low[...] = jnp.zeros_like(low)
    for copy in lists:
        copy.wait()

    def entry(c, k, carry):
        source = sources[0, 0, c * chunk + k]

        @pl.when(source >= 0)
        def _():
            owner = owner_map[source] // per_patch
            row = pl.multiple_of(rows[0, 0, c * chunk + k] * size, size)
            column = pl.multiple_of(owner * size, size)
            block = parts[c % slots, k]
            rounded = block.astype(high.dtype)
            rest = (block - rounded.astype(jnp.float32)).astype(low.dtype)
            high[pl.ds(row, size), pl.ds(column, size)] = rounded
            piece = column // low.shape[2]
            inside = pl.multiple_of(column - piece * low.shape[2], size)
            low[piece, pl.ds(row, size), pl.ds(inside, size)] = rest

        return carry

    for c in range(chunks):
        fetch(c).wait()
        lax.fori_loop(0, chunk, lambda k, carry, c=c: entry(c, k, carry), 0)
        if c + slots < chunks:
            fetch(c + slots).start()
    started((low, low_hbm, sems.at[0]))[0].wait()


def solved(excess, self_inverse):
    blocks, size, _ = self_inverse.shape
    parts = [
        jnp.dot(
            self_inverse[k],
            excess[k * size : (k + 1) * size],
            precision=lax.Precision.HIGHEST,
            preferred_element_type=jnp.float32,
        )
        for k in range(blocks)
    ]
    return jnp.concatenate(parts, axis=0).astype(jnp.bfloat16)


def product(here, high, low_hbm, arrived, low, total, sems, finish):
    patches, size, columns = arrived.shape
    pieces, _, depth = low.shape
    copies = [pltpu.make_async_copy(low_hbm.at[k], low.at[k], sems.at[k]) for k in range(pieces)]

    @pl.when(here)
    def _():
        for copy in copies:
            copy.start()
        rows = total.shape[0] // 2

        def half(part, carry):
            flat = arrived[...].reshape(patches * size, columns)
            mine = pl.ds(pl.multiple_of(part * rows, rows), rows)
            total[mine, :] = jnp.dot(high[mine, :], flat, preferred_element_type=jnp.float32)
            return carry

        lax.fori_loop(0, 2, half, 0)
        fresh = total[...]
        flat = arrived[...].reshape(patches * size, columns)
        for k, copy in enumerate(copies):
            copy.wait()
            part = flat[k * depth : (k + 1) * depth]
            fresh = fresh + jnp.dot(low[k], part, preferred_element_type=jnp.float32)
        finish(fresh)


def first_kernel(incident_hbm, field_hbm, inverse_hbm, after, current, incident, field, inverse, sems):
    del after

    @pl.when(lax.axis_index("lag") == 0)
    def _():
        copies = started(
            (incident_hbm.at[0], incident, sems.at[0]),
            (inverse_hbm, inverse, sems.at[1]),
            (field_hbm, field, sems.at[2]),
        )
        for copy in copies:
            copy.wait()
        current[...] = solved(incident[...].astype(jnp.float32) - field[...], inverse)


def stage_kernel(step, incident_hbm, field, staged, incident, sem):
    first = lax.axis_index("lag") == 0

    @pl.when(first)
    def _():
        started((incident_hbm.at[step], incident, sem))[0].wait()
        staged[...] = incident[...].astype(jnp.float32) - field[...]

    @pl.when(jnp.logical_not(first))
    def _():
        staged[...] = field[...]


def solve_kernel(high, low_hbm, arrived, staged, inverse, current, low, total, sems):
    def finish(fresh):
        current[...] = solved(staged[...] - fresh, inverse)

    product(lax.axis_index("lag") == 0, high, low_hbm, arrived, low, total, sems, finish)


def partial_kernel(high, low_hbm, arrived, staged, after, partial, low, total, sems):
    del after

    def finish(fresh):
        partial[...] = staged[...] + fresh

    product(lax.axis_index("lag") > 0, high, low_hbm, arrived, low, total, sems, finish)


def asked_kernel(table, asked, copy_of, sem):
    started((table, copy_of, sem))[0].wait()
    for q in range(table.shape[0]):
        asked[q] = jnp.maximum(copy_of[q, 0, 0], 0)


def ahead_kernel(high, arrived, field, ahead_hbm, ahead, sems):
    patches, size, columns = arrived.shape
    rows = ahead.shape[0] // sems.shape[0]
    copies = []
    for part in range(sems.shape[0]):
        here = pl.ds(part * rows, rows)
        flat = arrived[...].reshape(patches * size, columns)
        fresh = jnp.dot(high[here, :], flat, preferred_element_type=jnp.float32)
        ahead[here, :] = field[here, :] + fresh
        copies += started((ahead.at[here], ahead_hbm.at[here], sems.at[part]))
    for copy in copies:
        copy.wait()


def pack_kernel(step, keeps, early, asked, current, *refs):
    outgoing, currents, sems = refs[-3:]
    patches, size, _ = outgoing.shape
    section = lax.axis_index("lag")

    @pl.when(section < keeps if early else section >= keeps)
    def _():
        copies = []
        for q in range(patches):
            block = asked[q] if len(asked.shape) == 1 else jnp.max(jnp.maximum(asked[q], 0))
            start = pl.multiple_of(block * size, size)
            copies.append((current.at[pl.ds(start, size)], outgoing.at[q], sems.at[q]))
        copies.append((current, currents.at[step], sems.at[patches]))
        for copy in started(*copies):
            copy.wait()


def shifted(x):
    sections = lax.axis_size("lag")
    return lax.ppermute(x, "lag", [(i, i - 1) for i in range(1, sections)])


def spread(x):
    sections = lax.axis_size("lag")
    section = lax.axis_index("lag")
    received, keeps = x, 1
    while keeps < sections:
        if keeps > 1:
            x = jnp.where(section < keeps // 2, x, received)
        pairs = [(i, i + keeps) for i in range(keeps) if i + keeps < sections]
        received = lax.ppermute(x, "lag", pairs)
        keeps *= 2
    return x, received, max(keeps // 2, 1)


def body(incident, pending, self_inverse, retarded, block_rows, block_sources, owner_map):
    steps, unknowns, columns = incident.shape
    per_patch, size, _ = self_inverse.shape
    listed = retarded.shape[2]
    patches = lax.axis_size("patch")
    bf16, f32 = jnp.bfloat16, jnp.float32
    all_flops = 4 * unknowns * patches * size * columns
    solve_flops = 12 * unknowns * size * columns
    panel_bytes = 4 * unknowns * patches * size
    column = (unknowns, columns)
    arrived_bytes = 2 * patches * size * columns

    def exchange(x):
        return lax.all_to_all(x, "patch", split_axis=0, concat_axis=0, tiled=True)

    def pack(step, keeps, early, asked, current, filled, after=()):
        held = [x for x in filled if x is not None]
        aliases = {}
        for out, x in enumerate(filled):
            if x is not None:
                aliases[2 + len(after) + len(aliases)] = out
        return call(
            lambda *refs: pack_kernel(step, keeps, early, *refs),
            [(HBM, (patches, size, columns), bf16), (HBM, incident.shape, bf16)],
            [(SMEM if asked.ndim == 1 else VMEM, asked), (VMEM, current)] + [(VMEM, x) for x in after] + [(HBM, x) for x in held],
            [DMA((patches + 1,))],
            nbytes=0 if step else 128 * MIB,
            aliases=aliases,
        )

    wanted = call(
        lambda *refs: request_kernel(per_patch, *refs),
        [(HBM, (patches, 1, 128), jnp.int32)],
        [(HBM, block_sources), (HBM, owner_map)],
        [
            pltpu.VMEM((patches, 1, 128), jnp.int32),
            pltpu.SMEM(block_sources.shape, jnp.int32),
            pltpu.SMEM(owner_map.shape, jnp.int32),
            DMA((2,)),
        ],
    )
    requests = exchange(wanted)
    current = call(
        first_kernel,
        [(VMEM, column, bf16)],
        [(HBM, incident), (HBM, pending[0]), (HBM, self_inverse), (HBM, wanted)],
        [
            pltpu.VMEM(column, bf16),
            pltpu.VMEM(column, f32),
            pltpu.VMEM(self_inverse.shape, f32),
            DMA((3,)),
        ],
        solve_flops,
    )
    asked = call(
        asked_kernel,
        [(SMEM, (patches,), jnp.int32)],
        [(VMEM, requests)],
        [pltpu.SMEM(wanted.shape, jnp.int32), DMA],
    )
    chunk = max(n for n in range(1, 9) if listed % n == 0)
    panel = (unknowns, patches * size)
    pieces = 4 if patches % 4 == 0 else 1
    low_panel = (pieces, unknowns, patches * size // pieces)
    high, low, inverse = call(
        lambda *refs: panel_kernel(per_patch, *refs),
        [(VMEM, panel, bf16), (HBM, low_panel, bf16), (VMEM, self_inverse.shape, f32)],
        [(HBM, block_rows), (HBM, block_sources), (HBM, owner_map), (HBM, retarded), (HBM, self_inverse)],
        [
            pltpu.SMEM(block_rows.shape, jnp.int32),
            pltpu.SMEM(block_sources.shape, jnp.int32),
            pltpu.SMEM(owner_map.shape, jnp.int32),
            pltpu.VMEM((3, chunk, size, size), f32),
            pltpu.VMEM(low_panel, bf16),
            DMA((7,)),
        ],
        nbytes=listed * size * size * 4 + panel_bytes,
        vmem=panel_bytes // 2,
    )

    field = pending[0]
    currents = None
    for step in range(steps):
        own, received, keeps = spread(current)
        table = asked if step else requests
        outgoing, currents = pack(step, keeps, True, table, own, (None, currents))
        if lax.axis_size("lag") > 1:
            after = [field] if step else []
            outgoing, currents = pack(step, keeps, False, table, received, (outgoing, currents), after)
        arrived = exchange(outgoing)
        field = shifted(field)
        if step + 1 < steps:
            staged = call(
                lambda *refs, n=step + 1: stage_kernel(n, *refs),
                [(VMEM, column, f32)],
                [(HBM, incident), (VMEM, field)],
                [pltpu.VMEM(column, bf16), DMA],
            )
            shared = [(VMEM, high), (HBM, low), (VMEM, arrived), (VMEM, staged)]
            scratch = [pltpu.VMEM(low_panel, bf16), pltpu.VMEM(column, f32), DMA((pieces,))]
            sizes = [all_flops, panel_bytes + arrived_bytes, panel_bytes + arrived_bytes]
            current = call(
                solve_kernel, [(VMEM, column, bf16)], [*shared, (VMEM, inverse)], scratch, *sizes
            )
            field = call(
                partial_kernel, [(VMEM, column, f32)], [*shared, (VMEM, current)], scratch, *sizes
            )
        else:
            field = call(
                ahead_kernel,
                [(HBM, column, f32)],
                [(VMEM, high), (VMEM, arrived), (VMEM, field)],
                [pltpu.VMEM(column, f32), DMA((2,))],
                all_flops,
                panel_bytes + arrived_bytes,
                panel_bytes + arrived_bytes,
            )
    return currents, field[None]


def solution(mesh):
    in_specs = (
        P(None, "patch", None),
        P("lag", "patch", None),
        P("patch", None, None),
        P("lag", "patch", None, None, None),
        P("lag", "patch", None),
        P("lag", "patch", None),
        P(),
    )
    out_specs = (P(None, "patch", None), P("lag", "patch", None))
    return jax.shard_map(body, mesh=mesh, in_specs=in_specs, out_specs=out_specs, check_vma=False)
```

```python
import jax
import jax.numpy as jnp
from jax import lax
from jax.experimental import pallas as pl
from jax.experimental.pallas import tpu as pltpu
from jax.sharding import PartitionSpec as P

VMEM, SMEM, HBM = pltpu.VMEM, pltpu.SMEM, pltpu.HBM
DMA = pltpu.SemaphoreType.DMA
MIB = 1 << 20


def call(kernel, outs, ins, scratch=(), flops=0, nbytes=0, vmem=0, aliases=None):
    out_shape = tuple(space(dims, dtype) for space, dims, dtype in outs)
    out_specs = tuple(pl.BlockSpec(memory_space=space) for space, _, _ in outs)
    run = pl.pallas_call(
        kernel,
        out_shape=out_shape,
        in_specs=[pl.BlockSpec(memory_space=space) for space, _ in ins],
        out_specs=out_specs,
        scratch_shapes=scratch,
        input_output_aliases=aliases or {},
        cost_estimate=pl.CostEstimate(flops=flops, bytes_accessed=nbytes, transcendentals=0),
        compiler_params=pltpu.CompilerParams(vmem_limit_bytes=vmem + 6 * MIB),
    )
    results = run(*(pltpu.with_memory_space_constraint(x, space) for space, x in ins))
    return results if len(outs) > 1 else results[0]


def started(*copies):
    copies = [pltpu.make_async_copy(*copy) for copy in copies]
    for copy in copies:
        copy.start()
    return copies


def request_kernel(per_patch, sources_hbm, owner_hbm, wanted_hbm, wanted, sources, owner_map, sems):
    copies = started(
        (sources_hbm, sources, sems.at[0]),
        (owner_hbm, owner_map, sems.at[1]),
    )
    patch = lax.broadcasted_iota(jnp.int32, wanted.shape, 0)
    for copy in copies:
        copy.wait()

    def entry(j, table):
        source = sources[0, 0, j]
        storage = owner_map[jnp.maximum(source, 0)]
        here = (patch == storage // per_patch) & (source >= 0)
        return jnp.where(here, storage % per_patch, table)

    wanted[...] = lax.fori_loop(
        0, sources.shape[2], entry, jnp.full(wanted.shape, -1, jnp.int32), unroll=8
    )
    started((wanted, wanted_hbm, sems.at[0]))[0].wait()


def panel_kernel(
    per_patch,
    rows_hbm,
    sources_hbm,
    owner_hbm,
    retarded,
    inverse_hbm,
    high,
    low_hbm,
    inverse,
    rows,
    sources,
    owner_map,
    parts,
    low,
    sems,
):
    size = retarded.shape[-1]
    slots, chunk = parts.shape[:2]
    chunks = retarded.shape[2] // chunk

    def fetch(c):
        part = retarded.at[0, 0, pl.ds(c * chunk, chunk)]
        return pltpu.make_async_copy(part, parts.at[c % slots], sems.at[c % slots])

    lists = started(
        (rows_hbm, rows, sems.at[slots]),
        (sources_hbm, sources, sems.at[slots + 1]),
        (owner_hbm, owner_map, sems.at[slots + 2]),
        (inverse_hbm, inverse, sems.at[slots + 3]),
    )
    for c in range(min(slots, chunks)):
        fetch(c).start()
    high[...] = jnp.zeros_like(high)
    low[...] = jnp.zeros_like(low)
    for copy in lists:
        copy.wait()

    def entry(c, k, carry):
        source = sources[0, 0, c * chunk + k]

        @pl.when(source >= 0)
        def _():
            owner = owner_map[source] // per_patch
            row = pl.multiple_of(rows[0, 0, c * chunk + k] * size, size)
            column = pl.multiple_of(owner * size, size)
            block = parts[c % slots, k]
            rounded = block.astype(high.dtype)
            rest = (block - rounded.astype(jnp.float32)).astype(low.dtype)
            high[pl.ds(row, size), pl.ds(column, size)] = rounded
            piece = column // low.shape[2]
            inside = pl.multiple_of(column - piece * low.shape[2], size)
            low[piece, pl.ds(row, size), pl.ds(inside, size)] = rest

        return carry

    for c in range(chunks):
        fetch(c).wait()
        lax.fori_loop(0, chunk, lambda k, carry, c=c: entry(c, k, carry), 0)
        if c + slots < chunks:
            fetch(c + slots).start()
    started((low, low_hbm, sems.at[0]))[0].wait()


def solved(excess, self_inverse):
    blocks, size, _ = self_inverse.shape
    parts = [
        jnp.dot(
            self_inverse[k],
            excess[k * size : (k + 1) * size],
            precision=lax.Precision.HIGHEST,
            preferred_element_type=jnp.float32,
        )
        for k in range(blocks)
    ]
    return jnp.concatenate(parts, axis=0).astype(jnp.bfloat16)


def product(here, high, low_hbm, arrived, low, total, sems, finish):
    patches, size, columns = arrived.shape
    pieces, _, depth = low.shape
    copies = [pltpu.make_async_copy(low_hbm.at[k], low.at[k], sems.at[k]) for k in range(pieces)]

    @pl.when(here)
    def _():
        for copy in copies:
            copy.start()
        rows = total.shape[0] // 2

        def half(part, carry):
            flat = arrived[...].reshape(patches * size, columns)
            mine = pl.ds(pl.multiple_of(part * rows, rows), rows)
            total[mine, :] = jnp.dot(high[mine, :], flat, preferred_element_type=jnp.float32)
            return carry

        lax.fori_loop(0, 2, half, 0)
        fresh = total[...]
        flat = arrived[...].reshape(patches * size, columns)
        for k, copy in enumerate(copies):
            copy.wait()
            part = flat[k * depth : (k + 1) * depth]
            fresh = fresh + jnp.dot(low[k], part, preferred_element_type=jnp.float32)
        finish(fresh)


def first_kernel(incident_hbm, field_hbm, inverse_hbm, current, incident, field, inverse, sems):
    @pl.when(lax.axis_index("lag") == 0)
    def _():
        copies = started(
            (incident_hbm.at[0], incident, sems.at[0]),
            (inverse_hbm, inverse, sems.at[1]),
            (field_hbm, field, sems.at[2]),
        )
        for copy in copies:
            copy.wait()
        current[...] = solved(incident[...].astype(jnp.float32) - field[...], inverse)


def stage_kernel(step, incident_hbm, field, staged, incident, sem):
    first = lax.axis_index("lag") == 0

    @pl.when(first)
    def _():
        started((incident_hbm.at[step], incident, sem))[0].wait()
        staged[...] = incident[...].astype(jnp.float32) - field[...]

    @pl.when(jnp.logical_not(first))
    def _():
        staged[...] = field[...]


def solve_kernel(high, low_hbm, arrived, staged, inverse, current, low, total, sems):
    def finish(fresh):
        current[...] = solved(staged[...] - fresh, inverse)

    product(lax.axis_index("lag") == 0, high, low_hbm, arrived, low, total, sems, finish)


def partial_kernel(high, low_hbm, arrived, staged, after, partial, low, total, sems):
    del after

    def finish(fresh):
        partial[...] = staged[...] + fresh

    product(lax.axis_index("lag") > 0, high, low_hbm, arrived, low, total, sems, finish)


def asked_kernel(table, asked, copy_of, sem):
    started((table, copy_of, sem))[0].wait()
    for q in range(table.shape[0]):
        asked[q] = jnp.maximum(copy_of[q, 0, 0], 0)


def ahead_kernel(high, arrived, field, ahead_hbm, ahead, sems):
    patches, size, columns = arrived.shape
    rows = ahead.shape[0] // sems.shape[0]
    copies = []
    for part in range(sems.shape[0]):
        here = pl.ds(part * rows, rows)
        flat = arrived[...].reshape(patches * size, columns)
        fresh = jnp.dot(high[here, :], flat, preferred_element_type=jnp.float32)
        ahead[here, :] = field[here, :] + fresh
        copies += started((ahead.at[here], ahead_hbm.at[here], sems.at[part]))
    for copy in copies:
        copy.wait()


def pack_kernel(step, keeps, early, asked, current, *refs):
    outgoing, currents, sems = refs[-3:]
    patches, size, _ = outgoing.shape
    section = lax.axis_index("lag")

    @pl.when(section < keeps if early else section >= keeps)
    def _():
        copies = []
        for q in range(patches):
            block = asked[q] if len(asked.shape) == 1 else jnp.max(jnp.maximum(asked[q], 0))
            start = pl.multiple_of(block * size, size)
            copies.append((current.at[pl.ds(start, size)], outgoing.at[q], sems.at[q]))
        copies.append((current, currents.at[step], sems.at[patches]))
        for copy in started(*copies):
            copy.wait()


def shifted(x):
    sections = lax.axis_size("lag")
    return lax.ppermute(x, "lag", [(i, i - 1) for i in range(1, sections)])


def kept(sections):
    return 1 << max((sections - 1).bit_length() - 1, 0)


def spread(x):
    sections = lax.axis_size("lag")
    section = lax.axis_index("lag")
    received, keeps = x, 1
    while keeps < sections:
        if keeps > 1:
            x = jnp.where(section < keeps // 2, x, received)
        pairs = [(i, i + keeps) for i in range(keeps) if i + keeps < sections]
        received = lax.ppermute(x, "lag", pairs)
        keeps *= 2
    return x, received


def body(incident, pending, self_inverse, retarded, block_rows, block_sources, owner_map):
    steps, unknowns, columns = incident.shape
    per_patch, size, _ = self_inverse.shape
    listed = retarded.shape[2]
    patches = lax.axis_size("patch")
    bf16, f32 = jnp.bfloat16, jnp.float32
    all_flops = 4 * unknowns * patches * size * columns
    solve_flops = 12 * unknowns * size * columns
    panel_bytes = 4 * unknowns * patches * size
    column = (unknowns, columns)
    arrived_bytes = 2 * patches * size * columns

    def exchange(x):
        return lax.all_to_all(x, "patch", split_axis=0, concat_axis=0, tiled=True)

    def pack(step, keeps, early, asked, current, filled, after=()):
        held = [x for x in filled if x is not None]
        aliases = {}
        for out, x in enumerate(filled):
            if x is not None:
                aliases[2 + len(after) + len(aliases)] = out
        return call(
            lambda *refs: pack_kernel(step, keeps, early, *refs),
            [(HBM, (patches, size, columns), bf16), (HBM, incident.shape, bf16)],
            [(SMEM if asked.ndim == 1 else VMEM, asked), (VMEM if step else HBM, current)] + [(VMEM, x) for x in after] + [(HBM, x) for x in held],
            [DMA((patches + 1,))],
            aliases=aliases,
        )

    wanted = call(
        lambda *refs: request_kernel(per_patch, *refs),
        [(HBM, (patches, 1, 128), jnp.int32)],
        [(HBM, block_sources), (HBM, owner_map)],
        [
            pltpu.VMEM((patches, 1, 128), jnp.int32),
            pltpu.SMEM(block_sources.shape, jnp.int32),
            pltpu.SMEM(owner_map.shape, jnp.int32),
            DMA((2,)),
        ],
    )
    requests = exchange(wanted)
    def first():
        current = call(
            first_kernel,
            [(VMEM, column, bf16)],
            [(HBM, incident), (HBM, pending[0]), (HBM, self_inverse)],
            [
                pltpu.VMEM(column, bf16),
                pltpu.VMEM(column, f32),
                pltpu.VMEM(self_inverse.shape, f32),
                DMA((3,)),
            ],
            solve_flops,
        )
        return spread(current)

    def nothing():
        return (jnp.zeros(column, bf16),) * 2

    sections = lax.axis_size("lag")
    first_pair = lax.cond(lax.axis_index("lag") < sections, first, nothing)
    keeps = kept(sections)
    asked = call(
        asked_kernel,
        [(SMEM, (patches,), jnp.int32)],
        [(VMEM, requests)],
        [pltpu.SMEM(wanted.shape, jnp.int32), DMA],
    )
    chunk = max(n for n in range(1, 9) if listed % n == 0)
    panel = (unknowns, patches * size)
    pieces = 4 if patches % 4 == 0 else 1
    low_panel = (pieces, unknowns, patches * size // pieces)
    high, low, inverse = call(
        lambda *refs: panel_kernel(per_patch, *refs),
        [(VMEM, panel, bf16), (HBM, low_panel, bf16), (VMEM, self_inverse.shape, f32)],
        [(HBM, block_rows), (HBM, block_sources), (HBM, owner_map), (HBM, retarded), (HBM, self_inverse)],
        [
            pltpu.SMEM(block_rows.shape, jnp.int32),
            pltpu.SMEM(block_sources.shape, jnp.int32),
            pltpu.SMEM(owner_map.shape, jnp.int32),
            pltpu.VMEM((3, chunk, size, size), f32),
            pltpu.VMEM(low_panel, bf16),
            DMA((7,)),
        ],
        nbytes=listed * size * size * 4 + panel_bytes,
        vmem=panel_bytes // 2,
    )

    field = pending[0]
    currents = None
    for step in range(steps):
        own, received = spread(current) if step else first_pair
        table = asked if step else requests
        outgoing, currents = pack(step, keeps, True, table, own, (None, currents))
        if sections > 1:
            after = [field] if step else []
            outgoing, currents = pack(step, keeps, False, table, received, (outgoing, currents), after)
        arrived = exchange(outgoing)
        field = shifted(field)
        if step + 1 < steps:
            staged = call(
                lambda *refs, n=step + 1: stage_kernel(n, *refs),
                [(VMEM, column, f32)],
                [(HBM, incident), (VMEM, field)],
                [pltpu.VMEM(column, bf16), DMA],
            )
            shared = [(VMEM, high), (HBM, low), (VMEM, arrived), (VMEM, staged)]
            scratch = [pltpu.VMEM(low_panel, bf16), pltpu.VMEM(column, f32), DMA((pieces,))]
            sizes = [all_flops, panel_bytes + arrived_bytes, panel_bytes + arrived_bytes]
            current = call(
                solve_kernel, [(VMEM, column, bf16)], [*shared, (VMEM, inverse)], scratch, *sizes
            )
            field = call(
                partial_kernel, [(VMEM, column, f32)], [*shared, (VMEM, current)], scratch, *sizes
            )
        else:
            field = call(
                ahead_kernel,
                [(HBM, column, f32)],
                [(VMEM, high), (VMEM, arrived), (VMEM, field)],
                [pltpu.VMEM(column, f32), DMA((2,))],
                all_flops,
                panel_bytes + arrived_bytes,
                panel_bytes + arrived_bytes,
            )
    return currents, field[None]


def solution(mesh):
    in_specs = (
        P(None, "patch", None),
        P("lag", "patch", None),
        P("patch", None, None),
        P("lag", "patch", None, None, None),
        P("lag", "patch", None),
        P("lag", "patch", None),
        P(),
    )
    out_specs = (P(None, "patch", None), P("lag", "patch", None))
    return jax.shard_map(body, mesh=mesh, in_specs=in_specs, out_specs=out_specs, check_vma=False)
```

```python
import jax
import jax.numpy as jnp
from jax import lax
from jax.experimental import pallas as pl
from jax.experimental.pallas import tpu as pltpu
from jax.sharding import PartitionSpec as P

VMEM, SMEM, HBM = pltpu.VMEM, pltpu.SMEM, pltpu.HBM
DMA = pltpu.SemaphoreType.DMA
MIB = 1 << 20


def call(kernel, outs, ins, scratch=(), flops=0, nbytes=0, vmem=0, aliases=None):
    out_shape = tuple(space(dims, dtype) for space, dims, dtype in outs)
    out_specs = tuple(pl.BlockSpec(memory_space=space) for space, _, _ in outs)
    run = pl.pallas_call(
        kernel,
        out_shape=out_shape,
        in_specs=[pl.BlockSpec(memory_space=space) for space, _ in ins],
        out_specs=out_specs,
        scratch_shapes=scratch,
        input_output_aliases=aliases or {},
        cost_estimate=pl.CostEstimate(flops=flops, bytes_accessed=nbytes, transcendentals=0),
        compiler_params=pltpu.CompilerParams(vmem_limit_bytes=vmem + 6 * MIB),
    )
    results = run(*(pltpu.with_memory_space_constraint(x, space) for space, x in ins))
    return results if len(outs) > 1 else results[0]


def started(*copies):
    copies = [pltpu.make_async_copy(*copy) for copy in copies]
    for copy in copies:
        copy.start()
    return copies


def request_kernel(per_patch, sources_hbm, owner_hbm, wanted_hbm, wanted, sources, owner_map, sems):
    copies = started(
        (sources_hbm, sources, sems.at[0]),
        (owner_hbm, owner_map, sems.at[1]),
    )
    patch = lax.broadcasted_iota(jnp.int32, wanted.shape, 0)
    for copy in copies:
        copy.wait()

    def entry(j, table):
        source = sources[0, 0, j]
        storage = owner_map[jnp.maximum(source, 0)]
        here = (patch == storage // per_patch) & (source >= 0)
        return jnp.where(here, storage % per_patch, table)

    wanted[...] = lax.fori_loop(
        0, sources.shape[2], entry, jnp.full(wanted.shape, -1, jnp.int32), unroll=8
    )
    started((wanted, wanted_hbm, sems.at[0]))[0].wait()


def panel_kernel(
    per_patch,
    rows_hbm,
    sources_hbm,
    owner_hbm,
    retarded,
    inverse_hbm,
    high,
    low_hbm,
    inverse,
    rows,
    sources,
    owner_map,
    parts,
    low,
    sems,
):
    size = retarded.shape[-1]
    slots, chunk = parts.shape[:2]
    chunks = retarded.shape[2] // chunk

    def fetch(c):
        part = retarded.at[0, 0, pl.ds(c * chunk, chunk)]
        return pltpu.make_async_copy(part, parts.at[c % slots], sems.at[c % slots])

    lists = started(
        (rows_hbm, rows, sems.at[slots]),
        (sources_hbm, sources, sems.at[slots + 1]),
        (owner_hbm, owner_map, sems.at[slots + 2]),
        (inverse_hbm, inverse, sems.at[slots + 3]),
    )
    for c in range(min(slots, chunks)):
        fetch(c).start()
    high[...] = jnp.zeros_like(high)
    low[...] = jnp.zeros_like(low)
    for copy in lists:
        copy.wait()

    def entry(c, k, carry):
        source = sources[0, 0, c * chunk + k]

        @pl.when(source >= 0)
        def _():
            owner = owner_map[source] // per_patch
            row = pl.multiple_of(rows[0, 0, c * chunk + k] * size, size)
            column = pl.multiple_of(owner * size, size)
            block = parts[c % slots, k]
            rounded = block.astype(high.dtype)
            rest = (block - rounded.astype(jnp.float32)).astype(low.dtype)
            high[pl.ds(row, size), pl.ds(column, size)] = rounded
            piece = column // low.shape[2]
            inside = pl.multiple_of(column - piece * low.shape[2], size)
            low[piece, pl.ds(row, size), pl.ds(inside, size)] = rest

        return carry

    for c in range(chunks):
        fetch(c).wait()
        lax.fori_loop(0, chunk, lambda k, carry, c=c: entry(c, k, carry), 0)
        if c + slots < chunks:
            fetch(c + slots).start()
    started((low, low_hbm, sems.at[0]))[0].wait()


def solved(excess, self_inverse):
    blocks, size, _ = self_inverse.shape
    parts = [
        jnp.dot(
            self_inverse[k],
            excess[k * size : (k + 1) * size],
            precision=lax.Precision.HIGHEST,
            preferred_element_type=jnp.float32,
        )
        for k in range(blocks)
    ]
    return jnp.concatenate(parts, axis=0).astype(jnp.bfloat16)


def product(here, high, low_hbm, arrived, low, total, sems, finish):
    patches, size, columns = arrived.shape
    pieces, _, depth = low.shape
    copies = [pltpu.make_async_copy(low_hbm.at[k], low.at[k], sems.at[k]) for k in range(pieces)]

    @pl.when(here)
    def _():
        for copy in copies:
            copy.start()
        rows = total.shape[0] // 2

        def half(part, carry):
            flat = arrived[...].reshape(patches * size, columns)
            mine = pl.ds(pl.multiple_of(part * rows, rows), rows)
            total[mine, :] = jnp.dot(high[mine, :], flat, preferred_element_type=jnp.float32)
            return carry

        lax.fori_loop(0, 2, half, 0)
        fresh = total[...]
        flat = arrived[...].reshape(patches * size, columns)
        for k, copy in enumerate(copies):
            copy.wait()
            part = flat[k * depth : (k + 1) * depth]
            fresh = fresh + jnp.dot(low[k], part, preferred_element_type=jnp.float32)
        finish(fresh)


def first_kernel(incident_hbm, field_hbm, inverse_hbm, current, incident, field, inverse, sems):
    @pl.when(lax.axis_index("lag") == 0)
    def _():
        copies = started(
            (incident_hbm.at[0], incident, sems.at[0]),
            (inverse_hbm, inverse, sems.at[1]),
            (field_hbm, field, sems.at[2]),
        )
        for copy in copies:
            copy.wait()
        current[...] = solved(incident[...].astype(jnp.float32) - field[...], inverse)


def stage_kernel(step, incident_hbm, field, staged, incident, sem):
    first = lax.axis_index("lag") == 0

    @pl.when(first)
    def _():
        started((incident_hbm.at[step], incident, sem))[0].wait()
        staged[...] = incident[...].astype(jnp.float32) - field[...]

    @pl.when(jnp.logical_not(first))
    def _():
        staged[...] = field[...]


def solve_kernel(high, low_hbm, arrived, staged, inverse, current, low, total, sems):
    def finish(fresh):
        current[...] = solved(staged[...] - fresh, inverse)

    product(lax.axis_index("lag") == 0, high, low_hbm, arrived, low, total, sems, finish)


def partial_kernel(high, low_hbm, arrived, staged, after, partial, low, total, sems):
    del after

    def finish(fresh):
        partial[...] = staged[...] + fresh

    product(lax.axis_index("lag") > 0, high, low_hbm, arrived, low, total, sems, finish)


def asked_kernel(table, asked, copy_of, sem):
    started((table, copy_of, sem))[0].wait()
    for q in range(table.shape[0]):
        asked[q] = jnp.maximum(copy_of[q, 0, 0], 0)


def ahead_kernel(high, arrived, field, ahead_hbm, ahead, sems):
    patches, size, columns = arrived.shape
    rows = ahead.shape[0] // sems.shape[0]
    copies = []
    for part in range(sems.shape[0]):
        here = pl.ds(part * rows, rows)
        flat = arrived[...].reshape(patches * size, columns)
        fresh = jnp.dot(high[here, :], flat, preferred_element_type=jnp.float32)
        ahead[here, :] = field[here, :] + fresh
        copies += started((ahead.at[here], ahead_hbm.at[here], sems.at[part]))
    for copy in copies:
        copy.wait()


def pack_kernel(step, keeps, early, asked, current, *refs):
    outgoing, currents, sems = refs[-3:]
    patches, size, _ = outgoing.shape
    section = lax.axis_index("lag")

    @pl.when(section < keeps if early else section >= keeps)
    def _():
        copies = []
        for q in range(patches):
            block = asked[q] if len(asked.shape) == 1 else jnp.max(jnp.maximum(asked[q], 0))
            start = pl.multiple_of(block * size, size)
            copies.append((current.at[pl.ds(start, size)], outgoing.at[q], sems.at[q]))
        copies.append((current, currents.at[step], sems.at[patches]))
        for copy in started(*copies):
            copy.wait()


def shifted(x):
    sections = lax.axis_size("lag")
    return lax.ppermute(x, "lag", [(i, i - 1) for i in range(1, sections)])


def kept(sections):
    return 1 << max((sections - 1).bit_length() - 1, 0)


def spread(x):
    sections = lax.axis_size("lag")
    section = lax.axis_index("lag")
    received, keeps = x, 1
    while keeps < sections:
        if keeps > 1:
            x = jnp.where(section < keeps // 2, x, received)
        pairs = [(i, i + keeps) for i in range(keeps) if i + keeps < sections]
        received = lax.ppermute(x, "lag", pairs)
        keeps *= 2
    return x, received


def body(incident, pending, self_inverse, retarded, block_rows, block_sources, owner_map):
    steps, unknowns, columns = incident.shape
    per_patch, size, _ = self_inverse.shape
    listed = retarded.shape[2]
    patches = lax.axis_size("patch")
    bf16, f32 = jnp.bfloat16, jnp.float32
    all_flops = 4 * unknowns * patches * size * columns
    solve_flops = 12 * unknowns * size * columns
    panel_bytes = 4 * unknowns * patches * size
    column = (unknowns, columns)
    arrived_bytes = 2 * patches * size * columns

    def exchange(x):
        return lax.all_to_all(x, "patch", split_axis=0, concat_axis=0, tiled=True)

    def pack(step, keeps, early, asked, current, filled, after=()):
        held = [x for x in filled if x is not None]
        aliases = {}
        for out, x in enumerate(filled):
            if x is not None:
                aliases[2 + len(after) + len(aliases)] = out
        return call(
            lambda *refs: pack_kernel(step, keeps, early, *refs),
            [(HBM, (patches, size, columns), bf16), (HBM, incident.shape, bf16)],
            [(SMEM if asked.ndim == 1 else VMEM, asked), (VMEM, current)] + [(VMEM, x) for x in after] + [(HBM, x) for x in held],
            [DMA((patches + 1,))],
            aliases=aliases,
        )

    wanted = call(
        lambda *refs: request_kernel(per_patch, *refs),
        [(HBM, (patches, 1, 128), jnp.int32)],
        [(HBM, block_sources), (HBM, owner_map)],
        [
            pltpu.VMEM((patches, 1, 128), jnp.int32),
            pltpu.SMEM(block_sources.shape, jnp.int32),
            pltpu.SMEM(owner_map.shape, jnp.int32),
            DMA((2,)),
        ],
    )
    requests = exchange(wanted)
    def first():
        current = call(
            first_kernel,
            [(VMEM, column, bf16)],
            [(HBM, incident), (HBM, pending[0]), (HBM, self_inverse)],
            [
                pltpu.VMEM(column, bf16),
                pltpu.VMEM(column, f32),
                pltpu.VMEM(self_inverse.shape, f32),
                DMA((3,)),
            ],
            solve_flops,
        )
        return spread(current)

    def nothing():
        return (jnp.zeros(column, bf16),) * 2

    sections = lax.axis_size("lag")
    first_pair = lax.cond(lax.axis_index("lag") < sections, first, nothing)
    keeps = kept(sections)
    asked = call(
        asked_kernel,
        [(SMEM, (patches,), jnp.int32)],
        [(VMEM, requests)],
        [pltpu.SMEM(wanted.shape, jnp.int32), DMA],
    )
    chunk = max(n for n in range(1, 9) if listed % n == 0)
    panel = (unknowns, patches * size)
    pieces = 4 if patches % 4 == 0 else 1
    low_panel = (pieces, unknowns, patches * size // pieces)
    high, low, inverse = call(
        lambda *refs: panel_kernel(per_patch, *refs),
        [(VMEM, panel, bf16), (HBM, low_panel, bf16), (VMEM, self_inverse.shape, f32)],
        [(HBM, block_rows), (HBM, block_sources), (HBM, owner_map), (HBM, retarded), (HBM, self_inverse)],
        [
            pltpu.SMEM(block_rows.shape, jnp.int32),
            pltpu.SMEM(block_sources.shape, jnp.int32),
            pltpu.SMEM(owner_map.shape, jnp.int32),
            pltpu.VMEM((3, chunk, size, size), f32),
            pltpu.VMEM(low_panel, bf16),
            DMA((7,)),
        ],
        nbytes=listed * size * size * 4 + panel_bytes,
        vmem=panel_bytes // 2,
    )

    field = pending[0]
    currents = None
    for step in range(steps):
        own, received = spread(current) if step else first_pair
        table = asked if step else requests
        outgoing, currents = pack(step, keeps, True, table, own, (None, currents))
        if sections > 1:
            after = [field] if step else []
            outgoing, currents = pack(step, keeps, False, table, received, (outgoing, currents), after)
        arrived = exchange(outgoing)
        field = shifted(field)
        if step + 1 < steps:
            staged = call(
                lambda *refs, n=step + 1: stage_kernel(n, *refs),
                [(VMEM, column, f32)],
                [(HBM, incident), (VMEM, field)],
                [pltpu.VMEM(column, bf16), DMA],
            )
            shared = [(VMEM, high), (HBM, low), (VMEM, arrived), (VMEM, staged)]
            scratch = [pltpu.VMEM(low_panel, bf16), pltpu.VMEM(column, f32), DMA((pieces,))]
            sizes = [all_flops, panel_bytes + arrived_bytes, panel_bytes + arrived_bytes]
            current = call(
                solve_kernel, [(VMEM, column, bf16)], [*shared, (VMEM, inverse)], scratch, *sizes
            )
            field = call(
                partial_kernel, [(VMEM, column, f32)], [*shared, (VMEM, current)], scratch, *sizes
            )
        else:
            field = call(
                ahead_kernel,
                [(HBM, column, f32)],
                [(VMEM, high), (VMEM, arrived), (VMEM, field)],
                [pltpu.VMEM(column, f32), DMA((2,))],
                all_flops,
                panel_bytes + arrived_bytes,
                panel_bytes + arrived_bytes,
            )
    return currents, field[None]


def solution(mesh):
    in_specs = (
        P(None, "patch", None),
        P("lag", "patch", None),
        P("patch", None, None),
        P("lag", "patch", None, None, None),
        P("lag", "patch", None),
        P("lag", "patch", None),
        P(),
    )
    out_specs = (P(None, "patch", None), P("lag", "patch", None))
    return jax.shard_map(body, mesh=mesh, in_specs=in_specs, out_specs=out_specs, check_vma=False)
```

```python
import jax
import jax.numpy as jnp
from jax import lax
from jax.experimental import pallas as pl
from jax.experimental.pallas import tpu as pltpu
from jax.sharding import PartitionSpec as P

VMEM, SMEM, HBM = pltpu.VMEM, pltpu.SMEM, pltpu.HBM
DMA = pltpu.SemaphoreType.DMA
MIB = 1 << 20


def call(kernel, outs, ins, scratch=(), flops=0, nbytes=0, vmem=0, aliases=None):
    out_shape = tuple(space(dims, dtype) for space, dims, dtype in outs)
    out_specs = tuple(pl.BlockSpec(memory_space=space) for space, _, _ in outs)
    run = pl.pallas_call(
        kernel,
        out_shape=out_shape,
        in_specs=[pl.BlockSpec(memory_space=space) for space, _ in ins],
        out_specs=out_specs,
        scratch_shapes=scratch,
        input_output_aliases=aliases or {},
        cost_estimate=pl.CostEstimate(flops=flops, bytes_accessed=nbytes, transcendentals=0),
        compiler_params=pltpu.CompilerParams(vmem_limit_bytes=vmem + 6 * MIB),
    )
    results = run(*(pltpu.with_memory_space_constraint(x, space) for space, x in ins))
    return results if len(outs) > 1 else results[0]


def slot_of(patch, patches):
    half = patches // 2
    return patch if patches % 2 else patch % half * 2 + patch // half


def patch_in(slot, patches):
    return slot if patches % 2 else slot % 2 * (patches // 2) + slot // 2


def started(*copies):
    copies = [pltpu.make_async_copy(*copy) for copy in copies]
    for copy in copies:
        copy.start()
    return copies


def request_kernel(per_patch, sources_hbm, owner_hbm, wanted_hbm, wanted, sources, owner_map, sems):
    copies = started(
        (sources_hbm, sources, sems.at[0]),
        (owner_hbm, owner_map, sems.at[1]),
    )
    patches = wanted.shape[0]
    slot = lax.broadcasted_iota(jnp.int32, wanted.shape, 0)
    for copy in copies:
        copy.wait()

    def entry(j, table):
        source = sources[0, 0, j]
        storage = owner_map[jnp.maximum(source, 0)]
        here = (slot == slot_of(storage // per_patch, patches)) & (source >= 0)
        return jnp.where(here, storage % per_patch, table)

    wanted[...] = lax.fori_loop(
        0, sources.shape[2], entry, jnp.full(wanted.shape, -1, jnp.int32), unroll=8
    )
    started((wanted, wanted_hbm, sems.at[0]))[0].wait()


def panel_kernel(
    per_patch,
    rows_hbm,
    sources_hbm,
    owner_hbm,
    retarded,
    inverse_hbm,
    high,
    low_hbm,
    inverse,
    rows,
    sources,
    owner_map,
    parts,
    low,
    sems,
):
    size = retarded.shape[-1]
    slots, chunk = parts.shape[:2]
    chunks = retarded.shape[2] // chunk

    def fetch(c):
        part = retarded.at[0, 0, pl.ds(c * chunk, chunk)]
        return pltpu.make_async_copy(part, parts.at[c % slots], sems.at[c % slots])

    lists = started(
        (rows_hbm, rows, sems.at[slots]),
        (sources_hbm, sources, sems.at[slots + 1]),
        (owner_hbm, owner_map, sems.at[slots + 2]),
        (inverse_hbm, inverse, sems.at[slots + 3]),
    )
    for c in range(min(slots, chunks)):
        fetch(c).start()
    high[...] = jnp.zeros_like(high)
    low[...] = jnp.zeros_like(low)
    for copy in lists:
        copy.wait()

    def entry(c, k, carry):
        source = sources[0, 0, c * chunk + k]

        @pl.when(source >= 0)
        def _():
            owner = slot_of(owner_map[source] // per_patch, high.shape[1] // size)
            row = pl.multiple_of(rows[0, 0, c * chunk + k] * size, size)
            column = pl.multiple_of(owner * size, size)
            block = parts[c % slots, k]
            rounded = block.astype(high.dtype)
            rest = (block - rounded.astype(jnp.float32)).astype(low.dtype)
            high[pl.ds(row, size), pl.ds(column, size)] = rounded
            piece = column // low.shape[2]
            inside = pl.multiple_of(column - piece * low.shape[2], size)
            low[piece, pl.ds(row, size), pl.ds(inside, size)] = rest

        return carry

    for c in range(chunks):
        fetch(c).wait()
        lax.fori_loop(0, chunk, lambda k, carry, c=c: entry(c, k, carry), 0)
        if c + slots < chunks:
            fetch(c + slots).start()
    started((low, low_hbm, sems.at[0]))[0].wait()


def solved(excess, self_inverse):
    blocks, size, _ = self_inverse.shape
    parts = [
        jnp.dot(
            self_inverse[k],
            excess[k * size : (k + 1) * size],
            precision=lax.Precision.HIGHEST,
            preferred_element_type=jnp.float32,
        )
        for k in range(blocks)
    ]
    return jnp.concatenate(parts, axis=0).astype(jnp.bfloat16)


def product(here, high, low_hbm, arrived, low, total, sems, finish):
    patches, size, columns = arrived.shape
    pieces, _, depth = low.shape
    copies = [pltpu.make_async_copy(low_hbm.at[k], low.at[k], sems.at[k]) for k in range(pieces)]

    @pl.when(here)
    def _():
        for copy in copies:
            copy.start()
        rows = total.shape[0] // 2

        def half(part, carry):
            flat = arrived[...].reshape(patches * size, columns)
            mine = pl.ds(pl.multiple_of(part * rows, rows), rows)
            total[mine, :] = jnp.dot(high[mine, :], flat, preferred_element_type=jnp.float32)
            return carry

        lax.fori_loop(0, 2, half, 0)
        fresh = total[...]
        flat = arrived[...].reshape(patches * size, columns)
        for k, copy in enumerate(copies):
            copy.wait()
            part = flat[k * depth : (k + 1) * depth]
            fresh = fresh + jnp.dot(low[k], part, preferred_element_type=jnp.float32)
        finish(fresh)


def first_kernel(incident_hbm, field_hbm, inverse_hbm, after, current, incident, field, inverse, sems):
    del after

    @pl.when(lax.axis_index("lag") == 0)
    def _():
        copies = started(
            (incident_hbm.at[0], incident, sems.at[0]),
            (inverse_hbm, inverse, sems.at[1]),
            (field_hbm, field, sems.at[2]),
        )
        for copy in copies:
            copy.wait()
        current[...] = solved(incident[...].astype(jnp.float32) - field[...], inverse)


def stage_kernel(step, incident_hbm, field, staged, incident, sem):
    first = lax.axis_index("lag") == 0

    @pl.when(first)
    def _():
        started((incident_hbm.at[step], incident, sem))[0].wait()
        staged[...] = incident[...].astype(jnp.float32) - field[...]

    @pl.when(jnp.logical_not(first))
    def _():
        staged[...] = field[...]


def solve_kernel(high, low_hbm, arrived, staged, inverse, current, low, total, sems):
    def finish(fresh):
        current[...] = solved(staged[...] - fresh, inverse)

    product(lax.axis_index("lag") == 0, high, low_hbm, arrived, low, total, sems, finish)


def partial_kernel(high, low_hbm, arrived, staged, after, partial, low, total, sems):
    del after

    def finish(fresh):
        partial[...] = staged[...] + fresh

    product(lax.axis_index("lag") > 0, high, low_hbm, arrived, low, total, sems, finish)


def asked_kernel(table, asked, copy_of, sem):
    started((table, copy_of, sem))[0].wait()
    for q in range(table.shape[0]):
        asked[q] = jnp.maximum(copy_of[q, 0, 0], 0)


def ahead_kernel(high, arrived, field, ahead_hbm, ahead, sems):
    patches, size, columns = arrived.shape
    rows = ahead.shape[0] // sems.shape[0]
    copies = []
    for part in range(sems.shape[0]):
        here = pl.ds(part * rows, rows)
        flat = arrived[...].reshape(patches * size, columns)
        fresh = jnp.dot(high[here, :], flat, preferred_element_type=jnp.float32)
        ahead[here, :] = field[here, :] + fresh
        copies += started((ahead.at[here], ahead_hbm.at[here], sems.at[part]))
    for copy in copies:
        copy.wait()


def pack_kernel(step, keeps, early, asked, current, *refs):
    outgoing, currents, sems = refs[-3:]
    patches, size, _ = outgoing.shape
    section = lax.axis_index("lag")

    @pl.when(section < keeps if early else section >= keeps)
    def _():
        copies = []
        for q in range(patches):
            block = asked[q] if len(asked.shape) == 1 else jnp.max(jnp.maximum(asked[q], 0))
            start = pl.multiple_of(block * size, size)
            copies.append((current.at[pl.ds(start, size)], outgoing.at[q], sems.at[q]))
        copies.append((current, currents.at[step], sems.at[patches]))
        for copy in started(*copies):
            copy.wait()


def shifted(x):
    sections = lax.axis_size("lag")
    return lax.ppermute(x, "lag", [(i, i - 1) for i in range(1, sections)])


def spread(x):
    sections = lax.axis_size("lag")
    section = lax.axis_index("lag")
    received, keeps = x, 1
    while keeps < sections:
        if keeps > 1:
            x = jnp.where(section < keeps // 2, x, received)
        pairs = [(i, i + keeps) for i in range(keeps) if i + keeps < sections]
        received = lax.ppermute(x, "lag", pairs)
        keeps *= 2
    return x, received, max(keeps // 2, 1)


def body(incident, pending, self_inverse, retarded, block_rows, block_sources, owner_map):
    steps, unknowns, columns = incident.shape
    per_patch, size, _ = self_inverse.shape
    listed = retarded.shape[2]
    patches = lax.axis_size("patch")
    bf16, f32 = jnp.bfloat16, jnp.float32
    all_flops = 4 * unknowns * patches * size * columns
    solve_flops = 12 * unknowns * size * columns
    panel_bytes = 4 * unknowns * patches * size
    column = (unknowns, columns)
    arrived_bytes = 2 * patches * size * columns

    def exchange(x):
        order = [patch_in(slot, patches) for slot in range(patches)]
        return lax.all_to_all(
            x, "patch", split_axis=0, concat_axis=0, axis_index_groups=[order], tiled=True
        )

    def pack(step, keeps, early, asked, current, filled, after=()):
        held = [x for x in filled if x is not None]
        aliases = {}
        for out, x in enumerate(filled):
            if x is not None:
                aliases[2 + len(after) + len(aliases)] = out
        return call(
            lambda *refs: pack_kernel(step, keeps, early, *refs),
            [(HBM, (patches, size, columns), bf16), (HBM, incident.shape, bf16)],
            [(SMEM if asked.ndim == 1 else VMEM, asked), (VMEM, current)] + [(VMEM, x) for x in after] + [(HBM, x) for x in held],
            [DMA((patches + 1,))],
            nbytes=0 if step else 128 * MIB,
            aliases=aliases,
        )

    wanted = call(
        lambda *refs: request_kernel(per_patch, *refs),
        [(HBM, (patches, 1, 128), jnp.int32)],
        [(HBM, block_sources), (HBM, owner_map)],
        [
            pltpu.VMEM((patches, 1, 128), jnp.int32),
            pltpu.SMEM(block_sources.shape, jnp.int32),
            pltpu.SMEM(owner_map.shape, jnp.int32),
            DMA((2,)),
        ],
    )
    requests = exchange(wanted)
    current = call(
        first_kernel,
        [(VMEM, column, bf16)],
        [(HBM, incident), (HBM, pending[0]), (HBM, self_inverse), (HBM, wanted)],
        [
            pltpu.VMEM(column, bf16),
            pltpu.VMEM(column, f32),
            pltpu.VMEM(self_inverse.shape, f32),
            DMA((3,)),
        ],
        solve_flops,
    )
    asked = call(
        asked_kernel,
        [(SMEM, (patches,), jnp.int32)],
        [(VMEM, requests)],
        [pltpu.SMEM(wanted.shape, jnp.int32), DMA],
    )
    chunk = max(n for n in range(1, 9) if listed % n == 0)
    panel = (unknowns, patches * size)
    pieces = 4 if patches % 4 == 0 else 1
    low_panel = (pieces, unknowns, patches * size // pieces)
    high, low, inverse = call(
        lambda *refs: panel_kernel(per_patch, *refs),
        [(VMEM, panel, bf16), (HBM, low_panel, bf16), (VMEM, self_inverse.shape, f32)],
        [(HBM, block_rows), (HBM, block_sources), (HBM, owner_map), (HBM, retarded), (HBM, self_inverse)],
        [
            pltpu.SMEM(block_rows.shape, jnp.int32),
            pltpu.SMEM(block_sources.shape, jnp.int32),
            pltpu.SMEM(owner_map.shape, jnp.int32),
            pltpu.VMEM((3, chunk, size, size), f32),
            pltpu.VMEM(low_panel, bf16),
            DMA((7,)),
        ],
        nbytes=listed * size * size * 4 + panel_bytes,
        vmem=panel_bytes // 2,
    )

    field = pending[0]
    currents = None
    for step in range(steps):
        own, received, keeps = spread(current)
        table = asked if step else requests
        outgoing, currents = pack(step, keeps, True, table, own, (None, currents))
        if lax.axis_size("lag") > 1:
            after = [field] if step else []
            outgoing, currents = pack(step, keeps, False, table, received, (outgoing, currents), after)
        arrived = exchange(outgoing)
        field = shifted(field)
        if step + 1 < steps:
            staged = call(
                lambda *refs, n=step + 1: stage_kernel(n, *refs),
                [(VMEM, column, f32)],
                [(HBM, incident), (VMEM, field)],
                [pltpu.VMEM(column, bf16), DMA],
            )
            shared = [(VMEM, high), (HBM, low), (VMEM, arrived), (VMEM, staged)]
            scratch = [pltpu.VMEM(low_panel, bf16), pltpu.VMEM(column, f32), DMA((pieces,))]
            sizes = [all_flops, panel_bytes + arrived_bytes, panel_bytes + arrived_bytes]
            current = call(
                solve_kernel, [(VMEM, column, bf16)], [*shared, (VMEM, inverse)], scratch, *sizes
            )
            field = call(
                partial_kernel, [(VMEM, column, f32)], [*shared, (VMEM, current)], scratch, *sizes
            )
        else:
            field = call(
                ahead_kernel,
                [(HBM, column, f32)],
                [(VMEM, high), (VMEM, arrived), (VMEM, field)],
                [pltpu.VMEM(column, f32), DMA((2,))],
                all_flops,
                panel_bytes + arrived_bytes,
                panel_bytes + arrived_bytes,
            )
    return currents, field[None]


def solution(mesh):
    in_specs = (
        P(None, "patch", None),
        P("lag", "patch", None),
        P("patch", None, None),
        P("lag", "patch", None, None, None),
        P("lag", "patch", None),
        P("lag", "patch", None),
        P(),
    )
    out_specs = (P(None, "patch", None), P("lag", "patch", None))
    return jax.shard_map(body, mesh=mesh, in_specs=in_specs, out_specs=out_specs, check_vma=False)
```

```python
import jax
import jax.numpy as jnp
from jax import lax
from jax.experimental import pallas as pl
from jax.experimental.pallas import tpu as pltpu
from jax.sharding import PartitionSpec as P

VMEM, SMEM, HBM = pltpu.VMEM, pltpu.SMEM, pltpu.HBM
DMA = pltpu.SemaphoreType.DMA
MIB = 1 << 20


def call(kernel, outs, ins, scratch=(), flops=0, nbytes=0, vmem=0, aliases=None):
    out_shape = tuple(space(dims, dtype) for space, dims, dtype in outs)
    out_specs = tuple(pl.BlockSpec(memory_space=space) for space, _, _ in outs)
    run = pl.pallas_call(
        kernel,
        out_shape=out_shape,
        in_specs=[pl.BlockSpec(memory_space=space) for space, _ in ins],
        out_specs=out_specs,
        scratch_shapes=scratch,
        input_output_aliases=aliases or {},
        cost_estimate=pl.CostEstimate(flops=flops, bytes_accessed=nbytes, transcendentals=0),
        compiler_params=pltpu.CompilerParams(vmem_limit_bytes=vmem + 6 * MIB),
    )
    results = run(*(pltpu.with_memory_space_constraint(x, space) for space, x in ins))
    return results if len(outs) > 1 else results[0]


def started(*copies):
    copies = [pltpu.make_async_copy(*copy) for copy in copies]
    for copy in copies:
        copy.start()
    return copies


def request_kernel(per_patch, first, sources_hbm, owner_hbm, *refs):
    wanted_hbm, wanted, sources, owner_map, sems = refs[-5:]
    section = lax.axis_index("lag")

    def entry(j, table):
        source = sources[0, 0, j]
        storage = owner_map[jnp.maximum(source, 0)]
        patch = lax.broadcasted_iota(jnp.int32, wanted.shape, 0)
        here = (patch == storage // per_patch) & (source >= 0)
        return jnp.where(here, storage % per_patch, table)

    @pl.when(section == 0 if first else section > 0)
    def _():
        copies = started(
            (sources_hbm, sources, sems.at[0]),
            (owner_hbm, owner_map, sems.at[1]),
        )
        for copy in copies:
            copy.wait()
        wanted[...] = lax.fori_loop(
            0, sources.shape[2], entry, jnp.full(wanted.shape, -1, jnp.int32), unroll=8
        )
        started((wanted, wanted_hbm, sems.at[0]))[0].wait()


def panel_kernel(
    per_patch,
    rows_hbm,
    sources_hbm,
    owner_hbm,
    retarded,
    inverse_hbm,
    high,
    low_hbm,
    inverse,
    rows,
    sources,
    owner_map,
    parts,
    low,
    sems,
):
    size = retarded.shape[-1]
    slots, chunk = parts.shape[:2]
    chunks = retarded.shape[2] // chunk

    def fetch(c):
        part = retarded.at[0, 0, pl.ds(c * chunk, chunk)]
        return pltpu.make_async_copy(part, parts.at[c % slots], sems.at[c % slots])

    lists = started(
        (rows_hbm, rows, sems.at[slots]),
        (sources_hbm, sources, sems.at[slots + 1]),
        (owner_hbm, owner_map, sems.at[slots + 2]),
        (inverse_hbm, inverse, sems.at[slots + 3]),
    )
    for c in range(min(slots, chunks)):
        fetch(c).start()
    high[...] = jnp.zeros_like(high)
    low[...] = jnp.zeros_like(low)
    for copy in lists:
        copy.wait()

    def entry(c, k, carry):
        source = sources[0, 0, c * chunk + k]

        @pl.when(source >= 0)
        def _():
            owner = owner_map[source] // per_patch
            row = pl.multiple_of(rows[0, 0, c * chunk + k] * size, size)
            column = pl.multiple_of(owner * size, size)
            block = parts[c % slots, k]
            rounded = block.astype(high.dtype)
            rest = (block - rounded.astype(jnp.float32)).astype(low.dtype)
            high[pl.ds(row, size), pl.ds(column, size)] = rounded
            piece = column // low.shape[2]
            inside = pl.multiple_of(column - piece * low.shape[2], size)
            low[piece, pl.ds(row, size), pl.ds(inside, size)] = rest

        return carry

    for c in range(chunks):
        fetch(c).wait()
        lax.fori_loop(0, chunk, lambda k, carry, c=c: entry(c, k, carry), 0)
        if c + slots < chunks:
            fetch(c + slots).start()
    started((low, low_hbm, sems.at[0]))[0].wait()


def solved(excess, self_inverse):
    blocks, size, _ = self_inverse.shape
    parts = [
        jnp.dot(
            self_inverse[k],
            excess[k * size : (k + 1) * size],
            precision=lax.Precision.HIGHEST,
            preferred_element_type=jnp.float32,
        )
        for k in range(blocks)
    ]
    return jnp.concatenate(parts, axis=0).astype(jnp.bfloat16)


def product(here, high, low_hbm, arrived, low, total, sems, finish):
    patches, size, columns = arrived.shape
    pieces, _, depth = low.shape
    copies = [pltpu.make_async_copy(low_hbm.at[k], low.at[k], sems.at[k]) for k in range(pieces)]

    @pl.when(here)
    def _():
        for copy in copies:
            copy.start()
        rows = total.shape[0] // 2

        def half(part, carry):
            flat = arrived[...].reshape(patches * size, columns)
            mine = pl.ds(pl.multiple_of(part * rows, rows), rows)
            total[mine, :] = jnp.dot(high[mine, :], flat, preferred_element_type=jnp.float32)
            return carry

        lax.fori_loop(0, 2, half, 0)
        fresh = total[...]
        flat = arrived[...].reshape(patches * size, columns)
        for k, copy in enumerate(copies):
            copy.wait()
            part = flat[k * depth : (k + 1) * depth]
            fresh = fresh + jnp.dot(low[k], part, preferred_element_type=jnp.float32)
        finish(fresh)


def first_kernel(incident_hbm, field_hbm, inverse_hbm, after, current, incident, field, inverse, sems):
    del after

    @pl.when(lax.axis_index("lag") == 0)
    def _():
        copies = started(
            (incident_hbm.at[0], incident, sems.at[0]),
            (inverse_hbm, inverse, sems.at[1]),
            (field_hbm, field, sems.at[2]),
        )
        for copy in copies:
            copy.wait()
        current[...] = solved(incident[...].astype(jnp.float32) - field[...], inverse)


def stage_kernel(step, incident_hbm, field, staged, incident, sem):
    first = lax.axis_index("lag") == 0

    @pl.when(first)
    def _():
        started((incident_hbm.at[step], incident, sem))[0].wait()
        staged[...] = incident[...].astype(jnp.float32) - field[...]

    @pl.when(jnp.logical_not(first))
    def _():
        staged[...] = field[...]


def solve_kernel(high, low_hbm, arrived, staged, inverse, current, low, total, sems):
    def finish(fresh):
        current[...] = solved(staged[...] - fresh, inverse)

    product(lax.axis_index("lag") == 0, high, low_hbm, arrived, low, total, sems, finish)


def partial_kernel(high, low_hbm, arrived, staged, after, partial, low, total, sems):
    del after

    def finish(fresh):
        partial[...] = staged[...] + fresh

    product(lax.axis_index("lag") > 0, high, low_hbm, arrived, low, total, sems, finish)


def asked_kernel(table, asked, copy_of, sem):
    started((table, copy_of, sem))[0].wait()
    for q in range(table.shape[0]):
        asked[q] = jnp.maximum(copy_of[q, 0, 0], 0)


def ahead_kernel(high, arrived, field, ahead_hbm, ahead, sems):
    patches, size, columns = arrived.shape
    rows = ahead.shape[0] // sems.shape[0]
    copies = []
    for part in range(sems.shape[0]):
        here = pl.ds(part * rows, rows)
        flat = arrived[...].reshape(patches * size, columns)
        fresh = jnp.dot(high[here, :], flat, preferred_element_type=jnp.float32)
        ahead[here, :] = field[here, :] + fresh
        copies += started((ahead.at[here], ahead_hbm.at[here], sems.at[part]))
    for copy in copies:
        copy.wait()


def pack_kernel(step, keeps, early, asked, current, *refs):
    outgoing, currents, sems = refs[-3:]
    patches, size, _ = outgoing.shape
    section = lax.axis_index("lag")

    @pl.when(section < keeps if early else section >= keeps)
    def _():
        copies = []
        for q in range(patches):
            block = asked[q] if len(asked.shape) == 1 else jnp.max(jnp.maximum(asked[q], 0))
            start = pl.multiple_of(block * size, size)
            copies.append((current.at[pl.ds(start, size)], outgoing.at[q], sems.at[q]))
        copies.append((current, currents.at[step], sems.at[patches]))
        for copy in started(*copies):
            copy.wait()


def shifted(x):
    sections = lax.axis_size("lag")
    return lax.ppermute(x, "lag", [(i, i - 1) for i in range(1, sections)])


def spread(x):
    sections = lax.axis_size("lag")
    section = lax.axis_index("lag")
    received, keeps = x, 1
    while keeps < sections:
        if keeps > 1:
            x = jnp.where(section < keeps // 2, x, received)
        pairs = [(i, i + keeps) for i in range(keeps) if i + keeps < sections]
        received = lax.ppermute(x, "lag", pairs)
        keeps *= 2
    return x, received, max(keeps // 2, 1)


def body(incident, pending, self_inverse, retarded, block_rows, block_sources, owner_map):
    steps, unknowns, columns = incident.shape
    per_patch, size, _ = self_inverse.shape
    listed = retarded.shape[2]
    patches = lax.axis_size("patch")
    bf16, f32 = jnp.bfloat16, jnp.float32
    all_flops = 4 * unknowns * patches * size * columns
    solve_flops = 12 * unknowns * size * columns
    panel_bytes = 4 * unknowns * patches * size
    column = (unknowns, columns)
    arrived_bytes = 2 * patches * size * columns

    def exchange(x):
        return lax.all_to_all(x, "patch", split_axis=0, concat_axis=0, tiled=True)

    def pack(step, keeps, early, asked, current, filled, after=()):
        held = [x for x in filled if x is not None]
        aliases = {}
        for out, x in enumerate(filled):
            if x is not None:
                aliases[2 + len(after) + len(aliases)] = out
        return call(
            lambda *refs: pack_kernel(step, keeps, early, *refs),
            [(HBM, (patches, size, columns), bf16), (HBM, incident.shape, bf16)],
            [(SMEM if asked.ndim == 1 else VMEM, asked), (VMEM, current)] + [(VMEM, x) for x in after] + [(HBM, x) for x in held],
            [DMA((patches + 1,))],
            aliases=aliases,
        )

    def request(first, ins, aliases=None):
        return call(
            lambda *refs: request_kernel(per_patch, first, *refs),
            [(HBM, (patches, 1, 128), jnp.int32)],
            [(HBM, block_sources), (HBM, owner_map), *ins],
            [
                pltpu.VMEM((patches, 1, 128), jnp.int32),
                pltpu.SMEM(block_sources.shape, jnp.int32),
                pltpu.SMEM(owner_map.shape, jnp.int32),
                DMA((2,)),
            ],
            aliases=aliases,
        )

    wanted = request(True, [])
    current = call(
        first_kernel,
        [(VMEM, column, bf16)],
        [(HBM, incident), (HBM, pending[0]), (HBM, self_inverse), (HBM, wanted)],
        [
            pltpu.VMEM(column, bf16),
            pltpu.VMEM(column, f32),
            pltpu.VMEM(self_inverse.shape, f32),
            DMA((3,)),
        ],
        solve_flops,
    )
    if lax.axis_size("lag") > 1:
        wanted = request(False, [(HBM, wanted), (VMEM, current)], {2: 0})
    requests = exchange(wanted)
    asked = call(
        asked_kernel,
        [(SMEM, (patches,), jnp.int32)],
        [(VMEM, requests)],
        [pltpu.SMEM(wanted.shape, jnp.int32), DMA],
    )
    chunk = max(n for n in range(1, 9) if listed % n == 0)
    panel = (unknowns, patches * size)
    pieces = 4 if patches % 4 == 0 else 1
    low_panel = (pieces, unknowns, patches * size // pieces)
    high, low, inverse = call(
        lambda *refs: panel_kernel(per_patch, *refs),
        [(VMEM, panel, bf16), (HBM, low_panel, bf16), (VMEM, self_inverse.shape, f32)],
        [(HBM, block_rows), (HBM, block_sources), (HBM, owner_map), (HBM, retarded), (HBM, self_inverse)],
        [
            pltpu.SMEM(block_rows.shape, jnp.int32),
            pltpu.SMEM(block_sources.shape, jnp.int32),
            pltpu.SMEM(owner_map.shape, jnp.int32),
            pltpu.VMEM((3, chunk, size, size), f32),
            pltpu.VMEM(low_panel, bf16),
            DMA((7,)),
        ],
        nbytes=listed * size * size * 4 + panel_bytes,
        vmem=panel_bytes // 2,
    )

    field = pending[0]
    currents = None
    for step in range(steps):
        own, received, keeps = spread(current)
        table = asked if step else requests
        outgoing, currents = pack(step, keeps, True, table, own, (None, currents))
        if lax.axis_size("lag") > 1:
            after = [field] if step else []
            outgoing, currents = pack(step, keeps, False, table, received, (outgoing, currents), after)
        arrived = exchange(outgoing)
        field = shifted(field)
        if step + 1 < steps:
            staged = call(
                lambda *refs, n=step + 1: stage_kernel(n, *refs),
                [(VMEM, column, f32)],
                [(HBM, incident), (VMEM, field)],
                [pltpu.VMEM(column, bf16), DMA],
            )
            shared = [(VMEM, high), (HBM, low), (VMEM, arrived), (VMEM, staged)]
            scratch = [pltpu.VMEM(low_panel, bf16), pltpu.VMEM(column, f32), DMA((pieces,))]
            sizes = [all_flops, panel_bytes + arrived_bytes, panel_bytes + arrived_bytes]
            current = call(
                solve_kernel, [(VMEM, column, bf16)], [*shared, (VMEM, inverse)], scratch, *sizes
            )
            field = call(
                partial_kernel, [(VMEM, column, f32)], [*shared, (VMEM, current)], scratch, *sizes
            )
        else:
            field = call(
                ahead_kernel,
                [(HBM, column, f32)],
                [(VMEM, high), (VMEM, arrived), (VMEM, field)],
                [pltpu.VMEM(column, f32), DMA((2,))],
                all_flops,
                panel_bytes + arrived_bytes,
                panel_bytes + arrived_bytes,
            )
    return currents, field[None]


def solution(mesh):
    in_specs = (
        P(None, "patch", None),
        P("lag", "patch", None),
        P("patch", None, None),
        P("lag", "patch", None, None, None),
        P("lag", "patch", None),
        P("lag", "patch", None),
        P(),
    )
    out_specs = (P(None, "patch", None), P("lag", "patch", None))
    return jax.shard_map(body, mesh=mesh, in_specs=in_specs, out_specs=out_specs, check_vma=False)
```

```python
import jax
import jax.numpy as jnp
from jax import lax
from jax.experimental import pallas as pl
from jax.experimental.pallas import tpu as pltpu
from jax.sharding import PartitionSpec as P

VMEM, SMEM, HBM = pltpu.VMEM, pltpu.SMEM, pltpu.HBM
DMA = pltpu.SemaphoreType.DMA
MIB = 1 << 20


def call(kernel, outs, ins, scratch=(), flops=0, nbytes=0, vmem=0, aliases=None):
    out_shape = tuple(space(dims, dtype) for space, dims, dtype in outs)
    out_specs = tuple(pl.BlockSpec(memory_space=space) for space, _, _ in outs)
    run = pl.pallas_call(
        kernel,
        out_shape=out_shape,
        in_specs=[pl.BlockSpec(memory_space=space) for space, _ in ins],
        out_specs=out_specs,
        scratch_shapes=scratch,
        input_output_aliases=aliases or {},
        cost_estimate=pl.CostEstimate(flops=flops, bytes_accessed=nbytes, transcendentals=0),
        compiler_params=pltpu.CompilerParams(vmem_limit_bytes=vmem + 6 * MIB),
    )
    results = run(*(pltpu.with_memory_space_constraint(x, space) for space, x in ins))
    return results if len(outs) > 1 else results[0]


def started(*copies):
    copies = [pltpu.make_async_copy(*copy) for copy in copies]
    for copy in copies:
        copy.start()
    return copies


def requests_into(wanted, per_patch, sources, owner_map):
    patches, _, lanes = wanted.shape
    patch = lax.broadcasted_iota(jnp.int32, (patches, lanes), 0)

    def entry(j, table):
        source = sources[0, 0, j]
        storage = owner_map[jnp.maximum(source, 0)]
        here = (patch == storage // per_patch) & (source >= 0)
        return jnp.where(here, storage % per_patch, table)

    table = lax.fori_loop(
        0, sources.shape[2], entry, jnp.full((patches, lanes), -1, jnp.int32), unroll=8
    )
    for q in range(patches):
        wanted[q] = table[q : q + 1]


def first_kernel(
    per_patch,
    sources_hbm,
    owner_hbm,
    incident_hbm,
    field_hbm,
    inverse_hbm,
    wanted_hbm,
    current,
    wanted,
    sources,
    owner_map,
    incident,
    field,
    inverse,
    sems,
):
    @pl.when(lax.axis_index("lag") == 0)
    def _():
        lists = started(
            (sources_hbm, sources, sems.at[0]),
            (owner_hbm, owner_map, sems.at[1]),
        )
        arrays = started(
            (incident_hbm.at[0], incident, sems.at[2]),
            (inverse_hbm, inverse, sems.at[3]),
            (field_hbm, field, sems.at[4]),
        )
        for copy in lists:
            copy.wait()
        requests_into(wanted, per_patch, sources, owner_map)
        (done,) = started((wanted, wanted_hbm, sems.at[0]))
        for copy in arrays:
            copy.wait()
        current[...] = solved(incident[...].astype(jnp.float32) - field[...], inverse)
        done.wait()


def request_kernel(
    per_patch, sources_hbm, owner_hbm, held, after, wanted_hbm, wanted, sources, owner_map, sems
):
    del held, after

    @pl.when(lax.axis_index("lag") > 0)
    def _():
        lists = started(
            (sources_hbm, sources, sems.at[0]),
            (owner_hbm, owner_map, sems.at[1]),
        )
        for copy in lists:
            copy.wait()
        requests_into(wanted, per_patch, sources, owner_map)
        started((wanted, wanted_hbm, sems.at[0]))[0].wait()


def panel_kernel(
    per_patch,
    rows_hbm,
    sources_hbm,
    owner_hbm,
    retarded,
    inverse_hbm,
    high,
    low_hbm,
    inverse,
    rows,
    sources,
    owner_map,
    parts,
    low,
    sems,
):
    size = retarded.shape[-1]
    slots, chunk = parts.shape[:2]
    chunks = retarded.shape[2] // chunk

    def fetch(c):
        part = retarded.at[0, 0, pl.ds(c * chunk, chunk)]
        return pltpu.make_async_copy(part, parts.at[c % slots], sems.at[c % slots])

    lists = started(
        (rows_hbm, rows, sems.at[slots]),
        (sources_hbm, sources, sems.at[slots + 1]),
        (owner_hbm, owner_map, sems.at[slots + 2]),
        (inverse_hbm, inverse, sems.at[slots + 3]),
    )
    for c in range(min(slots, chunks)):
        fetch(c).start()
    high[...] = jnp.zeros_like(high)
    low[...] = jnp.zeros_like(low)
    for copy in lists:
        copy.wait()

    def entry(c, k, carry):
        source = sources[0, 0, c * chunk + k]

        @pl.when(source >= 0)
        def _():
            owner = owner_map[source] // per_patch
            row = pl.multiple_of(rows[0, 0, c * chunk + k] * size, size)
            column = pl.multiple_of(owner * size, size)
            block = parts[c % slots, k]
            rounded = block.astype(high.dtype)
            rest = (block - rounded.astype(jnp.float32)).astype(low.dtype)
            high[pl.ds(row, size), pl.ds(column, size)] = rounded
            piece = column // low.shape[2]
            inside = pl.multiple_of(column - piece * low.shape[2], size)
            low[piece, pl.ds(row, size), pl.ds(inside, size)] = rest

        return carry

    for c in range(chunks):
        fetch(c).wait()
        lax.fori_loop(0, chunk, lambda k, carry, c=c: entry(c, k, carry), 0)
        if c + slots < chunks:
            fetch(c + slots).start()
    started((low, low_hbm, sems.at[0]))[0].wait()


def solved(excess, self_inverse):
    blocks, size, _ = self_inverse.shape
    parts = [
        jnp.dot(
            self_inverse[k],
            excess[k * size : (k + 1) * size],
            precision=lax.Precision.HIGHEST,
            preferred_element_type=jnp.float32,
        )
        for k in range(blocks)
    ]
    return jnp.concatenate(parts, axis=0).astype(jnp.bfloat16)


def product(here, high, low_hbm, arrived, low, total, sems, finish):
    patches, size, columns = arrived.shape
    pieces, _, depth = low.shape
    copies = [pltpu.make_async_copy(low_hbm.at[k], low.at[k], sems.at[k]) for k in range(pieces)]

    @pl.when(here)
    def _():
        for copy in copies:
            copy.start()
        rows = total.shape[0] // 2

        def half(part, carry):
            flat = arrived[...].reshape(patches * size, columns)
            mine = pl.ds(pl.multiple_of(part * rows, rows), rows)
            total[mine, :] = jnp.dot(high[mine, :], flat, preferred_element_type=jnp.float32)
            return carry

        lax.fori_loop(0, 2, half, 0)
        fresh = total[...]
        flat = arrived[...].reshape(patches * size, columns)
        for k, copy in enumerate(copies):
            copy.wait()
            part = flat[k * depth : (k + 1) * depth]
            fresh = fresh + jnp.dot(low[k], part, preferred_element_type=jnp.float32)
        finish(fresh)


def stage_kernel(step, incident_hbm, field, staged, incident, sem):
    first = lax.axis_index("lag") == 0

    @pl.when(first)
    def _():
        started((incident_hbm.at[step], incident, sem))[0].wait()
        staged[...] = incident[...].astype(jnp.float32) - field[...]

    @pl.when(jnp.logical_not(first))
    def _():
        staged[...] = field[...]


def solve_kernel(high, low_hbm, arrived, staged, inverse, current, low, total, sems):
    def finish(fresh):
        current[...] = solved(staged[...] - fresh, inverse)

    product(lax.axis_index("lag") == 0, high, low_hbm, arrived, low, total, sems, finish)


def partial_kernel(high, low_hbm, arrived, staged, after, partial, low, total, sems):
    del after

    def finish(fresh):
        partial[...] = staged[...] + fresh

    product(lax.axis_index("lag") > 0, high, low_hbm, arrived, low, total, sems, finish)


def asked_kernel(table, asked, copy_of, sem):
    started((table, copy_of, sem))[0].wait()
    for q in range(table.shape[0]):
        asked[q] = jnp.maximum(copy_of[q, 0, 0], 0)


def ahead_kernel(high, arrived, field, ahead_hbm, ahead, sems):
    patches, size, columns = arrived.shape
    rows = ahead.shape[0] // sems.shape[0]
    copies = []
    for part in range(sems.shape[0]):
        here = pl.ds(part * rows, rows)
        flat = arrived[...].reshape(patches * size, columns)
        fresh = jnp.dot(high[here, :], flat, preferred_element_type=jnp.float32)
        ahead[here, :] = field[here, :] + fresh
        copies += started((ahead.at[here], ahead_hbm.at[here], sems.at[part]))
    for copy in copies:
        copy.wait()


def pack_kernel(step, keeps, early, asked, current, *refs):
    outgoing, currents, sems = refs[-3:]
    patches, size, _ = outgoing.shape
    section = lax.axis_index("lag")

    @pl.when(section < keeps if early else section >= keeps)
    def _():
        copies = []
        for q in range(patches):
            block = asked[q] if len(asked.shape) == 1 else jnp.max(jnp.maximum(asked[q], 0))
            start = pl.multiple_of(block * size, size)
            copies.append((current.at[pl.ds(start, size)], outgoing.at[q], sems.at[q]))
        copies.append((current, currents.at[step], sems.at[patches]))
        for copy in started(*copies):
            copy.wait()


def shifted(x):
    sections = lax.axis_size("lag")
    return lax.ppermute(x, "lag", [(i, i - 1) for i in range(1, sections)])


def spread(x):
    sections = lax.axis_size("lag")
    section = lax.axis_index("lag")
    received, keeps = x, 1
    while keeps < sections:
        if keeps > 1:
            x = jnp.where(section < keeps // 2, x, received)
        pairs = [(i, i + keeps) for i in range(keeps) if i + keeps < sections]
        received = lax.ppermute(x, "lag", pairs)
        keeps *= 2
    return x, received, max(keeps // 2, 1)


def body(incident, pending, self_inverse, retarded, block_rows, block_sources, owner_map):
    steps, unknowns, columns = incident.shape
    per_patch, size, _ = self_inverse.shape
    listed = retarded.shape[2]
    patches = lax.axis_size("patch")
    bf16, f32 = jnp.bfloat16, jnp.float32
    all_flops = 4 * unknowns * patches * size * columns
    solve_flops = 12 * unknowns * size * columns
    panel_bytes = 4 * unknowns * patches * size
    column = (unknowns, columns)
    arrived_bytes = 2 * patches * size * columns

    def exchange(x):
        return lax.all_to_all(x, "patch", split_axis=0, concat_axis=0, tiled=True)

    def pack(step, keeps, early, asked, current, filled, after=()):
        held = [x for x in filled if x is not None]
        aliases = {}
        for out, x in enumerate(filled):
            if x is not None:
                aliases[2 + len(after) + len(aliases)] = out
        return call(
            lambda *refs: pack_kernel(step, keeps, early, *refs),
            [(HBM, (patches, size, columns), bf16), (HBM, incident.shape, bf16)],
            [(SMEM if asked.ndim == 1 else VMEM, asked), (VMEM, current)] + [(VMEM, x) for x in after] + [(HBM, x) for x in held],
            [DMA((patches + 1,))],
            aliases=aliases,
        )

    table = [(HBM, (patches, 1, 128), jnp.int32)]
    lists = [(HBM, block_sources), (HBM, owner_map)]
    list_scratch = [
        pltpu.VMEM((patches, 1, 128), jnp.int32),
        pltpu.SMEM(block_sources.shape, jnp.int32),
        pltpu.SMEM(owner_map.shape, jnp.int32),
    ]
    wanted, current = call(
        lambda *refs: first_kernel(per_patch, *refs),
        [*table, (VMEM, column, bf16)],
        [*lists, (HBM, incident), (HBM, pending[0]), (HBM, self_inverse)],
        [
            *list_scratch,
            pltpu.VMEM(column, bf16),
            pltpu.VMEM(column, f32),
            pltpu.VMEM(self_inverse.shape, f32),
            DMA((5,)),
        ],
        solve_flops,
    )
    if lax.axis_size("lag") > 1:
        wanted = call(
            lambda *refs: request_kernel(per_patch, *refs),
            table,
            [*lists, (HBM, wanted), (VMEM, current)],
            [*list_scratch, DMA((2,))],
            aliases={2: 0},
        )
    requests = exchange(wanted)
    asked = call(
        asked_kernel,
        [(SMEM, (patches,), jnp.int32)],
        [(VMEM, requests)],
        [pltpu.SMEM(wanted.shape, jnp.int32), DMA],
    )
    chunk = max(n for n in range(1, 9) if listed % n == 0)
    panel = (unknowns, patches * size)
    pieces = 4 if patches % 4 == 0 else 1
    low_panel = (pieces, unknowns, patches * size // pieces)
    high, low, inverse = call(
        lambda *refs: panel_kernel(per_patch, *refs),
        [(VMEM, panel, bf16), (HBM, low_panel, bf16), (VMEM, self_inverse.shape, f32)],
        [(HBM, block_rows), (HBM, block_sources), (HBM, owner_map), (HBM, retarded), (HBM, self_inverse)],
        [
            pltpu.SMEM(block_rows.shape, jnp.int32),
            pltpu.SMEM(block_sources.shape, jnp.int32),
            pltpu.SMEM(owner_map.shape, jnp.int32),
            pltpu.VMEM((3, chunk, size, size), f32),
            pltpu.VMEM(low_panel, bf16),
            DMA((7,)),
        ],
        nbytes=listed * size * size * 4 + panel_bytes,
        vmem=panel_bytes // 2,
    )

    field = pending[0]
    currents = None
    for step in range(steps):
        own, received, keeps = spread(current)
        table = asked if step else requests
        outgoing, currents = pack(step, keeps, True, table, own, (None, currents))
        if lax.axis_size("lag") > 1:
            after = [field] if step else []
            outgoing, currents = pack(step, keeps, False, table, received, (outgoing, currents), after)
        arrived = exchange(outgoing)
        field = shifted(field)
        if step + 1 < steps:
            staged = call(
                lambda *refs, n=step + 1: stage_kernel(n, *refs),
                [(VMEM, column, f32)],
                [(HBM, incident), (VMEM, field)],
                [pltpu.VMEM(column, bf16), DMA],
            )
            shared = [(VMEM, high), (HBM, low), (VMEM, arrived), (VMEM, staged)]
            scratch = [pltpu.VMEM(low_panel, bf16), pltpu.VMEM(column, f32), DMA((pieces,))]
            sizes = [all_flops, panel_bytes + arrived_bytes, panel_bytes + arrived_bytes]
            current = call(
                solve_kernel, [(VMEM, column, bf16)], [*shared, (VMEM, inverse)], scratch, *sizes
            )
            field = call(
                partial_kernel, [(VMEM, column, f32)], [*shared, (VMEM, current)], scratch, *sizes
            )
        else:
            field = call(
                ahead_kernel,
                [(HBM, column, f32)],
                [(VMEM, high), (VMEM, arrived), (VMEM, field)],
                [pltpu.VMEM(column, f32), DMA((2,))],
                all_flops,
                panel_bytes + arrived_bytes,
                panel_bytes + arrived_bytes,
            )
    return currents, field[None]


def solution(mesh):
    in_specs = (
        P(None, "patch", None),
        P("lag", "patch", None),
        P("patch", None, None),
        P("lag", "patch", None, None, None),
        P("lag", "patch", None),
        P("lag", "patch", None),
        P(),
    )
    out_specs = (P(None, "patch", None), P("lag", "patch", None))
    return jax.shard_map(body, mesh=mesh, in_specs=in_specs, out_specs=out_specs, check_vma=False)
```

```python
import jax
import jax.numpy as jnp
from jax import lax
from jax.experimental import pallas as pl
from jax.experimental.pallas import tpu as pltpu
from jax.sharding import PartitionSpec as P

VMEM, SMEM, HBM = pltpu.VMEM, pltpu.SMEM, pltpu.HBM
DMA = pltpu.SemaphoreType.DMA
MIB = 1 << 20


def call(kernel, outs, ins, scratch=(), flops=0, nbytes=0, vmem=0, aliases=None):
    out_shape = tuple(space(dims, dtype) for space, dims, dtype in outs)
    out_specs = tuple(pl.BlockSpec(memory_space=space) for space, _, _ in outs)
    run = pl.pallas_call(
        kernel,
        out_shape=out_shape,
        in_specs=[pl.BlockSpec(memory_space=space) for space, _ in ins],
        out_specs=out_specs,
        scratch_shapes=scratch,
        input_output_aliases=aliases or {},
        cost_estimate=pl.CostEstimate(flops=flops, bytes_accessed=nbytes, transcendentals=0),
        compiler_params=pltpu.CompilerParams(vmem_limit_bytes=vmem + 6 * MIB),
    )
    results = run(*(pltpu.with_memory_space_constraint(x, space) for space, x in ins))
    return results if len(outs) > 1 else results[0]


def started(*copies):
    copies = [pltpu.make_async_copy(*copy) for copy in copies]
    for copy in copies:
        copy.start()
    return copies


def requests_into(wanted, per_patch, sources, owner_map):
    patches, _, lanes = wanted.shape
    patch = lax.broadcasted_iota(jnp.int32, (patches, lanes), 0)

    def entry(j, table):
        source = sources[0, 0, j]
        storage = owner_map[jnp.maximum(source, 0)]
        here = (patch == storage // per_patch) & (source >= 0)
        return jnp.where(here, storage % per_patch, table)

    table = lax.fori_loop(
        0, sources.shape[2], entry, jnp.full((patches, lanes), -1, jnp.int32), unroll=8
    )
    for q in range(patches):
        wanted[q] = table[q : q + 1]


def first_kernel(
    per_patch,
    sources_hbm,
    owner_hbm,
    incident_hbm,
    field_hbm,
    inverse_hbm,
    wanted_hbm,
    current,
    wanted,
    sources,
    owner_map,
    incident,
    field,
    inverse,
    sems,
):
    @pl.when(lax.axis_index("lag") == 0)
    def _():
        lists = started(
            (sources_hbm, sources, sems.at[0]),
            (owner_hbm, owner_map, sems.at[1]),
        )
        arrays = started(
            (incident_hbm.at[0], incident, sems.at[2]),
            (inverse_hbm, inverse, sems.at[3]),
            (field_hbm, field, sems.at[4]),
        )
        for copy in lists:
            copy.wait()
        requests_into(wanted, per_patch, sources, owner_map)
        (done,) = started((wanted, wanted_hbm, sems.at[0]))
        for copy in arrays:
            copy.wait()
        current[...] = solved(incident[...].astype(jnp.float32) - field[...], inverse)
        done.wait()


def request_kernel(
    per_patch, sources_hbm, owner_hbm, held, after, wanted_hbm, wanted, sources, owner_map, sems
):
    del held, after

    @pl.when(lax.axis_index("lag") > 0)
    def _():
        lists = started(
            (sources_hbm, sources, sems.at[0]),
            (owner_hbm, owner_map, sems.at[1]),
        )
        for copy in lists:
            copy.wait()
        requests_into(wanted, per_patch, sources, owner_map)
        started((wanted, wanted_hbm, sems.at[0]))[0].wait()


def panel_kernel(
    per_patch,
    rows_hbm,
    sources_hbm,
    owner_hbm,
    retarded,
    inverse_hbm,
    high,
    low_hbm,
    inverse,
    rows,
    sources,
    owner_map,
    parts,
    low,
    sems,
):
    size = retarded.shape[-1]
    slots, chunk = parts.shape[:2]
    chunks = retarded.shape[2] // chunk

    def fetch(c):
        part = retarded.at[0, 0, pl.ds(c * chunk, chunk)]
        return pltpu.make_async_copy(part, parts.at[c % slots], sems.at[c % slots])

    lists = started(
        (rows_hbm, rows, sems.at[slots]),
        (sources_hbm, sources, sems.at[slots + 1]),
        (owner_hbm, owner_map, sems.at[slots + 2]),
        (inverse_hbm, inverse, sems.at[slots + 3]),
    )
    for c in range(min(slots, chunks)):
        fetch(c).start()
    high[...] = jnp.zeros_like(high)
    low[...] = jnp.zeros_like(low)
    for copy in lists:
        copy.wait()

    def entry(c, k, carry):
        source = sources[0, 0, c * chunk + k]

        @pl.when(source >= 0)
        def _():
            owner = owner_map[source] // per_patch
            row = pl.multiple_of(rows[0, 0, c * chunk + k] * size, size)
            column = pl.multiple_of(owner * size, size)
            block = parts[c % slots, k]
            rounded = block.astype(high.dtype)
            rest = (block - rounded.astype(jnp.float32)).astype(low.dtype)
            high[pl.ds(row, size), pl.ds(column, size)] = rounded
            piece = column // low.shape[2]
            inside = pl.multiple_of(column - piece * low.shape[2], size)
            low[piece, pl.ds(row, size), pl.ds(inside, size)] = rest

        return carry

    for c in range(chunks):
        fetch(c).wait()
        lax.fori_loop(0, chunk, lambda k, carry, c=c: entry(c, k, carry), 0)
        if c + slots < chunks:
            fetch(c + slots).start()
    started((low, low_hbm, sems.at[0]))[0].wait()


def solved(excess, self_inverse):
    blocks, size, _ = self_inverse.shape
    parts = [
        jnp.dot(
            self_inverse[k],
            excess[k * size : (k + 1) * size],
            precision=lax.Precision.HIGHEST,
            preferred_element_type=jnp.float32,
        )
        for k in range(blocks)
    ]
    return jnp.concatenate(parts, axis=0).astype(jnp.bfloat16)


def product(here, high, low_hbm, arrived, low, total, sems, early, finish):
    patches, size, columns = arrived.shape
    pieces, _, depth = low.shape
    copies = [pltpu.make_async_copy(low_hbm.at[k], low.at[k], sems.at[k]) for k in range(pieces)]

    @pl.when(here)
    def _():
        for copy in copies:
            copy.start()
        rows = total.shape[0] // 2

        def half(part, carry):
            flat = arrived[...].reshape(patches * size, columns)
            mine = pl.ds(pl.multiple_of(part * rows, rows), rows)
            total[mine, :] = jnp.dot(high[mine, :], flat, preferred_element_type=jnp.float32)
            return carry

        lax.fori_loop(0, 2, half, 0)
        early()
        flat = arrived[...].reshape(patches * size, columns)
        rest = jnp.zeros(total.shape, jnp.float32)
        for k, copy in enumerate(copies):
            copy.wait()
            part = flat[k * depth : (k + 1) * depth]
            rest = rest + jnp.dot(low[k], part, preferred_element_type=jnp.float32)
        finish(rest)


def stage_kernel(step, keeps, incident_hbm, field, own, received, held, staged, currents, incident, sems):
    del held
    section = lax.axis_index("lag")

    @pl.when(section == 0)
    def _():
        started((incident_hbm.at[step], incident, sems.at[0]))[0].wait()
        staged[...] = incident[...].astype(jnp.float32) - field[...]

    @pl.when(section > 0)
    def _():
        staged[...] = field[...]

    keep(step - 1, keeps, own, received, currents, sems.at[1])


def keep(step, keeps, own, received, currents, sem):
    mine = lax.axis_index("lag") < keeps

    @pl.when(mine)
    def _():
        started((own, currents.at[step], sem))[0].wait()

    @pl.when(jnp.logical_not(mine))
    def _():
        started((received, currents.at[step], sem))[0].wait()


def solve_kernel(high, low_hbm, arrived, staged, inverse, current, low, total, sems):
    blocks, size, _ = inverse.shape

    def early():
        def one(k, carry):
            mine = pl.ds(pl.multiple_of(k * size, size), size)
            total[mine, :] = jnp.dot(
                inverse[k],
                staged[mine, :] - total[mine, :],
                precision=lax.Precision.HIGHEST,
                preferred_element_type=jnp.float32,
            )
            return carry

        lax.fori_loop(0, blocks, one, 0)

    def finish(rest):
        rest = rest.astype(jnp.bfloat16)
        for k in range(blocks):
            mine = slice(k * size, (k + 1) * size)
            less = jnp.dot(
                inverse[k].astype(jnp.bfloat16), rest[mine], preferred_element_type=jnp.float32
            )
            current[mine, :] = (total[mine, :] - less).astype(jnp.bfloat16)

    product(lax.axis_index("lag") == 0, high, low_hbm, arrived, low, total, sems, early, finish)


def partial_kernel(high, low_hbm, arrived, staged, after, partial, low, total, sems):
    del after

    def finish(rest):
        partial[...] = staged[...] + total[...] + rest

    product(
        lax.axis_index("lag") > 0, high, low_hbm, arrived, low, total, sems, lambda: None, finish
    )


def asked_kernel(table, asked, copy_of, sem):
    started((table, copy_of, sem))[0].wait()
    for q in range(table.shape[0]):
        asked[q] = jnp.maximum(copy_of[q, 0, 0], 0)


def ahead_kernel(step, keeps, high, arrived, field, own, received, held, ahead_hbm, currents, ahead, sems):
    del held
    patches, size, columns = arrived.shape
    parts = sems.shape[0] - 1
    rows = ahead.shape[0] // parts
    copies = []
    for part in range(parts):
        here = pl.ds(part * rows, rows)
        flat = arrived[...].reshape(patches * size, columns)
        fresh = jnp.dot(high[here, :], flat, preferred_element_type=jnp.float32)
        ahead[here, :] = field[here, :] + fresh
        copies += started((ahead.at[here], ahead_hbm.at[here], sems.at[part]))
    keep(step, keeps, own, received, currents, sems.at[parts])
    for copy in copies:
        copy.wait()


def pack(asked, current, outgoing, sems):
    patches, size, _ = outgoing.shape
    copies = []
    for q in range(patches):
        block = asked[q] if len(asked.shape) == 1 else jnp.max(jnp.maximum(asked[q], 0))
        start = pl.multiple_of(block * size, size)
        copies.append((current.at[pl.ds(start, size)], outgoing.at[q], sems.at[q]))
    for copy in started(*copies):
        copy.wait()


def own_pack_kernel(keeps, asked, current, outgoing, sems):
    pl.when(lax.axis_index("lag") < keeps)(lambda: pack(asked, current, outgoing, sems))


def rest_pack_kernel(keeps, asked, current, *refs):
    pl.when(lax.axis_index("lag") >= keeps)(lambda: pack(asked, current, *refs[-2:]))


def first_pack_kernel(keeps, asked, own, received, outgoing, sems):
    mine = lax.axis_index("lag") < keeps
    pl.when(mine)(lambda: pack(asked, own, outgoing, sems))
    pl.when(jnp.logical_not(mine))(lambda: pack(asked, received, outgoing, sems))


def shifted(x):
    sections = lax.axis_size("lag")
    return lax.ppermute(x, "lag", [(i, i - 1) for i in range(1, sections)])


def spread(x):
    sections = lax.axis_size("lag")
    section = lax.axis_index("lag")
    received, keeps = x, 1
    while keeps < sections:
        if keeps > 1:
            x = jnp.where(section < keeps // 2, x, received)
        pairs = [(i, i + keeps) for i in range(keeps) if i + keeps < sections]
        received = lax.ppermute(x, "lag", pairs)
        keeps *= 2
    return x, received, max(keeps // 2, 1)


def body(incident, pending, self_inverse, retarded, block_rows, block_sources, owner_map):
    steps, unknowns, columns = incident.shape
    per_patch, size, _ = self_inverse.shape
    listed = retarded.shape[2]
    patches = lax.axis_size("patch")
    bf16, f32 = jnp.bfloat16, jnp.float32
    all_flops = 4 * unknowns * patches * size * columns
    solve_flops = 12 * unknowns * size * columns
    panel_bytes = 4 * unknowns * patches * size
    column = (unknowns, columns)
    arrived_bytes = 2 * patches * size * columns

    def exchange(x):
        return lax.all_to_all(x, "patch", split_axis=0, concat_axis=0, tiled=True)

    table = [(HBM, (patches, 1, 128), jnp.int32)]
    lists = [(HBM, block_sources), (HBM, owner_map)]
    list_scratch = [
        pltpu.VMEM((patches, 1, 128), jnp.int32),
        pltpu.SMEM(block_sources.shape, jnp.int32),
        pltpu.SMEM(owner_map.shape, jnp.int32),
    ]
    wanted, current = call(
        lambda *refs: first_kernel(per_patch, *refs),
        [*table, (VMEM, column, bf16)],
        [*lists, (HBM, incident), (HBM, pending[0]), (HBM, self_inverse)],
        [
            *list_scratch,
            pltpu.VMEM(column, bf16),
            pltpu.VMEM(column, f32),
            pltpu.VMEM(self_inverse.shape, f32),
            DMA((5,)),
        ],
        solve_flops,
    )
    if lax.axis_size("lag") > 1:
        wanted = call(
            lambda *refs: request_kernel(per_patch, *refs),
            table,
            [*lists, (HBM, wanted), (VMEM, current)],
            [*list_scratch, DMA((2,))],
            aliases={2: 0},
        )
    requests = exchange(wanted)
    asked = call(
        asked_kernel,
        [(SMEM, (patches,), jnp.int32)],
        [(VMEM, requests)],
        [pltpu.SMEM(wanted.shape, jnp.int32), DMA],
    )
    chunk = max(n for n in range(1, 9) if listed % n == 0)
    panel = (unknowns, patches * size)
    pieces = 4 if patches % 4 == 0 else 1
    low_panel = (pieces, unknowns, patches * size // pieces)
    high, low, inverse = call(
        lambda *refs: panel_kernel(per_patch, *refs),
        [(VMEM, panel, bf16), (HBM, low_panel, bf16), (VMEM, self_inverse.shape, f32)],
        [(HBM, block_rows), (HBM, block_sources), (HBM, owner_map), (HBM, retarded), (HBM, self_inverse)],
        [
            pltpu.SMEM(block_rows.shape, jnp.int32),
            pltpu.SMEM(block_sources.shape, jnp.int32),
            pltpu.SMEM(owner_map.shape, jnp.int32),
            pltpu.VMEM((3, chunk, size, size), f32),
            pltpu.VMEM(low_panel, bf16),
            DMA((7,)),
        ],
        nbytes=listed * size * size * 4 + panel_bytes,
        vmem=panel_bytes // 2,
    )

    outgoing_like = [(HBM, (patches, size, columns), bf16)]
    currents_like = (HBM, incident.shape, bf16)
    pack_scratch = [DMA((patches,))]

    field = pending[0]
    held = []
    for step in range(steps):
        own, received, keeps = spread(current)
        pair = [(VMEM, own), (VMEM, received)]
        if step == 0:
            outgoing = call(
                lambda *refs: first_pack_kernel(keeps, *refs),
                outgoing_like,
                [(VMEM, requests), *pair],
                pack_scratch,
            )
        else:
            outgoing = call(
                lambda *refs: own_pack_kernel(keeps, *refs),
                outgoing_like,
                [(SMEM, asked), (VMEM, own)],
                pack_scratch,
            )
            if lax.axis_size("lag") > 1:
                outgoing = call(
                    lambda *refs: rest_pack_kernel(keeps, *refs),
                    outgoing_like,
                    [(SMEM, asked), (VMEM, received), (VMEM, field), (HBM, outgoing)],
                    pack_scratch,
                    aliases={3: 0},
                )
        arrived = exchange(outgoing)
        field = shifted(field)
        if step + 1 < steps:
            ins = [(HBM, incident), (VMEM, field), *pair, *(held or [(HBM, incident)])]
            staged, currents = call(
                lambda *refs, n=step + 1: stage_kernel(n, keeps, *refs),
                [(VMEM, column, f32), currents_like],
                ins,
                [pltpu.VMEM(column, bf16), DMA((2,))],
                aliases={len(ins) - 1: 1} if held else None,
            )
            held = [(HBM, currents)]
            shared = [(VMEM, high), (HBM, low), (VMEM, arrived), (VMEM, staged)]
            scratch = [pltpu.VMEM(low_panel, bf16), pltpu.VMEM(column, f32), DMA((pieces,))]
            sizes = [all_flops, panel_bytes + arrived_bytes, panel_bytes + arrived_bytes]
            current = call(
                solve_kernel, [(VMEM, column, bf16)], [*shared, (VMEM, inverse)], scratch, *sizes
            )
            field = call(
                partial_kernel, [(VMEM, column, f32)], [*shared, (VMEM, current)], scratch, *sizes
            )
        else:
            ins = [(VMEM, high), (VMEM, arrived), (VMEM, field), *pair, *(held or [(HBM, incident)])]
            field, currents = call(
                lambda *refs, n=step: ahead_kernel(n, keeps, *refs),
                [(HBM, column, f32), currents_like],
                ins,
                [pltpu.VMEM(column, f32), DMA((3,))],
                all_flops,
                panel_bytes + arrived_bytes,
                panel_bytes + arrived_bytes,
                aliases={len(ins) - 1: 1} if held else None,
            )
    return currents, field[None]


def solution(mesh):
    in_specs = (
        P(None, "patch", None),
        P("lag", "patch", None),
        P("patch", None, None),
        P("lag", "patch", None, None, None),
        P("lag", "patch", None),
        P("lag", "patch", None),
        P(),
    )
    out_specs = (P(None, "patch", None), P("lag", "patch", None))
    return jax.shard_map(body, mesh=mesh, in_specs=in_specs, out_specs=out_specs, check_vma=False)
```

```python
import jax
import jax.numpy as jnp
from jax import lax
from jax.experimental import pallas as pl
from jax.experimental.pallas import tpu as pltpu
from jax.sharding import PartitionSpec as P

VMEM, SMEM, HBM = pltpu.VMEM, pltpu.SMEM, pltpu.HBM
DMA = pltpu.SemaphoreType.DMA
MIB = 1 << 20


def call(kernel, outs, ins, scratch=(), flops=0, nbytes=0, vmem=0, aliases=None):
    out_shape = tuple(space(dims, dtype) for space, dims, dtype in outs)
    out_specs = tuple(pl.BlockSpec(memory_space=space) for space, _, _ in outs)
    run = pl.pallas_call(
        kernel,
        out_shape=out_shape,
        in_specs=[pl.BlockSpec(memory_space=space) for space, _ in ins],
        out_specs=out_specs,
        scratch_shapes=scratch,
        input_output_aliases=aliases or {},
        cost_estimate=pl.CostEstimate(flops=flops, bytes_accessed=nbytes, transcendentals=0),
        compiler_params=pltpu.CompilerParams(vmem_limit_bytes=vmem + 6 * MIB),
    )
    results = run(*(pltpu.with_memory_space_constraint(x, space) for space, x in ins))
    return results if len(outs) > 1 else results[0]


def started(*copies):
    copies = [pltpu.make_async_copy(*copy) for copy in copies]
    for copy in copies:
        copy.start()
    return copies


def requests_into(wanted, per_patch, sources, owner_map):
    patches, _, lanes = wanted.shape
    blocks = owner_map.shape[1]

    def numbered(dims, axis):
        return lax.broadcasted_iota(jnp.int32, dims, axis)

    source = sources[...]
    square = (blocks, blocks)
    on_diagonal = numbered(square, 0) == numbered(square, 1)
    owners = jnp.max(jnp.where(on_diagonal, owner_map[...], 0), axis=1, keepdims=True)
    looked_up = numbered((blocks, source.shape[1]), 0) == source
    storage = jnp.max(jnp.where(looked_up, owners, -1), axis=0, keepdims=True)
    patch = numbered((patches, source.shape[1]), 0)
    here = (storage >= patch * per_patch) & (storage < (patch + 1) * per_patch)
    table = jnp.max(jnp.where(here, storage - patch * per_patch, -1), axis=1, keepdims=True)
    for q in range(patches):
        wanted[q] = jnp.broadcast_to(table[q : q + 1], (1, lanes))


def first_kernel(
    per_patch,
    sources_hbm,
    owner_hbm,
    incident_hbm,
    field_hbm,
    inverse_hbm,
    wanted_hbm,
    current,
    wanted,
    sources,
    owner_map,
    incident,
    field,
    inverse,
    sems,
):
    @pl.when(lax.axis_index("lag") == 0)
    def _():
        lists = started(
            (sources_hbm, sources, sems.at[0]),
            (owner_hbm, owner_map, sems.at[1]),
        )
        arrays = started(
            (incident_hbm.at[0], incident, sems.at[2]),
            (inverse_hbm, inverse, sems.at[3]),
            (field_hbm, field, sems.at[4]),
        )
        for copy in lists:
            copy.wait()
        requests_into(wanted, per_patch, sources, owner_map)
        (done,) = started((wanted, wanted_hbm, sems.at[0]))
        for copy in arrays:
            copy.wait()
        current[...] = solved(incident[...].astype(jnp.float32) - field[...], inverse)
        done.wait()


def request_kernel(
    per_patch, sources_hbm, owner_hbm, held, after, wanted_hbm, wanted, sources, owner_map, sems
):
    del held, after

    @pl.when(lax.axis_index("lag") > 0)
    def _():
        lists = started(
            (sources_hbm, sources, sems.at[0]),
            (owner_hbm, owner_map, sems.at[1]),
        )
        for copy in lists:
            copy.wait()
        requests_into(wanted, per_patch, sources, owner_map)
        started((wanted, wanted_hbm, sems.at[0]))[0].wait()


def panel_kernel(
    per_patch,
    rows_hbm,
    sources_hbm,
    owner_hbm,
    retarded,
    inverse_hbm,
    high,
    low_hbm,
    inverse,
    rows,
    sources,
    owner_map,
    parts,
    low,
    sems,
):
    size = retarded.shape[-1]
    slots, chunk = parts.shape[:2]
    chunks = retarded.shape[2] // chunk

    def fetch(c):
        part = retarded.at[0, 0, pl.ds(c * chunk, chunk)]
        return pltpu.make_async_copy(part, parts.at[c % slots], sems.at[c % slots])

    lists = started(
        (rows_hbm, rows, sems.at[slots]),
        (sources_hbm, sources, sems.at[slots + 1]),
        (owner_hbm, owner_map, sems.at[slots + 2]),
        (inverse_hbm, inverse, sems.at[slots + 3]),
    )
    for c in range(min(slots, chunks)):
        fetch(c).start()
    high[...] = jnp.zeros_like(high)
    low[...] = jnp.zeros_like(low)
    for copy in lists:
        copy.wait()

    def entry(c, k, carry):
        source = sources[0, 0, c * chunk + k]

        @pl.when(source >= 0)
        def _():
            owner = owner_map[source] // per_patch
            row = pl.multiple_of(rows[0, 0, c * chunk + k] * size, size)
            column = pl.multiple_of(owner * size, size)
            block = parts[c % slots, k]
            rounded = block.astype(high.dtype)
            rest = (block - rounded.astype(jnp.float32)).astype(low.dtype)
            high[pl.ds(row, size), pl.ds(column, size)] = rounded
            piece = column // low.shape[2]
            inside = pl.multiple_of(column - piece * low.shape[2], size)
            low[piece, pl.ds(row, size), pl.ds(inside, size)] = rest

        return carry

    for c in range(chunks):
        fetch(c).wait()
        lax.fori_loop(0, chunk, lambda k, carry, c=c: entry(c, k, carry), 0)
        if c + slots < chunks:
            fetch(c + slots).start()
    started((low, low_hbm, sems.at[0]))[0].wait()


def solved(excess, self_inverse):
    blocks, size, _ = self_inverse.shape
    parts = [
        jnp.dot(
            self_inverse[k],
            excess[k * size : (k + 1) * size],
            precision=lax.Precision.HIGHEST,
            preferred_element_type=jnp.float32,
        )
        for k in range(blocks)
    ]
    return jnp.concatenate(parts, axis=0).astype(jnp.bfloat16)


def product(here, high, low_hbm, arrived, low, total, sems, finish):
    patches, size, columns = arrived.shape
    pieces, _, depth = low.shape
    copies = [pltpu.make_async_copy(low_hbm.at[k], low.at[k], sems.at[k]) for k in range(pieces)]

    @pl.when(here)
    def _():
        for copy in copies:
            copy.start()
        rows = total.shape[0] // 2

        def half(part, carry):
            flat = arrived[...].reshape(patches * size, columns)
            mine = pl.ds(pl.multiple_of(part * rows, rows), rows)
            total[mine, :] = jnp.dot(high[mine, :], flat, preferred_element_type=jnp.float32)
            return carry

        lax.fori_loop(0, 2, half, 0)
        fresh = total[...]
        flat = arrived[...].reshape(patches * size, columns)
        for k, copy in enumerate(copies):
            copy.wait()
            part = flat[k * depth : (k + 1) * depth]
            fresh = fresh + jnp.dot(low[k], part, preferred_element_type=jnp.float32)
        finish(fresh)


def stage_kernel(step, incident_hbm, field, staged, incident, sem):
    first = lax.axis_index("lag") == 0

    @pl.when(first)
    def _():
        started((incident_hbm.at[step], incident, sem))[0].wait()
        staged[...] = incident[...].astype(jnp.float32) - field[...]

    @pl.when(jnp.logical_not(first))
    def _():
        staged[...] = field[...]


def solve_kernel(high, low_hbm, arrived, staged, inverse, current, low, total, sems):
    def finish(fresh):
        current[...] = solved(staged[...] - fresh, inverse)

    product(lax.axis_index("lag") == 0, high, low_hbm, arrived, low, total, sems, finish)


def partial_kernel(high, low_hbm, arrived, staged, after, partial, low, total, sems):
    del after

    def finish(fresh):
        partial[...] = staged[...] + fresh

    product(lax.axis_index("lag") > 0, high, low_hbm, arrived, low, total, sems, finish)


def asked_kernel(table, asked, copy_of, sem):
    started((table, copy_of, sem))[0].wait()
    for q in range(table.shape[0]):
        asked[q] = jnp.maximum(copy_of[q, 0, 0], 0)


def ahead_kernel(high, arrived, field, ahead_hbm, ahead, sems):
    patches, size, columns = arrived.shape
    rows = ahead.shape[0] // sems.shape[0]
    copies = []
    for part in range(sems.shape[0]):
        here = pl.ds(part * rows, rows)
        flat = arrived[...].reshape(patches * size, columns)
        fresh = jnp.dot(high[here, :], flat, preferred_element_type=jnp.float32)
        ahead[here, :] = field[here, :] + fresh
        copies += started((ahead.at[here], ahead_hbm.at[here], sems.at[part]))
    for copy in copies:
        copy.wait()


def pack_kernel(step, keeps, early, asked, current, *refs):
    outgoing, currents, sems = refs[-3:]
    patches, size, _ = outgoing.shape
    section = lax.axis_index("lag")

    @pl.when(section < keeps if early else section >= keeps)
    def _():
        copies = []
        for q in range(patches):
            block = asked[q] if len(asked.shape) == 1 else jnp.max(jnp.maximum(asked[q], 0))
            start = pl.multiple_of(block * size, size)
            copies.append((current.at[pl.ds(start, size)], outgoing.at[q], sems.at[q]))
        copies.append((current, currents.at[step], sems.at[patches]))
        for copy in started(*copies):
            copy.wait()


def first_pack_kernel(step, keeps, asked, own, received, outgoing, currents, sems):
    pack_kernel(step, keeps, True, asked, own, outgoing, currents, sems)
    pack_kernel(step, keeps, False, asked, received, outgoing, currents, sems)


def shifted(x):
    sections = lax.axis_size("lag")
    return lax.ppermute(x, "lag", [(i, i - 1) for i in range(1, sections)])


def spread(x):
    sections = lax.axis_size("lag")
    section = lax.axis_index("lag")
    received, keeps = x, 1
    while keeps < sections:
        if keeps > 1:
            x = jnp.where(section < keeps // 2, x, received)
        pairs = [(i, i + keeps) for i in range(keeps) if i + keeps < sections]
        received = lax.ppermute(x, "lag", pairs)
        keeps *= 2
    return x, received, max(keeps // 2, 1)


def body(incident, pending, self_inverse, retarded, block_rows, block_sources, owner_map):
    steps, unknowns, columns = incident.shape
    per_patch, size, _ = self_inverse.shape
    listed = retarded.shape[2]
    patches = lax.axis_size("patch")
    bf16, f32 = jnp.bfloat16, jnp.float32
    all_flops = 4 * unknowns * patches * size * columns
    solve_flops = 12 * unknowns * size * columns
    panel_bytes = 4 * unknowns * patches * size
    column = (unknowns, columns)
    arrived_bytes = 2 * patches * size * columns

    def exchange(x):
        return lax.all_to_all(x, "patch", split_axis=0, concat_axis=0, tiled=True)

    def pack(step, keeps, early, current, filled, after=()):
        held = [x for x in filled if x is not None]
        aliases = {}
        for out, x in enumerate(filled):
            if x is not None:
                aliases[2 + len(after) + len(aliases)] = out
        return call(
            lambda *refs: pack_kernel(step, keeps, early, *refs),
            [(HBM, (patches, size, columns), bf16), (HBM, incident.shape, bf16)],
            [(SMEM, asked), (VMEM, current)] + [(VMEM, x) for x in after] + [(HBM, x) for x in held],
            [DMA((patches + 1,))],
            aliases=aliases,
        )

    table = [(HBM, (patches, 1, 128), jnp.int32)]
    lists = [(HBM, block_sources[0]), (HBM, owner_map[None])]
    list_scratch = [
        pltpu.VMEM((patches, 1, 128), jnp.int32),
        pltpu.VMEM(block_sources.shape[1:], jnp.int32),
        pltpu.VMEM((1, owner_map.shape[0]), jnp.int32),
    ]
    wanted, current = call(
        lambda *refs: first_kernel(per_patch, *refs),
        [*table, (VMEM, column, bf16)],
        [*lists, (HBM, incident), (HBM, pending[0]), (HBM, self_inverse)],
        [
            *list_scratch,
            pltpu.VMEM(column, bf16),
            pltpu.VMEM(column, f32),
            pltpu.VMEM(self_inverse.shape, f32),
            DMA((5,)),
        ],
        solve_flops,
    )
    if lax.axis_size("lag") > 1:
        wanted = call(
            lambda *refs: request_kernel(per_patch, *refs),
            table,
            [*lists, (HBM, wanted), (VMEM, current)],
            [*list_scratch, DMA((2,))],
            aliases={2: 0},
        )
    requests = exchange(wanted)
    asked = call(
        asked_kernel,
        [(SMEM, (patches,), jnp.int32)],
        [(VMEM, requests)],
        [pltpu.SMEM(wanted.shape, jnp.int32), DMA],
    )
    chunk = max(n for n in range(1, 9) if listed % n == 0)
    panel = (unknowns, patches * size)
    pieces = 4 if patches % 4 == 0 else 1
    low_panel = (pieces, unknowns, patches * size // pieces)
    high, low, inverse = call(
        lambda *refs: panel_kernel(per_patch, *refs),
        [(VMEM, panel, bf16), (HBM, low_panel, bf16), (VMEM, self_inverse.shape, f32)],
        [(HBM, block_rows), (HBM, block_sources), (HBM, owner_map), (HBM, retarded), (HBM, self_inverse)],
        [
            pltpu.SMEM(block_rows.shape, jnp.int32),
            pltpu.SMEM(block_sources.shape, jnp.int32),
            pltpu.SMEM(owner_map.shape, jnp.int32),
            pltpu.VMEM((3, chunk, size, size), f32),
            pltpu.VMEM(low_panel, bf16),
            DMA((7,)),
        ],
        nbytes=listed * size * size * 4 + panel_bytes,
        vmem=panel_bytes // 2,
    )

    field = pending[0]
    currents = None
    for step in range(steps):
        own, received, keeps = spread(current)
        if step == 0:
            outgoing, currents = call(
                lambda *refs: first_pack_kernel(0, keeps, *refs),
                [(HBM, (patches, size, columns), bf16), (HBM, incident.shape, bf16)],
                [(VMEM, requests), (VMEM, own), (VMEM, received)],
                [DMA((patches + 1,))],
            )
        else:
            outgoing, currents = pack(step, keeps, True, own, (None, currents))
            if lax.axis_size("lag") > 1:
                outgoing, currents = pack(step, keeps, False, received, (outgoing, currents), [field])
        arrived = exchange(outgoing)
        field = shifted(field)
        if step + 1 < steps:
            staged = call(
                lambda *refs, n=step + 1: stage_kernel(n, *refs),
                [(VMEM, column, f32)],
                [(HBM, incident), (VMEM, field)],
                [pltpu.VMEM(column, bf16), DMA],
            )
            shared = [(VMEM, high), (HBM, low), (VMEM, arrived), (VMEM, staged)]
            scratch = [pltpu.VMEM(low_panel, bf16), pltpu.VMEM(column, f32), DMA((pieces,))]
            sizes = [all_flops, panel_bytes + arrived_bytes, panel_bytes + arrived_bytes]
            current = call(
                solve_kernel, [(VMEM, column, bf16)], [*shared, (VMEM, inverse)], scratch, *sizes
            )
            field = call(
                partial_kernel, [(VMEM, column, f32)], [*shared, (VMEM, current)], scratch, *sizes
            )
        else:
            field = call(
                ahead_kernel,
                [(HBM, column, f32)],
                [(VMEM, high), (VMEM, arrived), (VMEM, field)],
                [pltpu.VMEM(column, f32), DMA((2,))],
                all_flops,
                panel_bytes + arrived_bytes,
                panel_bytes + arrived_bytes,
            )
    return currents, field[None]


def solution(mesh):
    in_specs = (
        P(None, "patch", None),
        P("lag", "patch", None),
        P("patch", None, None),
        P("lag", "patch", None, None, None),
        P("lag", "patch", None),
        P("lag", "patch", None),
        P(),
    )
    out_specs = (P(None, "patch", None), P("lag", "patch", None))
    return jax.shard_map(body, mesh=mesh, in_specs=in_specs, out_specs=out_specs, check_vma=False)
```

```python
import jax
import jax.numpy as jnp
from jax import lax
from jax.experimental import pallas as pl
from jax.experimental.pallas import tpu as pltpu
from jax.sharding import PartitionSpec as P

VMEM, SMEM, HBM = pltpu.VMEM, pltpu.SMEM, pltpu.HBM
DMA = pltpu.SemaphoreType.DMA
MIB = 1 << 20


def call(kernel, outs, ins, scratch=(), flops=0, nbytes=0, vmem=0, aliases=None):
    out_shape = tuple(space(dims, dtype) for space, dims, dtype in outs)
    out_specs = tuple(pl.BlockSpec(memory_space=space) for space, _, _ in outs)
    run = pl.pallas_call(
        kernel,
        out_shape=out_shape,
        in_specs=[pl.BlockSpec(memory_space=space) for space, _ in ins],
        out_specs=out_specs,
        scratch_shapes=scratch,
        input_output_aliases=aliases or {},
        cost_estimate=pl.CostEstimate(flops=flops, bytes_accessed=nbytes, transcendentals=0),
        compiler_params=pltpu.CompilerParams(vmem_limit_bytes=vmem + 6 * MIB),
    )
    results = run(*(pltpu.with_memory_space_constraint(x, space) for space, x in ins))
    return results if len(outs) > 1 else results[0]


def started(*copies):
    copies = [pltpu.make_async_copy(*copy) for copy in copies]
    for copy in copies:
        copy.start()
    return copies


def requests_into(wanted, per_patch, sources, owner_map):
    patches, _, lanes = wanted.shape
    blocks = owner_map.shape[1]

    def numbered(dims, axis):
        return lax.broadcasted_iota(jnp.int32, dims, axis)

    source = sources[...]
    square = (blocks, blocks)
    on_diagonal = numbered(square, 0) == numbered(square, 1)
    owners = jnp.max(jnp.where(on_diagonal, owner_map[...], 0), axis=1, keepdims=True)
    looked_up = numbered((blocks, source.shape[1]), 0) == source
    storage = jnp.max(jnp.where(looked_up, owners, -1), axis=0, keepdims=True)
    patch = numbered((patches, source.shape[1]), 0)
    here = (storage >= patch * per_patch) & (storage < (patch + 1) * per_patch)
    table = jnp.max(jnp.where(here, storage - patch * per_patch, -1), axis=1, keepdims=True)
    for q in range(patches):
        wanted[q] = jnp.broadcast_to(table[q : q + 1], (1, lanes))


def first_kernel(
    per_patch,
    sources_hbm,
    owner_hbm,
    incident_hbm,
    field_hbm,
    inverse_hbm,
    wanted_hbm,
    current,
    wanted,
    sources,
    owner_map,
    incident,
    field,
    inverse,
    sems,
):
    @pl.when(lax.axis_index("lag") == 0)
    def _():
        lists = started(
            (sources_hbm, sources, sems.at[0]),
            (owner_hbm, owner_map, sems.at[1]),
        )
        arrays = started(
            (incident_hbm.at[0], incident, sems.at[2]),
            (inverse_hbm, inverse, sems.at[3]),
            (field_hbm, field, sems.at[4]),
        )
        for copy in lists:
            copy.wait()
        requests_into(wanted, per_patch, sources, owner_map)
        (done,) = started((wanted, wanted_hbm, sems.at[0]))
        for copy in arrays:
            copy.wait()
        current[...] = solved(incident[...].astype(jnp.float32) - field[...], inverse)
        done.wait()


def request_kernel(
    per_patch, sources_hbm, owner_hbm, held, after, wanted_hbm, wanted, sources, owner_map, sems
):
    del held, after

    @pl.when(lax.axis_index("lag") > 0)
    def _():
        lists = started(
            (sources_hbm, sources, sems.at[0]),
            (owner_hbm, owner_map, sems.at[1]),
        )
        for copy in lists:
            copy.wait()
        requests_into(wanted, per_patch, sources, owner_map)
        started((wanted, wanted_hbm, sems.at[0]))[0].wait()


def panel_kernel(
    per_patch,
    rows_hbm,
    sources_hbm,
    owner_hbm,
    retarded,
    inverse_hbm,
    high,
    low_hbm,
    inverse,
    rows,
    sources,
    owner_map,
    parts,
    low,
    sems,
):
    size = retarded.shape[-1]
    slots, chunk = parts.shape[:2]
    chunks = retarded.shape[2] // chunk

    def fetch(c):
        part = retarded.at[0, 0, pl.ds(c * chunk, chunk)]
        return pltpu.make_async_copy(part, parts.at[c % slots], sems.at[c % slots])

    lists = started(
        (rows_hbm, rows, sems.at[slots]),
        (sources_hbm, sources, sems.at[slots + 1]),
        (owner_hbm, owner_map, sems.at[slots + 2]),
        (inverse_hbm, inverse, sems.at[slots + 3]),
    )
    for c in range(min(slots, chunks)):
        fetch(c).start()
    high[...] = jnp.zeros_like(high)
    low[...] = jnp.zeros_like(low)
    for copy in lists:
        copy.wait()

    def entry(c, k, carry):
        source = sources[0, 0, c * chunk + k]

        @pl.when(source >= 0)
        def _():
            owner = owner_map[source] // per_patch
            row = pl.multiple_of(rows[0, 0, c * chunk + k] * size, size)
            column = pl.multiple_of(owner * size, size)
            block = parts[c % slots, k]
            rounded = block.astype(high.dtype)
            rest = (block - rounded.astype(jnp.float32)).astype(low.dtype)
            high[pl.ds(row, size), pl.ds(column, size)] = rounded
            piece = column // low.shape[2]
            inside = pl.multiple_of(column - piece * low.shape[2], size)
            low[piece, pl.ds(row, size), pl.ds(inside, size)] = rest

        return carry

    for c in range(chunks):
        fetch(c).wait()
        lax.fori_loop(0, chunk, lambda k, carry, c=c: entry(c, k, carry), 0)
        if c + slots < chunks:
            fetch(c + slots).start()
    started((low, low_hbm, sems.at[0]))[0].wait()


def solved(excess, self_inverse):
    blocks, size, _ = self_inverse.shape
    parts = [
        jnp.dot(
            self_inverse[k],
            excess[k * size : (k + 1) * size],
            precision=lax.Precision.HIGHEST,
            preferred_element_type=jnp.float32,
        )
        for k in range(blocks)
    ]
    return jnp.concatenate(parts, axis=0).astype(jnp.bfloat16)


def product(here, high, low_hbm, arrived, low, total, sems, finish):
    patches, size, columns = arrived.shape
    pieces, _, depth = low.shape
    copies = [pltpu.make_async_copy(low_hbm.at[k], low.at[k], sems.at[k]) for k in range(pieces)]

    @pl.when(here)
    def _():
        for copy in copies:
            copy.start()
        rows = total.shape[0] // 2

        def half(part, carry):
            flat = arrived[...].reshape(patches * size, columns)
            mine = pl.ds(pl.multiple_of(part * rows, rows), rows)
            total[mine, :] = jnp.dot(high[mine, :], flat, preferred_element_type=jnp.float32)
            return carry

        lax.fori_loop(0, 2, half, 0)
        fresh = total[...]
        flat = arrived[...].reshape(patches * size, columns)
        for k, copy in enumerate(copies):
            copy.wait()
            part = flat[k * depth : (k + 1) * depth]
            fresh = fresh + jnp.dot(low[k], part, preferred_element_type=jnp.float32)
        finish(fresh)


def stage_kernel(step, incident_hbm, field, staged, incident, sem):
    first = lax.axis_index("lag") == 0

    @pl.when(first)
    def _():
        started((incident_hbm.at[step], incident, sem))[0].wait()
        staged[...] = incident[...].astype(jnp.float32) - field[...]

    @pl.when(jnp.logical_not(first))
    def _():
        staged[...] = field[...]


def solve_kernel(high, low_hbm, arrived, staged, inverse, current, low, total, sems):
    def finish(fresh):
        current[...] = solved(staged[...] - fresh, inverse)

    product(lax.axis_index("lag") == 0, high, low_hbm, arrived, low, total, sems, finish)


def partial_kernel(high, low_hbm, arrived, staged, after, partial, low, total, sems):
    del after

    def finish(fresh):
        partial[...] = staged[...] + fresh

    product(lax.axis_index("lag") > 0, high, low_hbm, arrived, low, total, sems, finish)


def asked_kernel(table, asked, copy_of, sem):
    started((table, copy_of, sem))[0].wait()
    for q in range(table.shape[0]):
        asked[q] = jnp.maximum(copy_of[q, 0, 0], 0)


def ahead_kernel(high, arrived, field, ahead_hbm, ahead, sems):
    patches, size, columns = arrived.shape
    rows = ahead.shape[0] // sems.shape[0]
    copies = []
    for part in range(sems.shape[0]):
        here = pl.ds(part * rows, rows)
        flat = arrived[...].reshape(patches * size, columns)
        fresh = jnp.dot(high[here, :], flat, preferred_element_type=jnp.float32)
        ahead[here, :] = field[here, :] + fresh
        copies += started((ahead.at[here], ahead_hbm.at[here], sems.at[part]))
    for copy in copies:
        copy.wait()


def pack_kernel(step, keeps, early, asked, current, *refs):
    outgoing, currents, sems = refs[-3:]
    patches, size, _ = outgoing.shape
    section = lax.axis_index("lag")

    @pl.when(section < keeps if early else section >= keeps)
    def _():
        for q in range(patches):
            block = asked[q] if len(asked.shape) == 1 else jnp.max(jnp.maximum(asked[q], 0))
            start = pl.multiple_of(block * size, size)
            started((current.at[pl.ds(start, size)], outgoing.at[q], sems.at[0]))
        (kept_copy,) = started((current, currents.at[step], sems.at[1]))
        pltpu.make_async_copy(outgoing, outgoing, sems.at[0]).wait()
        kept_copy.wait()


def first_pack_kernel(step, keeps, asked, own, received, outgoing, currents, sems):
    pack_kernel(step, keeps, True, asked, own, outgoing, currents, sems)
    pack_kernel(step, keeps, False, asked, received, outgoing, currents, sems)


def shifted(x):
    sections = lax.axis_size("lag")
    return lax.ppermute(x, "lag", [(i, i - 1) for i in range(1, sections)])


def spread(x):
    sections = lax.axis_size("lag")
    section = lax.axis_index("lag")
    received, keeps = x, 1
    while keeps < sections:
        if keeps > 1:
            x = jnp.where(section < keeps // 2, x, received)
        pairs = [(i, i + keeps) for i in range(keeps) if i + keeps < sections]
        received = lax.ppermute(x, "lag", pairs)
        keeps *= 2
    return x, received, max(keeps // 2, 1)


def body(incident, pending, self_inverse, retarded, block_rows, block_sources, owner_map):
    steps, unknowns, columns = incident.shape
    per_patch, size, _ = self_inverse.shape
    listed = retarded.shape[2]
    patches = lax.axis_size("patch")
    bf16, f32 = jnp.bfloat16, jnp.float32
    all_flops = 4 * unknowns * patches * size * columns
    solve_flops = 12 * unknowns * size * columns
    panel_bytes = 4 * unknowns * patches * size
    column = (unknowns, columns)
    arrived_bytes = 2 * patches * size * columns

    def exchange(x):
        return lax.all_to_all(x, "patch", split_axis=0, concat_axis=0, tiled=True)

    def pack(step, keeps, early, current, filled, after=()):
        held = [x for x in filled if x is not None]
        aliases = {}
        for out, x in enumerate(filled):
            if x is not None:
                aliases[2 + len(after) + len(aliases)] = out
        return call(
            lambda *refs: pack_kernel(step, keeps, early, *refs),
            [(HBM, (patches, size, columns), bf16), (HBM, incident.shape, bf16)],
            [(SMEM, asked), (VMEM, current)] + [(VMEM, x) for x in after] + [(HBM, x) for x in held],
            [DMA((2,))],
            aliases=aliases,
        )

    table = [(HBM, (patches, 1, 128), jnp.int32)]
    lists = [(HBM, block_sources[0]), (HBM, owner_map[None])]
    list_scratch = [
        pltpu.VMEM((patches, 1, 128), jnp.int32),
        pltpu.VMEM(block_sources.shape[1:], jnp.int32),
        pltpu.VMEM((1, owner_map.shape[0]), jnp.int32),
    ]
    wanted, current = call(
        lambda *refs: first_kernel(per_patch, *refs),
        [*table, (VMEM, column, bf16)],
        [*lists, (HBM, incident), (HBM, pending[0]), (HBM, self_inverse)],
        [
            *list_scratch,
            pltpu.VMEM(column, bf16),
            pltpu.VMEM(column, f32),
            pltpu.VMEM(self_inverse.shape, f32),
            DMA((5,)),
        ],
        solve_flops,
    )
    if lax.axis_size("lag") > 1:
        wanted = call(
            lambda *refs: request_kernel(per_patch, *refs),
            table,
            [*lists, (HBM, wanted), (VMEM, current)],
            [*list_scratch, DMA((2,))],
            aliases={2: 0},
        )
    requests = exchange(wanted)
    asked = call(
        asked_kernel,
        [(SMEM, (patches,), jnp.int32)],
        [(VMEM, requests)],
        [pltpu.SMEM(wanted.shape, jnp.int32), DMA],
    )
    chunk = max(n for n in range(1, 9) if listed % n == 0)
    panel = (unknowns, patches * size)
    pieces = 4 if patches % 4 == 0 else 1
    low_panel = (pieces, unknowns, patches * size // pieces)
    high, low, inverse = call(
        lambda *refs: panel_kernel(per_patch, *refs),
        [(VMEM, panel, bf16), (HBM, low_panel, bf16), (VMEM, self_inverse.shape, f32)],
        [(HBM, block_rows), (HBM, block_sources), (HBM, owner_map), (HBM, retarded), (HBM, self_inverse)],
        [
            pltpu.SMEM(block_rows.shape, jnp.int32),
            pltpu.SMEM(block_sources.shape, jnp.int32),
            pltpu.SMEM(owner_map.shape, jnp.int32),
            pltpu.VMEM((3, chunk, size, size), f32),
            pltpu.VMEM(low_panel, bf16),
            DMA((7,)),
        ],
        nbytes=listed * size * size * 4 + panel_bytes,
        vmem=panel_bytes // 2,
    )

    field = pending[0]
    currents = None
    for step in range(steps):
        own, received, keeps = spread(current)
        if step == 0:
            outgoing, currents = call(
                lambda *refs: first_pack_kernel(0, keeps, *refs),
                [(HBM, (patches, size, columns), bf16), (HBM, incident.shape, bf16)],
                [(VMEM, requests), (VMEM, own), (VMEM, received)],
                [DMA((2,))],
            )
        else:
            outgoing, currents = pack(step, keeps, True, own, (None, currents))
            if lax.axis_size("lag") > 1:
                outgoing, currents = pack(step, keeps, False, received, (outgoing, currents), [field])
        arrived = exchange(outgoing)
        field = shifted(field)
        if step + 1 < steps:
            staged = call(
                lambda *refs, n=step + 1: stage_kernel(n, *refs),
                [(VMEM, column, f32)],
                [(HBM, incident), (VMEM, field)],
                [pltpu.VMEM(column, bf16), DMA],
            )
            shared = [(VMEM, high), (HBM, low), (VMEM, arrived), (VMEM, staged)]
            scratch = [pltpu.VMEM(low_panel, bf16), pltpu.VMEM(column, f32), DMA((pieces,))]
            sizes = [all_flops, panel_bytes + arrived_bytes, panel_bytes + arrived_bytes]
            current = call(
                solve_kernel, [(VMEM, column, bf16)], [*shared, (VMEM, inverse)], scratch, *sizes
            )
            field = call(
                partial_kernel, [(VMEM, column, f32)], [*shared, (VMEM, current)], scratch, *sizes
            )
        else:
            field = call(
                ahead_kernel,
                [(HBM, column, f32)],
                [(VMEM, high), (VMEM, arrived), (VMEM, field)],
                [pltpu.VMEM(column, f32), DMA((2,))],
                all_flops,
                panel_bytes + arrived_bytes,
                panel_bytes + arrived_bytes,
            )
    return currents, field[None]


def solution(mesh):
    in_specs = (
        P(None, "patch", None),
        P("lag", "patch", None),
        P("patch", None, None),
        P("lag", "patch", None, None, None),
        P("lag", "patch", None),
        P("lag", "patch", None),
        P(),
    )
    out_specs = (P(None, "patch", None), P("lag", "patch", None))
    return jax.shard_map(body, mesh=mesh, in_specs=in_specs, out_specs=out_specs, check_vma=False)
```

```python
import jax
import jax.numpy as jnp
from jax import lax
from jax.experimental import pallas as pl
from jax.experimental.pallas import tpu as pltpu
from jax.sharding import PartitionSpec as P

VMEM, SMEM, HBM = pltpu.VMEM, pltpu.SMEM, pltpu.HBM
DMA = pltpu.SemaphoreType.DMA
MIB = 1 << 20


def call(kernel, outs, ins, scratch=(), flops=0, nbytes=0, vmem=0, aliases=None):
    out_shape = tuple(space(dims, dtype) for space, dims, dtype in outs)
    out_specs = tuple(pl.BlockSpec(memory_space=space) for space, _, _ in outs)
    run = pl.pallas_call(
        kernel,
        out_shape=out_shape,
        in_specs=[pl.BlockSpec(memory_space=space) for space, _ in ins],
        out_specs=out_specs,
        scratch_shapes=scratch,
        input_output_aliases=aliases or {},
        cost_estimate=pl.CostEstimate(flops=flops, bytes_accessed=nbytes, transcendentals=0),
        compiler_params=pltpu.CompilerParams(vmem_limit_bytes=vmem + 6 * MIB),
    )
    results = run(*(pltpu.with_memory_space_constraint(x, space) for space, x in ins))
    return results if len(outs) > 1 else results[0]


def started(*copies):
    copies = [pltpu.make_async_copy(*copy) for copy in copies]
    for copy in copies:
        copy.start()
    return copies


def requests_into(wanted, per_patch, sources, owner_map):
    patches, _, lanes = wanted.shape
    blocks = owner_map.shape[1]

    def numbered(dims, axis):
        return lax.broadcasted_iota(jnp.int32, dims, axis)

    source = sources[...]
    square = (blocks, blocks)
    on_diagonal = numbered(square, 0) == numbered(square, 1)
    owners = jnp.max(jnp.where(on_diagonal, owner_map[...], 0), axis=1, keepdims=True)
    looked_up = numbered((blocks, source.shape[1]), 0) == source
    storage = jnp.max(jnp.where(looked_up, owners, -1), axis=0, keepdims=True)
    patch = numbered((patches, source.shape[1]), 0)
    here = (storage >= patch * per_patch) & (storage < (patch + 1) * per_patch)
    table = jnp.max(jnp.where(here, storage - patch * per_patch, -1), axis=1, keepdims=True)
    for q in range(patches):
        wanted[q] = jnp.broadcast_to(table[q : q + 1], (1, lanes))


def first_kernel(
    per_patch,
    sources_hbm,
    owner_hbm,
    incident_hbm,
    field_hbm,
    inverse_hbm,
    wanted_hbm,
    current,
    wanted,
    sources,
    owner_map,
    incident,
    field,
    inverse,
    sems,
):
    @pl.when(lax.axis_index("lag") == 0)
    def _():
        lists = started(
            (sources_hbm, sources, sems.at[0]),
            (owner_hbm, owner_map, sems.at[1]),
        )
        arrays = started(
            (incident_hbm.at[0], incident, sems.at[2]),
            (inverse_hbm, inverse, sems.at[3]),
            (field_hbm, field, sems.at[4]),
        )
        for copy in lists:
            copy.wait()
        requests_into(wanted, per_patch, sources, owner_map)
        (done,) = started((wanted, wanted_hbm, sems.at[0]))
        for copy in arrays:
            copy.wait()
        current[...] = solved(incident[...].astype(jnp.float32) - field[...], inverse)
        done.wait()


def request_kernel(
    per_patch, sources_hbm, owner_hbm, held, after, wanted_hbm, wanted, sources, owner_map, sems
):
    del held, after

    @pl.when(lax.axis_index("lag") > 0)
    def _():
        lists = started(
            (sources_hbm, sources, sems.at[0]),
            (owner_hbm, owner_map, sems.at[1]),
        )
        for copy in lists:
            copy.wait()
        requests_into(wanted, per_patch, sources, owner_map)
        started((wanted, wanted_hbm, sems.at[0]))[0].wait()


def panel_kernel(
    per_patch,
    rows_hbm,
    sources_hbm,
    owner_hbm,
    retarded,
    inverse_hbm,
    high,
    low_hbm,
    inverse,
    rows,
    sources,
    owner_map,
    parts,
    low,
    sems,
):
    size = retarded.shape[-1]
    slots, chunk = parts.shape[:2]
    chunks = retarded.shape[2] // chunk

    def fetch(c):
        part = retarded.at[0, 0, pl.ds(c * chunk, chunk)]
        return pltpu.make_async_copy(part, parts.at[c % slots], sems.at[c % slots])

    lists = started(
        (rows_hbm, rows, sems.at[slots]),
        (sources_hbm, sources, sems.at[slots + 1]),
        (owner_hbm, owner_map, sems.at[slots + 2]),
        (inverse_hbm, inverse, sems.at[slots + 3]),
    )
    for c in range(min(slots, chunks)):
        fetch(c).start()
    high[...] = jnp.zeros_like(high)
    low[...] = jnp.zeros_like(low)
    for copy in lists:
        copy.wait()

    def entry(c, k, carry):
        source = sources[0, 0, c * chunk + k]

        @pl.when(source >= 0)
        def _():
            owner = owner_map[source] // per_patch
            row = pl.multiple_of(rows[0, 0, c * chunk + k] * size, size)
            column = pl.multiple_of(owner * size, size)
            block = parts[c % slots, k]
            rounded = block.astype(high.dtype)
            rest = (block - rounded.astype(jnp.float32)).astype(low.dtype)
            high[pl.ds(row, size), pl.ds(column, size)] = rounded
            piece = column // low.shape[2]
            inside = pl.multiple_of(column - piece * low.shape[2], size)
            low[piece, pl.ds(row, size), pl.ds(inside, size)] = rest

        return carry

    for c in range(chunks):
        fetch(c).wait()
        lax.fori_loop(0, chunk, lambda k, carry, c=c: entry(c, k, carry), 0)
        if c + slots < chunks:
            fetch(c + slots).start()
    started((low, low_hbm, sems.at[0]))[0].wait()


def solved(excess, self_inverse):
    blocks, size, _ = self_inverse.shape
    parts = [
        jnp.dot(
            self_inverse[k],
            excess[k * size : (k + 1) * size],
            precision=lax.Precision.HIGHEST,
            preferred_element_type=jnp.float32,
        )
        for k in range(blocks)
    ]
    return jnp.concatenate(parts, axis=0).astype(jnp.bfloat16)


def product(here, high, low_hbm, arrived, low, total, sems, early, finish):
    patches, size, columns = arrived.shape
    pieces, _, depth = low.shape
    copies = [pltpu.make_async_copy(low_hbm.at[k], low.at[k], sems.at[k]) for k in range(pieces)]

    @pl.when(here)
    def _():
        for copy in copies:
            copy.start()
        rows = total.shape[0] // 2

        def half(part, carry):
            flat = arrived[...].reshape(patches * size, columns)
            mine = pl.ds(pl.multiple_of(part * rows, rows), rows)
            early(mine, part, jnp.dot(high[mine, :], flat, preferred_element_type=jnp.float32))
            return carry

        lax.fori_loop(0, 2, half, 0)
        flat = arrived[...].reshape(patches * size, columns)
        rest = jnp.zeros(total.shape, jnp.float32)
        for k, copy in enumerate(copies):
            copy.wait()
            part = flat[k * depth : (k + 1) * depth]
            rest = rest + jnp.dot(low[k], part, preferred_element_type=jnp.float32)
        finish(rest)


def stage_kernel(step, incident_hbm, field, staged, incident, sem):
    first = lax.axis_index("lag") == 0

    @pl.when(first)
    def _():
        started((incident_hbm.at[step], incident, sem))[0].wait()
        staged[...] = incident[...].astype(jnp.float32) - field[...]

    @pl.when(jnp.logical_not(first))
    def _():
        staged[...] = field[...]


def solve_kernel(high, low_hbm, arrived, staged, inverse, current, low, total, sems):
    blocks, size, _ = inverse.shape

    def early(mine, part, fresh):
        excess = staged[mine, :] - fresh
        parts = [
            jnp.dot(
                inverse[part * (blocks // 2) + k],
                excess[k * size : (k + 1) * size],
                precision=lax.Precision.HIGHEST,
                preferred_element_type=jnp.float32,
            )
            for k in range(blocks // 2)
        ]
        total[mine, :] = jnp.concatenate(parts, axis=0)

    def finish(rest):
        rest = rest.astype(jnp.bfloat16)
        for k in range(blocks):
            mine = slice(k * size, (k + 1) * size)
            less = jnp.dot(
                inverse[k].astype(jnp.bfloat16), rest[mine], preferred_element_type=jnp.float32
            )
            current[mine, :] = (total[mine, :] - less).astype(jnp.bfloat16)

    product(lax.axis_index("lag") == 0, high, low_hbm, arrived, low, total, sems, early, finish)


def partial_kernel(high, low_hbm, arrived, staged, after, partial, low, total, sems):
    del after

    def early(mine, part, fresh):
        total[mine, :] = staged[mine, :] + fresh

    def finish(rest):
        partial[...] = total[...] + rest

    product(lax.axis_index("lag") > 0, high, low_hbm, arrived, low, total, sems, early, finish)


def asked_kernel(table, asked, copy_of, sem):
    started((table, copy_of, sem))[0].wait()
    for q in range(table.shape[0]):
        asked[q] = jnp.maximum(copy_of[q, 0, 0], 0)


def ahead_kernel(high, arrived, field, ahead_hbm, ahead, sems):
    patches, size, columns = arrived.shape
    rows = ahead.shape[0] // sems.shape[0]
    copies = []
    for part in range(sems.shape[0]):
        here = pl.ds(part * rows, rows)
        flat = arrived[...].reshape(patches * size, columns)
        fresh = jnp.dot(high[here, :], flat, preferred_element_type=jnp.float32)
        ahead[here, :] = field[here, :] + fresh
        copies += started((ahead.at[here], ahead_hbm.at[here], sems.at[part]))
    for copy in copies:
        copy.wait()


def pack_kernel(step, keeps, early, asked, current, *refs):
    outgoing, currents, sems = refs[-3:]
    patches, size, _ = outgoing.shape
    section = lax.axis_index("lag")

    @pl.when(section < keeps if early else section >= keeps)
    def _():
        for q in range(patches):
            block = asked[q] if len(asked.shape) == 1 else jnp.max(jnp.maximum(asked[q], 0))
            start = pl.multiple_of(block * size, size)
            started((current.at[pl.ds(start, size)], outgoing.at[q], sems.at[0]))
        (kept_copy,) = started((current, currents.at[step], sems.at[1]))
        pltpu.make_async_copy(outgoing, outgoing, sems.at[0]).wait()
        kept_copy.wait()


def first_pack_kernel(step, keeps, asked, own, received, outgoing, currents, sems):
    pack_kernel(step, keeps, True, asked, own, outgoing, currents, sems)
    pack_kernel(step, keeps, False, asked, received, outgoing, currents, sems)


def shifted(x):
    sections = lax.axis_size("lag")
    return lax.ppermute(x, "lag", [(i, i - 1) for i in range(1, sections)])


def spread(x):
    sections = lax.axis_size("lag")
    section = lax.axis_index("lag")
    received, keeps = x, 1
    while keeps < sections:
        if keeps > 1:
            x = jnp.where(section < keeps // 2, x, received)
        pairs = [(i, i + keeps) for i in range(keeps) if i + keeps < sections]
        received = lax.ppermute(x, "lag", pairs)
        keeps *= 2
    return x, received, max(keeps // 2, 1)


def body(incident, pending, self_inverse, retarded, block_rows, block_sources, owner_map):
    steps, unknowns, columns = incident.shape
    per_patch, size, _ = self_inverse.shape
    listed = retarded.shape[2]
    patches = lax.axis_size("patch")
    bf16, f32 = jnp.bfloat16, jnp.float32
    all_flops = 4 * unknowns * patches * size * columns
    solve_flops = 12 * unknowns * size * columns
    panel_bytes = 4 * unknowns * patches * size
    column = (unknowns, columns)
    arrived_bytes = 2 * patches * size * columns

    def exchange(x):
        return lax.all_to_all(x, "patch", split_axis=0, concat_axis=0, tiled=True)

    def pack(step, keeps, early, current, filled, after=()):
        held = [x for x in filled if x is not None]
        aliases = {}
        for out, x in enumerate(filled):
            if x is not None:
                aliases[2 + len(after) + len(aliases)] = out
        return call(
            lambda *refs: pack_kernel(step, keeps, early, *refs),
            [(HBM, (patches, size, columns), bf16), (HBM, incident.shape, bf16)],
            [(SMEM, asked), (VMEM, current)] + [(VMEM, x) for x in after] + [(HBM, x) for x in held],
            [DMA((2,))],
            aliases=aliases,
        )

    table = [(HBM, (patches, 1, 128), jnp.int32)]
    lists = [(HBM, block_sources[0]), (HBM, owner_map[None])]
    list_scratch = [
        pltpu.VMEM((patches, 1, 128), jnp.int32),
        pltpu.VMEM(block_sources.shape[1:], jnp.int32),
        pltpu.VMEM((1, owner_map.shape[0]), jnp.int32),
    ]
    wanted, current = call(
        lambda *refs: first_kernel(per_patch, *refs),
        [*table, (VMEM, column, bf16)],
        [*lists, (HBM, incident), (HBM, pending[0]), (HBM, self_inverse)],
        [
            *list_scratch,
            pltpu.VMEM(column, bf16),
            pltpu.VMEM(column, f32),
            pltpu.VMEM(self_inverse.shape, f32),
            DMA((5,)),
        ],
        solve_flops,
    )
    if lax.axis_size("lag") > 1:
        wanted = call(
            lambda *refs: request_kernel(per_patch, *refs),
            table,
            [*lists, (HBM, wanted), (VMEM, current)],
            [*list_scratch, DMA((2,))],
            aliases={2: 0},
        )
    requests = exchange(wanted)
    asked = call(
        asked_kernel,
        [(SMEM, (patches,), jnp.int32)],
        [(VMEM, requests)],
        [pltpu.SMEM(wanted.shape, jnp.int32), DMA],
    )
    chunk = max(n for n in range(1, 9) if listed % n == 0)
    panel = (unknowns, patches * size)
    pieces = 4 if patches % 4 == 0 else 1
    low_panel = (pieces, unknowns, patches * size // pieces)
    high, low, inverse = call(
        lambda *refs: panel_kernel(per_patch, *refs),
        [(VMEM, panel, bf16), (HBM, low_panel, bf16), (VMEM, self_inverse.shape, f32)],
        [(HBM, block_rows), (HBM, block_sources), (HBM, owner_map), (HBM, retarded), (HBM, self_inverse)],
        [
            pltpu.SMEM(block_rows.shape, jnp.int32),
            pltpu.SMEM(block_sources.shape, jnp.int32),
            pltpu.SMEM(owner_map.shape, jnp.int32),
            pltpu.VMEM((3, chunk, size, size), f32),
            pltpu.VMEM(low_panel, bf16),
            DMA((7,)),
        ],
        nbytes=listed * size * size * 4 + panel_bytes,
        vmem=panel_bytes // 2,
    )

    field = pending[0]
    currents = None
    for step in range(steps):
        own, received, keeps = spread(current)
        if step == 0:
            outgoing, currents = call(
                lambda *refs: first_pack_kernel(0, keeps, *refs),
                [(HBM, (patches, size, columns), bf16), (HBM, incident.shape, bf16)],
                [(VMEM, requests), (VMEM, own), (VMEM, received)],
                [DMA((2,))],
            )
        else:
            outgoing, currents = pack(step, keeps, True, own, (None, currents))
            if lax.axis_size("lag") > 1:
                outgoing, currents = pack(step, keeps, False, received, (outgoing, currents), [field])
        arrived = exchange(outgoing)
        field = shifted(field)
        if step + 1 < steps:
            staged = call(
                lambda *refs, n=step + 1: stage_kernel(n, *refs),
                [(VMEM, column, f32)],
                [(HBM, incident), (VMEM, field)],
                [pltpu.VMEM(column, bf16), DMA],
            )
            shared = [(VMEM, high), (HBM, low), (VMEM, arrived), (VMEM, staged)]
            scratch = [pltpu.VMEM(low_panel, bf16), pltpu.VMEM(column, f32), DMA((pieces,))]
            sizes = [all_flops, panel_bytes + arrived_bytes, panel_bytes + arrived_bytes]
            current = call(
                solve_kernel, [(VMEM, column, bf16)], [*shared, (VMEM, inverse)], scratch, *sizes
            )
            field = call(
                partial_kernel, [(VMEM, column, f32)], [*shared, (VMEM, current)], scratch, *sizes
            )
        else:
            field = call(
                ahead_kernel,
                [(HBM, column, f32)],
                [(VMEM, high), (VMEM, arrived), (VMEM, field)],
                [pltpu.VMEM(column, f32), DMA((2,))],
                all_flops,
                panel_bytes + arrived_bytes,
                panel_bytes + arrived_bytes,
            )
    return currents, field[None]


def solution(mesh):
    in_specs = (
        P(None, "patch", None),
        P("lag", "patch", None),
        P("patch", None, None),
        P("lag", "patch", None, None, None),
        P("lag", "patch", None),
        P("lag", "patch", None),
        P(),
    )
    out_specs = (P(None, "patch", None), P("lag", "patch", None))
    return jax.shard_map(body, mesh=mesh, in_specs=in_specs, out_specs=out_specs, check_vma=False)
```

```python
import jax
import jax.numpy as jnp
from jax import lax
from jax.experimental import pallas as pl
from jax.experimental.pallas import tpu as pltpu
from jax.sharding import PartitionSpec as P

VMEM, SMEM, HBM = pltpu.VMEM, pltpu.SMEM, pltpu.HBM
DMA = pltpu.SemaphoreType.DMA
MIB = 1 << 20


def call(kernel, outs, ins, scratch=(), flops=0, nbytes=0, vmem=0, aliases=None):
    out_shape = tuple(space(dims, dtype) for space, dims, dtype in outs)
    out_specs = tuple(pl.BlockSpec(memory_space=space) for space, _, _ in outs)
    run = pl.pallas_call(
        kernel,
        out_shape=out_shape,
        in_specs=[pl.BlockSpec(memory_space=space) for space, _ in ins],
        out_specs=out_specs,
        scratch_shapes=scratch,
        input_output_aliases=aliases or {},
        cost_estimate=pl.CostEstimate(flops=flops, bytes_accessed=nbytes, transcendentals=0),
        compiler_params=pltpu.CompilerParams(vmem_limit_bytes=vmem + 6 * MIB),
    )
    results = run(*(pltpu.with_memory_space_constraint(x, space) for space, x in ins))
    return results if len(outs) > 1 else results[0]


def slot_of(patch, patches):
    quarter = patches // 4
    return patch if patches % 4 else patch % quarter * 4 + patch // quarter


def patch_in(slot, patches):
    return slot if patches % 4 else slot % 4 * (patches // 4) + slot // 4


def started(*copies):
    copies = [pltpu.make_async_copy(*copy) for copy in copies]
    for copy in copies:
        copy.start()
    return copies


def requests_into(wanted, per_patch, sources, owner_map):
    patches, _, lanes = wanted.shape
    blocks = owner_map.shape[1]

    def numbered(dims, axis):
        return lax.broadcasted_iota(jnp.int32, dims, axis)

    source = sources[...]
    square = (blocks, blocks)
    on_diagonal = numbered(square, 0) == numbered(square, 1)
    owners = jnp.max(jnp.where(on_diagonal, owner_map[...], 0), axis=1, keepdims=True)
    looked_up = numbered((blocks, source.shape[1]), 0) == source
    storage = jnp.max(jnp.where(looked_up, owners, -1), axis=0, keepdims=True)
    patch = patch_in(numbered((patches, source.shape[1]), 0), patches)
    here = (storage >= patch * per_patch) & (storage < (patch + 1) * per_patch)
    table = jnp.max(jnp.where(here, storage - patch * per_patch, -1), axis=1, keepdims=True)
    for q in range(patches):
        wanted[q] = jnp.broadcast_to(table[q : q + 1], (1, lanes))


def first_kernel(
    per_patch,
    sources_hbm,
    owner_hbm,
    incident_hbm,
    field_hbm,
    inverse_hbm,
    wanted_hbm,
    current,
    wanted,
    sources,
    owner_map,
    incident,
    field,
    inverse,
    sems,
):
    @pl.when(lax.axis_index("lag") == 0)
    def _():
        lists = started(
            (sources_hbm, sources, sems.at[0]),
            (owner_hbm, owner_map, sems.at[1]),
        )
        arrays = started(
            (incident_hbm.at[0], incident, sems.at[2]),
            (inverse_hbm, inverse, sems.at[3]),
            (field_hbm, field, sems.at[4]),
        )
        for copy in lists:
            copy.wait()
        requests_into(wanted, per_patch, sources, owner_map)
        (done,) = started((wanted, wanted_hbm, sems.at[0]))
        for copy in arrays:
            copy.wait()
        current[...] = solved(incident[...].astype(jnp.float32) - field[...], inverse)
        done.wait()


def request_kernel(
    per_patch, sources_hbm, owner_hbm, held, after, wanted_hbm, wanted, sources, owner_map, sems
):
    del held, after

    @pl.when(lax.axis_index("lag") > 0)
    def _():
        lists = started(
            (sources_hbm, sources, sems.at[0]),
            (owner_hbm, owner_map, sems.at[1]),
        )
        for copy in lists:
            copy.wait()
        requests_into(wanted, per_patch, sources, owner_map)
        started((wanted, wanted_hbm, sems.at[0]))[0].wait()


def panel_kernel(
    per_patch,
    rows_hbm,
    sources_hbm,
    owner_hbm,
    retarded,
    inverse_hbm,
    high,
    low_hbm,
    inverse,
    rows,
    sources,
    owner_map,
    parts,
    low,
    sems,
):
    size = retarded.shape[-1]
    slots, chunk = parts.shape[:2]
    chunks = retarded.shape[2] // chunk

    def fetch(c):
        part = retarded.at[0, 0, pl.ds(c * chunk, chunk)]
        return pltpu.make_async_copy(part, parts.at[c % slots], sems.at[c % slots])

    lists = started(
        (rows_hbm, rows, sems.at[slots]),
        (sources_hbm, sources, sems.at[slots + 1]),
        (owner_hbm, owner_map, sems.at[slots + 2]),
        (inverse_hbm, inverse, sems.at[slots + 3]),
    )
    for c in range(min(slots, chunks)):
        fetch(c).start()
    high[...] = jnp.zeros_like(high)
    low[...] = jnp.zeros_like(low)
    for copy in lists:
        copy.wait()

    def entry(c, k, carry):
        source = sources[0, 0, c * chunk + k]

        @pl.when(source >= 0)
        def _():
            owner = slot_of(owner_map[source] // per_patch, high.shape[1] // size)
            row = pl.multiple_of(rows[0, 0, c * chunk + k] * size, size)
            column = pl.multiple_of(owner * size, size)
            block = parts[c % slots, k]
            rounded = block.astype(high.dtype)
            rest = (block - rounded.astype(jnp.float32)).astype(low.dtype)
            high[pl.ds(row, size), pl.ds(column, size)] = rounded
            piece = column // low.shape[2]
            inside = pl.multiple_of(column - piece * low.shape[2], size)
            low[piece, pl.ds(row, size), pl.ds(inside, size)] = rest

        return carry

    for c in range(chunks):
        fetch(c).wait()
        lax.fori_loop(0, chunk, lambda k, carry, c=c: entry(c, k, carry), 0)
        if c + slots < chunks:
            fetch(c + slots).start()
    started((low, low_hbm, sems.at[0]))[0].wait()


def solved(excess, self_inverse):
    blocks, size, _ = self_inverse.shape
    parts = [
        jnp.dot(
            self_inverse[k],
            excess[k * size : (k + 1) * size],
            precision=lax.Precision.HIGHEST,
            preferred_element_type=jnp.float32,
        )
        for k in range(blocks)
    ]
    return jnp.concatenate(parts, axis=0).astype(jnp.bfloat16)


def product(here, high, low_hbm, arrived, low, total, sems, finish):
    patches, size, columns = arrived.shape
    pieces, _, depth = low.shape
    copies = [pltpu.make_async_copy(low_hbm.at[k], low.at[k], sems.at[k]) for k in range(pieces)]

    @pl.when(here)
    def _():
        for copy in copies:
            copy.start()
        rows = total.shape[0] // 2

        def half(part, carry):
            flat = arrived[...].reshape(patches * size, columns)
            mine = pl.ds(pl.multiple_of(part * rows, rows), rows)
            total[mine, :] = jnp.dot(high[mine, :], flat, preferred_element_type=jnp.float32)
            return carry

        lax.fori_loop(0, 2, half, 0)
        fresh = total[...]
        flat = arrived[...].reshape(patches * size, columns)
        for k, copy in enumerate(copies):
            copy.wait()
            part = flat[k * depth : (k + 1) * depth]
            fresh = fresh + jnp.dot(low[k], part, preferred_element_type=jnp.float32)
        finish(fresh)


def stage_kernel(step, incident_hbm, field, staged, incident, sem):
    first = lax.axis_index("lag") == 0

    @pl.when(first)
    def _():
        started((incident_hbm.at[step], incident, sem))[0].wait()
        staged[...] = incident[...].astype(jnp.float32) - field[...]

    @pl.when(jnp.logical_not(first))
    def _():
        staged[...] = field[...]


def solve_kernel(high, low_hbm, arrived, staged, inverse, current, low, total, sems):
    def finish(fresh):
        current[...] = solved(staged[...] - fresh, inverse)

    product(lax.axis_index("lag") == 0, high, low_hbm, arrived, low, total, sems, finish)


def partial_kernel(high, low_hbm, arrived, staged, after, partial, low, total, sems):
    del after

    def finish(fresh):
        partial[...] = staged[...] + fresh

    product(lax.axis_index("lag") > 0, high, low_hbm, arrived, low, total, sems, finish)


def asked_kernel(table, asked, copy_of, sem):
    started((table, copy_of, sem))[0].wait()
    for q in range(table.shape[0]):
        asked[q] = jnp.maximum(copy_of[q, 0, 0], 0)


def ahead_kernel(high, arrived, field, ahead_hbm, ahead, sems):
    patches, size, columns = arrived.shape
    rows = ahead.shape[0] // sems.shape[0]
    copies = []
    for part in range(sems.shape[0]):
        here = pl.ds(part * rows, rows)
        flat = arrived[...].reshape(patches * size, columns)
        fresh = jnp.dot(high[here, :], flat, preferred_element_type=jnp.float32)
        ahead[here, :] = field[here, :] + fresh
        copies += started((ahead.at[here], ahead_hbm.at[here], sems.at[part]))
    for copy in copies:
        copy.wait()


def pack_kernel(step, keeps, early, asked, current, *refs):
    outgoing, currents, sems = refs[-3:]
    patches, size, _ = outgoing.shape
    section = lax.axis_index("lag")

    @pl.when(section < keeps if early else section >= keeps)
    def _():
        for q in range(patches):
            block = asked[q] if len(asked.shape) == 1 else jnp.max(jnp.maximum(asked[q], 0))
            start = pl.multiple_of(block * size, size)
            started((current.at[pl.ds(start, size)], outgoing.at[q], sems.at[0]))
        (kept_copy,) = started((current, currents.at[step], sems.at[1]))
        pltpu.make_async_copy(outgoing, outgoing, sems.at[0]).wait()
        kept_copy.wait()


def first_pack_kernel(step, keeps, asked, own, received, outgoing, currents, sems):
    pack_kernel(step, keeps, True, asked, own, outgoing, currents, sems)
    pack_kernel(step, keeps, False, asked, received, outgoing, currents, sems)


def shifted(x):
    sections = lax.axis_size("lag")
    return lax.ppermute(x, "lag", [(i, i - 1) for i in range(1, sections)])


def spread(x):
    sections = lax.axis_size("lag")
    section = lax.axis_index("lag")
    received, keeps = x, 1
    while keeps < sections:
        if keeps > 1:
            x = jnp.where(section < keeps // 2, x, received)
        pairs = [(i, i + keeps) for i in range(keeps) if i + keeps < sections]
        received = lax.ppermute(x, "lag", pairs)
        keeps *= 2
    return x, received, max(keeps // 2, 1)


def body(incident, pending, self_inverse, retarded, block_rows, block_sources, owner_map):
    steps, unknowns, columns = incident.shape
    per_patch, size, _ = self_inverse.shape
    listed = retarded.shape[2]
    patches = lax.axis_size("patch")
    bf16, f32 = jnp.bfloat16, jnp.float32
    all_flops = 4 * unknowns * patches * size * columns
    solve_flops = 12 * unknowns * size * columns
    panel_bytes = 4 * unknowns * patches * size
    column = (unknowns, columns)
    arrived_bytes = 2 * patches * size * columns

    def exchange(x):
        order = [patch_in(slot, patches) for slot in range(patches)]
        return lax.all_to_all(
            x, "patch", split_axis=0, concat_axis=0, axis_index_groups=[order], tiled=True
        )

    def pack(step, keeps, early, current, filled, after=()):
        held = [x for x in filled if x is not None]
        aliases = {}
        for out, x in enumerate(filled):
            if x is not None:
                aliases[2 + len(after) + len(aliases)] = out
        return call(
            lambda *refs: pack_kernel(step, keeps, early, *refs),
            [(HBM, (patches, size, columns), bf16), (HBM, incident.shape, bf16)],
            [(SMEM, asked), (VMEM, current)] + [(VMEM, x) for x in after] + [(HBM, x) for x in held],
            [DMA((2,))],
            aliases=aliases,
        )

    table = [(HBM, (patches, 1, 128), jnp.int32)]
    lists = [(HBM, block_sources[0]), (HBM, owner_map[None])]
    list_scratch = [
        pltpu.VMEM((patches, 1, 128), jnp.int32),
        pltpu.VMEM(block_sources.shape[1:], jnp.int32),
        pltpu.VMEM((1, owner_map.shape[0]), jnp.int32),
    ]
    wanted, current = call(
        lambda *refs: first_kernel(per_patch, *refs),
        [*table, (VMEM, column, bf16)],
        [*lists, (HBM, incident), (HBM, pending[0]), (HBM, self_inverse)],
        [
            *list_scratch,
            pltpu.VMEM(column, bf16),
            pltpu.VMEM(column, f32),
            pltpu.VMEM(self_inverse.shape, f32),
            DMA((5,)),
        ],
        solve_flops,
    )
    if lax.axis_size("lag") > 1:
        wanted = call(
            lambda *refs: request_kernel(per_patch, *refs),
            table,
            [*lists, (HBM, wanted), (VMEM, current)],
            [*list_scratch, DMA((2,))],
            aliases={2: 0},
        )
    requests = exchange(wanted)
    asked = call(
        asked_kernel,
        [(SMEM, (patches,), jnp.int32)],
        [(VMEM, requests)],
        [pltpu.SMEM(wanted.shape, jnp.int32), DMA],
    )
    chunk = max(n for n in range(1, 9) if listed % n == 0)
    panel = (unknowns, patches * size)
    pieces = 4 if patches % 4 == 0 else 1
    low_panel = (pieces, unknowns, patches * size // pieces)
    high, low, inverse = call(
        lambda *refs: panel_kernel(per_patch, *refs),
        [(VMEM, panel, bf16), (HBM, low_panel, bf16), (VMEM, self_inverse.shape, f32)],
        [(HBM, block_rows), (HBM, block_sources), (HBM, owner_map), (HBM, retarded), (HBM, self_inverse)],
        [
            pltpu.SMEM(block_rows.shape, jnp.int32),
            pltpu.SMEM(block_sources.shape, jnp.int32),
            pltpu.SMEM(owner_map.shape, jnp.int32),
            pltpu.VMEM((3, chunk, size, size), f32),
            pltpu.VMEM(low_panel, bf16),
            DMA((7,)),
        ],
        nbytes=listed * size * size * 4 + panel_bytes,
        vmem=panel_bytes // 2,
    )

    field = pending[0]
    currents = None
    for step in range(steps):
        own, received, keeps = spread(current)
        if step == 0:
            outgoing, currents = call(
                lambda *refs: first_pack_kernel(0, keeps, *refs),
                [(HBM, (patches, size, columns), bf16), (HBM, incident.shape, bf16)],
                [(VMEM, requests), (VMEM, own), (VMEM, received)],
                [DMA((2,))],
            )
        else:
            outgoing, currents = pack(step, keeps, True, own, (None, currents))
            if lax.axis_size("lag") > 1:
                outgoing, currents = pack(step, keeps, False, received, (outgoing, currents), [field])
        arrived = exchange(outgoing)
        field = shifted(field)
        if step + 1 < steps:
            staged = call(
                lambda *refs, n=step + 1: stage_kernel(n, *refs),
                [(VMEM, column, f32)],
                [(HBM, incident), (VMEM, field)],
                [pltpu.VMEM(column, bf16), DMA],
            )
            shared = [(VMEM, high), (HBM, low), (VMEM, arrived), (VMEM, staged)]
            scratch = [pltpu.VMEM(low_panel, bf16), pltpu.VMEM(column, f32), DMA((pieces,))]
            sizes = [all_flops, panel_bytes + arrived_bytes, panel_bytes + arrived_bytes]
            current = call(
                solve_kernel, [(VMEM, column, bf16)], [*shared, (VMEM, inverse)], scratch, *sizes
            )
            field = call(
                partial_kernel, [(VMEM, column, f32)], [*shared, (VMEM, current)], scratch, *sizes
            )
        else:
            field = call(
                ahead_kernel,
                [(HBM, column, f32)],
                [(VMEM, high), (VMEM, arrived), (VMEM, field)],
                [pltpu.VMEM(column, f32), DMA((2,))],
                all_flops,
                panel_bytes + arrived_bytes,
                panel_bytes + arrived_bytes,
            )
    return currents, field[None]


def solution(mesh):
    in_specs = (
        P(None, "patch", None),
        P("lag", "patch", None),
        P("patch", None, None),
        P("lag", "patch", None, None, None),
        P("lag", "patch", None),
        P("lag", "patch", None),
        P(),
    )
    out_specs = (P(None, "patch", None), P("lag", "patch", None))
    return jax.shard_map(body, mesh=mesh, in_specs=in_specs, out_specs=out_specs, check_vma=False)
```

```python
import jax
import jax.numpy as jnp
from jax import lax
from jax.experimental import pallas as pl
from jax.experimental.pallas import tpu as pltpu
from jax.sharding import PartitionSpec as P

VMEM, SMEM, HBM = pltpu.VMEM, pltpu.SMEM, pltpu.HBM
DMA = pltpu.SemaphoreType.DMA
MIB = 1 << 20


def call(kernel, outs, ins, scratch=(), flops=0, nbytes=0, vmem=0, aliases=None):
    out_shape = tuple(space(dims, dtype) for space, dims, dtype in outs)
    out_specs = tuple(pl.BlockSpec(memory_space=space) for space, _, _ in outs)
    run = pl.pallas_call(
        kernel,
        out_shape=out_shape,
        in_specs=[pl.BlockSpec(memory_space=space) for space, _ in ins],
        out_specs=out_specs,
        scratch_shapes=scratch,
        input_output_aliases=aliases or {},
        cost_estimate=pl.CostEstimate(flops=flops, bytes_accessed=nbytes, transcendentals=0),
        compiler_params=pltpu.CompilerParams(vmem_limit_bytes=vmem + 6 * MIB),
    )
    results = run(*(pltpu.with_memory_space_constraint(x, space) for space, x in ins))
    return results if len(outs) > 1 else results[0]


def started(*copies):
    copies = [pltpu.make_async_copy(*copy) for copy in copies]
    for copy in copies:
        copy.start()
    return copies


def requests_into(wanted, per_patch, sources, owner_map):
    patches, _, lanes = wanted.shape
    blocks = owner_map.shape[1]

    def numbered(dims, axis):
        return lax.broadcasted_iota(jnp.int32, dims, axis)

    source = sources[...]
    square = (blocks, blocks)
    on_diagonal = numbered(square, 0) == numbered(square, 1)
    owners = jnp.max(jnp.where(on_diagonal, owner_map[...], 0), axis=1, keepdims=True)
    looked_up = numbered((blocks, source.shape[1]), 0) == source
    storage = jnp.max(jnp.where(looked_up, owners, -1), axis=0, keepdims=True)
    patch = numbered((patches, source.shape[1]), 0)
    here = (storage >= patch * per_patch) & (storage < (patch + 1) * per_patch)
    table = jnp.max(jnp.where(here, storage - patch * per_patch, -1), axis=1, keepdims=True)
    for q in range(patches):
        wanted[q] = jnp.broadcast_to(table[q : q + 1], (1, lanes))


def first_kernel(
    per_patch,
    sources_hbm,
    owner_hbm,
    incident_hbm,
    field_hbm,
    inverse_hbm,
    wanted_hbm,
    current,
    wanted,
    sources,
    owner_map,
    incident,
    field,
    inverse,
    sems,
):
    @pl.when(lax.axis_index("lag") == 0)
    def _():
        lists = started(
            (sources_hbm, sources, sems.at[0]),
            (owner_hbm, owner_map, sems.at[1]),
        )
        arrays = started(
            (incident_hbm.at[0], incident, sems.at[2]),
            (inverse_hbm, inverse, sems.at[3]),
            (field_hbm, field, sems.at[4]),
        )
        for copy in lists:
            copy.wait()
        requests_into(wanted, per_patch, sources, owner_map)
        (done,) = started((wanted, wanted_hbm, sems.at[0]))
        for copy in arrays:
            copy.wait()
        current[...] = solved(incident[...].astype(jnp.float32) - field[...], inverse)
        done.wait()


def request_kernel(
    per_patch, sources_hbm, owner_hbm, held, after, wanted_hbm, wanted, sources, owner_map, sems
):
    del held, after

    @pl.when(lax.axis_index("lag") > 0)
    def _():
        lists = started(
            (sources_hbm, sources, sems.at[0]),
            (owner_hbm, owner_map, sems.at[1]),
        )
        for copy in lists:
            copy.wait()
        requests_into(wanted, per_patch, sources, owner_map)
        started((wanted, wanted_hbm, sems.at[0]))[0].wait()


def panel_kernel(
    per_patch,
    rows_hbm,
    sources_hbm,
    owner_hbm,
    retarded,
    inverse_hbm,
    high,
    low_hbm,
    inverse,
    rows,
    sources,
    owner_map,
    parts,
    low,
    sems,
):
    size = retarded.shape[-1]
    slots, chunk = parts.shape[:2]
    chunks = retarded.shape[2] // chunk

    def fetch(c):
        part = retarded.at[0, 0, pl.ds(c * chunk, chunk)]
        return pltpu.make_async_copy(part, parts.at[c % slots], sems.at[c % slots])

    lists = started(
        (rows_hbm, rows, sems.at[slots]),
        (sources_hbm, sources, sems.at[slots + 1]),
        (owner_hbm, owner_map, sems.at[slots + 2]),
        (inverse_hbm, inverse, sems.at[slots + 3]),
    )
    for c in range(min(slots, chunks)):
        fetch(c).start()
    high[...] = jnp.zeros_like(high)
    low[...] = jnp.zeros_like(low)
    for copy in lists:
        copy.wait()

    def entry(c, k, carry):
        source = sources[0, 0, c * chunk + k]

        @pl.when(source >= 0)
        def _():
            owner = owner_map[source] // per_patch
            row = pl.multiple_of(rows[0, 0, c * chunk + k] * size, size)
            column = pl.multiple_of(owner * size, size)
            block = parts[c % slots, k]
            rounded = block.astype(high.dtype)
            rest = (block - rounded.astype(jnp.float32)).astype(low.dtype)
            high[pl.ds(row, size), pl.ds(column, size)] = rounded
            piece = column // low.shape[2]
            inside = pl.multiple_of(column - piece * low.shape[2], size)
            low[piece, pl.ds(row, size), pl.ds(inside, size)] = rest

        return carry

    for c in range(chunks):
        fetch(c).wait()
        lax.fori_loop(0, chunk, lambda k, carry, c=c: entry(c, k, carry), 0)
        if c + slots < chunks:
            fetch(c + slots).start()
    started((low, low_hbm, sems.at[0]))[0].wait()


def solved(excess, self_inverse):
    blocks, size, _ = self_inverse.shape
    parts = [
        jnp.dot(
            self_inverse[k],
            excess[k * size : (k + 1) * size],
            precision=lax.Precision.HIGHEST,
            preferred_element_type=jnp.float32,
        )
        for k in range(blocks)
    ]
    return jnp.concatenate(parts, axis=0).astype(jnp.bfloat16)


def product(here, high, low_hbm, arrived, low, total, sems, finish):
    patches, size, columns = arrived.shape
    pieces, _, depth = low.shape
    copies = [pltpu.make_async_copy(low_hbm.at[k], low.at[k], sems.at[k]) for k in range(pieces)]

    @pl.when(here)
    def _():
        for copy in copies:
            copy.start()
        rows = total.shape[0] // 2

        def half(part, carry):
            flat = arrived[...].reshape(patches * size, columns)
            mine = pl.ds(pl.multiple_of(part * rows, rows), rows)
            total[mine, :] = jnp.dot(high[mine, :], flat, preferred_element_type=jnp.float32)
            return carry

        lax.fori_loop(0, 2, half, 0)
        fresh = total[...]
        flat = arrived[...].reshape(patches * size, columns)
        for k, copy in enumerate(copies):
            copy.wait()
            part = flat[k * depth : (k + 1) * depth]
            fresh = fresh + jnp.dot(low[k], part, preferred_element_type=jnp.float32)
        finish(fresh)


def stage_kernel(step, incident_hbm, field, staged, incident, sem):
    first = lax.axis_index("lag") == 0

    @pl.when(first)
    def _():
        started((incident_hbm.at[step], incident, sem))[0].wait()
        staged[...] = incident[...].astype(jnp.float32) - field[...]

    @pl.when(jnp.logical_not(first))
    def _():
        staged[...] = field[...]


def solve_kernel(high, low_hbm, arrived, staged, inverse, current, low, total, sems):
    def finish(fresh):
        current[...] = solved(staged[...] - fresh, inverse)

    product(lax.axis_index("lag") == 0, high, low_hbm, arrived, low, total, sems, finish)


def partial_kernel(high, low_hbm, arrived, staged, after, partial, low, total, sems):
    del after

    def finish(fresh):
        partial[...] = staged[...] + fresh

    product(lax.axis_index("lag") > 0, high, low_hbm, arrived, low, total, sems, finish)


def asked_kernel(table, asked, copy_of, sem):
    started((table, copy_of, sem))[0].wait()
    for q in range(table.shape[0]):
        asked[q] = jnp.maximum(copy_of[q, 0, 0], 0)


def ahead_kernel(high, arrived, field, ahead_hbm, ahead, sems):
    patches, size, columns = arrived.shape
    rows = ahead.shape[0] // sems.shape[0]
    copies = []
    for part in range(sems.shape[0]):
        here = pl.ds(part * rows, rows)
        flat = arrived[...].reshape(patches * size, columns)
        fresh = jnp.dot(high[here, :], flat, preferred_element_type=jnp.float32)
        ahead[here, :] = field[here, :] + fresh
        copies += started((ahead.at[here], ahead_hbm.at[here], sems.at[part]))
    for copy in copies:
        copy.wait()


def pack_kernel(step, keeps, early, asked, current, *refs):
    outgoing, currents, sems = refs[-3:]
    patches, size, _ = outgoing.shape
    section = lax.axis_index("lag")

    @pl.when(section < keeps if early else section >= keeps)
    def _():
        for q in range(patches):
            block = asked[q] if len(asked.shape) == 1 else jnp.maximum(asked[q][0, 0], 0)
            start = pl.multiple_of(block * size, size)
            started((current.at[pl.ds(start, size)], outgoing.at[q], sems.at[0]))
        (kept_copy,) = started((current, currents.at[step], sems.at[1]))
        pltpu.make_async_copy(outgoing, outgoing, sems.at[0]).wait()
        kept_copy.wait()


def first_pack_kernel(step, keeps, asked, own, received, outgoing, currents, sems):
    pack_kernel(step, keeps, True, asked, own, outgoing, currents, sems)
    pack_kernel(step, keeps, False, asked, received, outgoing, currents, sems)


def shifted(x):
    sections = lax.axis_size("lag")
    return lax.ppermute(x, "lag", [(i, i - 1) for i in range(1, sections)])


def spread(x):
    sections = lax.axis_size("lag")
    section = lax.axis_index("lag")
    received, keeps = x, 1
    while keeps < sections:
        if keeps > 1:
            x = jnp.where(section < keeps // 2, x, received)
        pairs = [(i, i + keeps) for i in range(keeps) if i + keeps < sections]
        received = lax.ppermute(x, "lag", pairs)
        keeps *= 2
    return x, received, max(keeps // 2, 1)


def body(incident, pending, self_inverse, retarded, block_rows, block_sources, owner_map):
    steps, unknowns, columns = incident.shape
    per_patch, size, _ = self_inverse.shape
    listed = retarded.shape[2]
    patches = lax.axis_size("patch")
    bf16, f32 = jnp.bfloat16, jnp.float32
    all_flops = 4 * unknowns * patches * size * columns
    solve_flops = 12 * unknowns * size * columns
    panel_bytes = 4 * unknowns * patches * size
    column = (unknowns, columns)
    arrived_bytes = 2 * patches * size * columns

    def exchange(x):
        return lax.all_to_all(x, "patch", split_axis=0, concat_axis=0, tiled=True)

    def pack(step, keeps, early, current, filled, after=()):
        held = [x for x in filled if x is not None]
        aliases = {}
        for out, x in enumerate(filled):
            if x is not None:
                aliases[2 + len(after) + len(aliases)] = out
        return call(
            lambda *refs: pack_kernel(step, keeps, early, *refs),
            [(HBM, (patches, size, columns), bf16), (HBM, incident.shape, bf16)],
            [(SMEM, asked), (VMEM, current)] + [(VMEM, x) for x in after] + [(HBM, x) for x in held],
            [DMA((2,))],
            aliases=aliases,
        )

    table = [(HBM, (patches, 1, 128), jnp.int32)]
    lists = [(HBM, block_sources[0]), (HBM, owner_map[None])]
    list_scratch = [
        pltpu.VMEM((patches, 1, 128), jnp.int32),
        pltpu.VMEM(block_sources.shape[1:], jnp.int32),
        pltpu.VMEM((1, owner_map.shape[0]), jnp.int32),
    ]
    wanted, current = call(
        lambda *refs: first_kernel(per_patch, *refs),
        [*table, (VMEM, column, bf16)],
        [*lists, (HBM, incident), (HBM, pending[0]), (HBM, self_inverse)],
        [
            *list_scratch,
            pltpu.VMEM(column, bf16),
            pltpu.VMEM(column, f32),
            pltpu.VMEM(self_inverse.shape, f32),
            DMA((5,)),
        ],
        solve_flops,
    )
    if lax.axis_size("lag") > 1:
        wanted = call(
            lambda *refs: request_kernel(per_patch, *refs),
            table,
            [*lists, (HBM, wanted), (VMEM, current)],
            [*list_scratch, DMA((2,))],
            aliases={2: 0},
        )
    requests = exchange(wanted)
    asked = call(
        asked_kernel,
        [(SMEM, (patches,), jnp.int32)],
        [(VMEM, requests)],
        [pltpu.SMEM(wanted.shape, jnp.int32), DMA],
    )
    chunk = max(n for n in range(1, 9) if listed % n == 0)
    panel = (unknowns, patches * size)
    pieces = 4 if patches % 4 == 0 else 1
    low_panel = (pieces, unknowns, patches * size // pieces)
    high, low, inverse = call(
        lambda *refs: panel_kernel(per_patch, *refs),
        [(VMEM, panel, bf16), (HBM, low_panel, bf16), (VMEM, self_inverse.shape, f32)],
        [(HBM, block_rows), (HBM, block_sources), (HBM, owner_map), (HBM, retarded), (HBM, self_inverse)],
        [
            pltpu.SMEM(block_rows.shape, jnp.int32),
            pltpu.SMEM(block_sources.shape, jnp.int32),
            pltpu.SMEM(owner_map.shape, jnp.int32),
            pltpu.VMEM((3, chunk, size, size), f32),
            pltpu.VMEM(low_panel, bf16),
            DMA((7,)),
        ],
        nbytes=listed * size * size * 4 + panel_bytes,
        vmem=panel_bytes // 2,
    )

    field = pending[0]
    currents = None
    for step in range(steps):
        own, received, keeps = spread(current)
        if step == 0:
            outgoing, currents = call(
                lambda *refs: first_pack_kernel(0, keeps, *refs),
                [(HBM, (patches, size, columns), bf16), (HBM, incident.shape, bf16)],
                [(VMEM, requests), (VMEM, own), (VMEM, received)],
                [DMA((2,))],
            )
        else:
            outgoing, currents = pack(step, keeps, True, own, (None, currents))
            if lax.axis_size("lag") > 1:
                outgoing, currents = pack(step, keeps, False, received, (outgoing, currents), [field])
        arrived = exchange(outgoing)
        field = shifted(field)
        if step + 1 < steps:
            staged = call(
                lambda *refs, n=step + 1: stage_kernel(n, *refs),
                [(VMEM, column, f32)],
                [(HBM, incident), (VMEM, field)],
                [pltpu.VMEM(column, bf16), DMA],
            )
            shared = [(VMEM, high), (HBM, low), (VMEM, arrived), (VMEM, staged)]
            scratch = [pltpu.VMEM(low_panel, bf16), pltpu.VMEM(column, f32), DMA((pieces,))]
            sizes = [all_flops, panel_bytes + arrived_bytes, panel_bytes + arrived_bytes]
            current = call(
                solve_kernel, [(VMEM, column, bf16)], [*shared, (VMEM, inverse)], scratch, *sizes
            )
            field = call(
                partial_kernel, [(VMEM, column, f32)], [*shared, (VMEM, current)], scratch, *sizes
            )
        else:
            field = call(
                ahead_kernel,
                [(HBM, column, f32)],
                [(VMEM, high), (VMEM, arrived), (VMEM, field)],
                [pltpu.VMEM(column, f32), DMA((2,))],
                all_flops,
                panel_bytes + arrived_bytes,
                panel_bytes + arrived_bytes,
            )
    return currents, field[None]


def solution(mesh):
    in_specs = (
        P(None, "patch", None),
        P("lag", "patch", None),
        P("patch", None, None),
        P("lag", "patch", None, None, None),
        P("lag", "patch", None),
        P("lag", "patch", None),
        P(),
    )
    out_specs = (P(None, "patch", None), P("lag", "patch", None))
    return jax.shard_map(body, mesh=mesh, in_specs=in_specs, out_specs=out_specs, check_vma=False)
```

```python
import jax
import jax.numpy as jnp
from jax import lax
from jax.experimental import pallas as pl
from jax.experimental.pallas import tpu as pltpu
from jax.sharding import PartitionSpec as P

VMEM, SMEM, HBM = pltpu.VMEM, pltpu.SMEM, pltpu.HBM
DMA = pltpu.SemaphoreType.DMA
MIB = 1 << 20


def call(kernel, outs, ins, scratch=(), flops=0, nbytes=0, vmem=0, aliases=None):
    out_shape = tuple(space(dims, dtype) for space, dims, dtype in outs)
    out_specs = tuple(pl.BlockSpec(memory_space=space) for space, _, _ in outs)
    run = pl.pallas_call(
        kernel,
        out_shape=out_shape,
        in_specs=[pl.BlockSpec(memory_space=space) for space, _ in ins],
        out_specs=out_specs,
        scratch_shapes=scratch,
        input_output_aliases=aliases or {},
        cost_estimate=pl.CostEstimate(flops=flops, bytes_accessed=nbytes, transcendentals=0),
        compiler_params=pltpu.CompilerParams(vmem_limit_bytes=vmem + 6 * MIB),
    )
    results = run(*(pltpu.with_memory_space_constraint(x, space) for space, x in ins))
    return results if len(outs) > 1 else results[0]


def started(*copies):
    copies = [pltpu.make_async_copy(*copy) for copy in copies]
    for copy in copies:
        copy.start()
    return copies


def requests_into(wanted, per_patch, sources, owner_map):
    patches, _, lanes = wanted.shape
    blocks = owner_map.shape[1]

    def numbered(dims, axis):
        return lax.broadcasted_iota(jnp.int32, dims, axis)

    source = sources[...]
    square = (blocks, blocks)
    on_diagonal = numbered(square, 0) == numbered(square, 1)
    owners = jnp.max(jnp.where(on_diagonal, owner_map[...], 0), axis=1, keepdims=True)
    looked_up = numbered((blocks, source.shape[1]), 0) == source
    storage = jnp.max(jnp.where(looked_up, owners, -1), axis=0, keepdims=True)
    patch = numbered((patches, source.shape[1]), 0)
    here = (storage >= patch * per_patch) & (storage < (patch + 1) * per_patch)
    table = jnp.max(jnp.where(here, storage - patch * per_patch, -1), axis=1, keepdims=True)
    for q in range(patches):
        wanted[q] = jnp.broadcast_to(table[q : q + 1], (1, lanes))


def first_kernel(
    per_patch,
    sources_hbm,
    owner_hbm,
    incident_hbm,
    field_hbm,
    inverse_hbm,
    wanted_hbm,
    current,
    wanted,
    sources,
    owner_map,
    incident,
    field,
    inverse,
    sems,
):
    @pl.when(lax.axis_index("lag") == 0)
    def _():
        lists = started(
            (sources_hbm, sources, sems.at[0]),
            (owner_hbm, owner_map, sems.at[1]),
        )
        arrays = started(
            (incident_hbm.at[0], incident, sems.at[2]),
            (inverse_hbm, inverse, sems.at[3]),
            (field_hbm, field, sems.at[4]),
        )
        for copy in lists:
            copy.wait()
        requests_into(wanted, per_patch, sources, owner_map)
        (done,) = started((wanted, wanted_hbm, sems.at[0]))
        for copy in arrays:
            copy.wait()
        current[...] = solved(incident[...].astype(jnp.float32) - field[...], inverse)
        done.wait()


def request_kernel(
    per_patch, sources_hbm, owner_hbm, held, after, wanted_hbm, wanted, sources, owner_map, sems
):
    del held, after

    @pl.when(lax.axis_index("lag") > 0)
    def _():
        lists = started(
            (sources_hbm, sources, sems.at[0]),
            (owner_hbm, owner_map, sems.at[1]),
        )
        for copy in lists:
            copy.wait()
        requests_into(wanted, per_patch, sources, owner_map)
        started((wanted, wanted_hbm, sems.at[0]))[0].wait()


def panel_kernel(
    per_patch,
    rows_hbm,
    sources_hbm,
    owner_hbm,
    retarded,
    inverse_hbm,
    high,
    low_hbm,
    inverse,
    rows,
    sources,
    owner_map,
    parts,
    low,
    sems,
):
    size = retarded.shape[-1]
    slots, chunk = parts.shape[:2]
    chunks = retarded.shape[2] // chunk

    def fetch(c):
        part = retarded.at[0, 0, pl.ds(c * chunk, chunk)]
        return pltpu.make_async_copy(part, parts.at[c % slots], sems.at[c % slots])

    lists = started(
        (rows_hbm, rows, sems.at[slots]),
        (sources_hbm, sources, sems.at[slots + 1]),
        (owner_hbm, owner_map, sems.at[slots + 2]),
        (inverse_hbm, inverse, sems.at[slots + 3]),
    )
    for c in range(min(slots, chunks)):
        fetch(c).start()
    high[...] = jnp.zeros_like(high)
    low[...] = jnp.zeros_like(low)
    for copy in lists:
        copy.wait()

    def entry(c, k, carry):
        source = sources[0, 0, c * chunk + k]

        @pl.when(source >= 0)
        def _():
            owner = owner_map[source] // per_patch
            row = pl.multiple_of(rows[0, 0, c * chunk + k] * size, size)
            column = pl.multiple_of(owner * size, size)
            block = parts[c % slots, k]
            rounded = block.astype(high.dtype)
            rest = (block - rounded.astype(jnp.float32)).astype(low.dtype)
            high[pl.ds(row, size), pl.ds(column, size)] = rounded
            piece = column // low.shape[2]
            inside = pl.multiple_of(column - piece * low.shape[2], size)
            low[piece, pl.ds(row, size), pl.ds(inside, size)] = rest

        return carry

    for c in range(chunks):
        fetch(c).wait()
        lax.fori_loop(0, chunk, lambda k, carry, c=c: entry(c, k, carry), 0)
        if c + slots < chunks:
            fetch(c + slots).start()
    started((low, low_hbm, sems.at[0]))[0].wait()


def solved(excess, self_inverse):
    blocks, size, _ = self_inverse.shape
    parts = [
        jnp.dot(
            self_inverse[k],
            excess[k * size : (k + 1) * size],
            precision=lax.Precision.HIGHEST,
            preferred_element_type=jnp.float32,
        )
        for k in range(blocks)
    ]
    return jnp.concatenate(parts, axis=0).astype(jnp.bfloat16)


def product(here, high, low_hbm, arrived, low, total, sems, finish):
    patches, size, columns = arrived.shape
    pieces, _, depth = low.shape
    copies = [pltpu.make_async_copy(low_hbm.at[k], low.at[k], sems.at[k]) for k in range(pieces)]

    @pl.when(here)
    def _():
        for copy in copies:
            copy.start()
        rows = total.shape[0] // 2

        def half(part, carry):
            flat = arrived[...].reshape(patches * size, columns)
            mine = pl.ds(pl.multiple_of(part * rows, rows), rows)
            total[mine, :] = jnp.dot(high[mine, :], flat, preferred_element_type=jnp.float32)
            return carry

        lax.fori_loop(0, 2, half, 0)
        fresh = total[...]
        flat = arrived[...].reshape(patches * size, columns)
        for k, copy in enumerate(copies):
            copy.wait()
            part = flat[k * depth : (k + 1) * depth]
            fresh = fresh + jnp.dot(low[k], part, preferred_element_type=jnp.float32)
        finish(fresh)


def stage_kernel(step, incident_hbm, field, staged, incident, sem):
    first = lax.axis_index("lag") == 0

    @pl.when(first)
    def _():
        started((incident_hbm.at[step], incident, sem))[0].wait()
        staged[...] = incident[...].astype(jnp.float32) - field[...]

    @pl.when(jnp.logical_not(first))
    def _():
        staged[...] = field[...]


def solve_kernel(high, low_hbm, arrived, staged, inverse, current, low, total, sems):
    def finish(fresh):
        current[...] = solved(staged[...] - fresh, inverse)

    product(lax.axis_index("lag") == 0, high, low_hbm, arrived, low, total, sems, finish)


def partial_kernel(high, low_hbm, arrived, staged, after, partial, low, total, sems):
    del after

    def finish(fresh):
        partial[...] = staged[...] + fresh

    product(lax.axis_index("lag") > 0, high, low_hbm, arrived, low, total, sems, finish)


def asked_kernel(table, asked, copy_of, sem):
    started((table, copy_of, sem))[0].wait()
    for q in range(table.shape[0]):
        asked[q] = jnp.maximum(copy_of[q, 0, 0], 0)


def ahead_kernel(high, arrived, field, ahead_hbm, ahead, sems):
    patches, size, columns = arrived.shape
    rows = ahead.shape[0] // sems.shape[0]
    copies = []
    for part in range(sems.shape[0]):
        here = pl.ds(part * rows, rows)
        flat = arrived[...].reshape(patches * size, columns)
        fresh = jnp.dot(high[here, :], flat, preferred_element_type=jnp.float32)
        ahead[here, :] = field[here, :] + fresh
        copies += started((ahead.at[here], ahead_hbm.at[here], sems.at[part]))
    for copy in copies:
        copy.wait()


def pack_kernel(step, keeps, early, asked, current, *refs):
    outgoing, currents, sems = refs[-3:]
    patches, size, _ = outgoing.shape
    section = lax.axis_index("lag")

    @pl.when(section < keeps if early else section >= keeps)
    def _():
        for q in range(patches):
            block = asked[q] if len(asked.shape) == 1 else jnp.max(jnp.maximum(asked[q], 0))
            start = pl.multiple_of(block * size, size)
            started((current.at[pl.ds(start, size)], outgoing.at[q], sems.at[0]))
        (kept_copy,) = started((current, currents.at[step], sems.at[1]))
        pltpu.make_async_copy(outgoing, outgoing, sems.at[0]).wait()
        kept_copy.wait()


def first_pack_kernel(step, keeps, asked, own, received, outgoing, currents, sems):
    pack_kernel(step, keeps, True, asked, own, outgoing, currents, sems)
    pack_kernel(step, keeps, False, asked, received, outgoing, currents, sems)


def shifted(x):
    sections = lax.axis_size("lag")
    return lax.ppermute(x, "lag", [(i, i - 1) for i in range(1, sections)])


def spread(x):
    sections = lax.axis_size("lag")
    section = lax.axis_index("lag")
    received, keeps = x, 1
    while keeps < sections:
        if keeps > 1:
            x = jnp.where(section < keeps // 2, x, received)
        pairs = [(i, i + keeps) for i in range(keeps) if i + keeps < sections]
        received = lax.ppermute(x, "lag", pairs)
        keeps *= 2
    return x, received, max(keeps // 2, 1)


def body(incident, pending, self_inverse, retarded, block_rows, block_sources, owner_map):
    steps, unknowns, columns = incident.shape
    per_patch, size, _ = self_inverse.shape
    listed = retarded.shape[2]
    patches = lax.axis_size("patch")
    bf16, f32 = jnp.bfloat16, jnp.float32
    all_flops = 4 * unknowns * patches * size * columns
    solve_flops = 12 * unknowns * size * columns
    panel_bytes = 4 * unknowns * patches * size
    column = (unknowns, columns)
    arrived_bytes = 2 * patches * size * columns

    def exchange(x):
        return lax.all_to_all(x, "patch", split_axis=0, concat_axis=0, tiled=True)

    def pack(step, keeps, early, current, filled, after=()):
        held = [x for x in filled if x is not None]
        aliases = {}
        for out, x in enumerate(filled):
            if x is not None:
                aliases[2 + len(after) + len(aliases)] = out
        return call(
            lambda *refs: pack_kernel(step, keeps, early, *refs),
            [(HBM, (patches, size, columns), bf16), (HBM, incident.shape, bf16)],
            [(SMEM, asked), (VMEM, current)] + [(VMEM, x) for x in after] + [(HBM, x) for x in held],
            [DMA((2,))],
            aliases=aliases,
        )

    table = [(HBM, (patches, 1, 128), jnp.int32)]
    lists = [(HBM, block_sources[0]), (HBM, owner_map[None])]
    list_scratch = [
        pltpu.VMEM((patches, 1, 128), jnp.int32),
        pltpu.VMEM(block_sources.shape[1:], jnp.int32),
        pltpu.VMEM((1, owner_map.shape[0]), jnp.int32),
    ]
    wanted, current = call(
        lambda *refs: first_kernel(per_patch, *refs),
        [*table, (VMEM, column, bf16)],
        [*lists, (HBM, incident), (HBM, pending[0]), (HBM, self_inverse)],
        [
            *list_scratch,
            pltpu.VMEM(column, bf16),
            pltpu.VMEM(column, f32),
            pltpu.VMEM(self_inverse.shape, f32),
            DMA((5,)),
        ],
        solve_flops,
    )
    if lax.axis_size("lag") > 1:
        wanted = call(
            lambda *refs: request_kernel(per_patch, *refs),
            table,
            [*lists, (HBM, wanted), (VMEM, current)],
            [*list_scratch, DMA((2,))],
            aliases={2: 0},
        )
    requests = exchange(wanted)
    asked = call(
        asked_kernel,
        [(SMEM, (patches,), jnp.int32)],
        [(VMEM, requests)],
        [pltpu.SMEM(wanted.shape, jnp.int32), DMA],
    )
    chunk = max(n for n in range(1, 9) if listed % n == 0)
    panel = (unknowns, patches * size)
    pieces = 8 if patches % 8 == 0 else 1
    low_panel = (pieces, unknowns, patches * size // pieces)
    high, low, inverse = call(
        lambda *refs: panel_kernel(per_patch, *refs),
        [(VMEM, panel, bf16), (HBM, low_panel, bf16), (VMEM, self_inverse.shape, f32)],
        [(HBM, block_rows), (HBM, block_sources), (HBM, owner_map), (HBM, retarded), (HBM, self_inverse)],
        [
            pltpu.SMEM(block_rows.shape, jnp.int32),
            pltpu.SMEM(block_sources.shape, jnp.int32),
            pltpu.SMEM(owner_map.shape, jnp.int32),
            pltpu.VMEM((3, chunk, size, size), f32),
            pltpu.VMEM(low_panel, bf16),
            DMA((7,)),
        ],
        nbytes=listed * size * size * 4 + panel_bytes,
        vmem=panel_bytes // 2,
    )

    field = pending[0]
    currents = None
    for step in range(steps):
        own, received, keeps = spread(current)
        if step == 0:
            outgoing, currents = call(
                lambda *refs: first_pack_kernel(0, keeps, *refs),
                [(HBM, (patches, size, columns), bf16), (HBM, incident.shape, bf16)],
                [(VMEM, requests), (VMEM, own), (VMEM, received)],
                [DMA((2,))],
            )
        else:
            outgoing, currents = pack(step, keeps, True, own, (None, currents))
            if lax.axis_size("lag") > 1:
                outgoing, currents = pack(step, keeps, False, received, (outgoing, currents), [field])
        arrived = exchange(outgoing)
        field = shifted(field)
        if step + 1 < steps:
            staged = call(
                lambda *refs, n=step + 1: stage_kernel(n, *refs),
                [(VMEM, column, f32)],
                [(HBM, incident), (VMEM, field)],
                [pltpu.VMEM(column, bf16), DMA],
            )
            shared = [(VMEM, high), (HBM, low), (VMEM, arrived), (VMEM, staged)]
            scratch = [pltpu.VMEM(low_panel, bf16), pltpu.VMEM(column, f32), DMA((pieces,))]
            sizes = [all_flops, panel_bytes + arrived_bytes, panel_bytes + arrived_bytes]
            current = call(
                solve_kernel, [(VMEM, column, bf16)], [*shared, (VMEM, inverse)], scratch, *sizes
            )
            field = call(
                partial_kernel, [(VMEM, column, f32)], [*shared, (VMEM, current)], scratch, *sizes
            )
        else:
            field = call(
                ahead_kernel,
                [(HBM, column, f32)],
                [(VMEM, high), (VMEM, arrived), (VMEM, field)],
                [pltpu.VMEM(column, f32), DMA((2,))],
                all_flops,
                panel_bytes + arrived_bytes,
                panel_bytes + arrived_bytes,
            )
    return currents, field[None]


def solution(mesh):
    in_specs = (
        P(None, "patch", None),
        P("lag", "patch", None),
        P("patch", None, None),
        P("lag", "patch", None, None, None),
        P("lag", "patch", None),
        P("lag", "patch", None),
        P(),
    )
    out_specs = (P(None, "patch", None), P("lag", "patch", None))
    return jax.shard_map(body, mesh=mesh, in_specs=in_specs, out_specs=out_specs, check_vma=False)
```
